32 devices in a mesh: slide: 4 (over x, core), gy: 2 (over y), gx: 4 (over z).
Axes of the slice: x: 2, y: 2, z: 4, core: 2. Of those that a mesh axis runs over, the one named last changes fastest.
Arguments:
- tokens: bfloat16 [4, 32, 64, 1024], P('slide', 'gy', 'gx'), may hold values from -64 to 64, as said below
- weights: bfloat16 [1024, 4096], replicated, may hold values from -5 to 5
- norm_gain: float32 [1024], replicated, may hold values from 0.25 to 1.75
- tissue: int32 [4, 32, 64], P('slide', 'gy', 'gx'), may hold values from 0 to 1, as said below
- cotangent: bfloat16 [4, 32, 64, 1024], P('slide', 'gy', 'gx'), may hold values from -6 to 6
Outputs:
- block_output: bfloat16 [4, 32, 64, 1024], P('slide', 'gy', 'gx')
- input_grad: bfloat16 [4, 32, 64, 1024], P('slide', 'gy', 'gx')
- weight_grads: float32 [1024, 4096], P(('slide', 'gy', 'gx'))
The draws below stay inside these ranges and needn't reach their ends.
Inputs may be any that keep to these rules, and one draw needn't show every extreme that they name: `tokens`: token activations. 1 marks a tissue token, 0 background.
All inputs are finite; a program needn't handle non-finite values.
Results may differ from the reference program's by a relative error of at most 0.015.
The reference program's roundings to bfloat16 on the way count: a program that leaves them out, or rounds other values in their place, can miss the bound.
Values may be sent and summed in bfloat16 or wider, within the bound.
No kernel may reach another device: no remote copies, remote signals or barrier semaphores. Data moves between devices by JAX's collectives and lax.ppermute only.
A program may use at most 128 MiB of HBM per device.

```python
import math
import jax
import jax.numpy as jnp
from jax import lax

D = 1024
HEADS = 16
RADIUS = 6
SLIDES = 4
NY = 32
NX = 64
ALL_TOKENS = 8192


def draw_tokens(key, part):
    first_key = jax.random.fold_in(key, 0)
    drawn = jnp.clip(jax.random.normal(first_key, (SLIDES, NY, NX, D), jnp.float32), -6.0, 6.0)
    return drawn.astype(jnp.bfloat16)


def draw_weights(key, part):
    drawn = jnp.clip(jax.random.normal(key, (D, 4 * D), jnp.float32), -6.0, 6.0)
    column = jnp.arange(4 * D)
    quarter = column // D
    factor = jnp.where(quarter < 2, 1.3, jnp.where(quarter == 2, 1.0, 4.0))
    return (drawn * factor[None, :] / math.sqrt(D)).astype(jnp.bfloat16)


def draw_tissue(key, part):
    subkeys = jax.random.split(key, 5)
    row_index = jnp.arange(NY)[None, :, None]
    col_index = jnp.arange(NX)[None, None, :]
    centre_rows = jax.random.randint(subkeys[0], (3, SLIDES, 1, 1), 1, NY)
    centre_cols = jax.random.randint(subkeys[1], (3, SLIDES, 1, 1), 1, NX)
    radius_rows = jax.random.randint(subkeys[2], (3, SLIDES, 1, 1), NY // 8 + 1, NY // 3 + 2)
    radius_cols = jax.random.randint(subkeys[3], (3, SLIDES, 1, 1), NX // 8 + 1, NX // 3 + 2)
    covered = jnp.zeros((SLIDES, NY, NX), bool)
    for blob_index in range(3):
        down = row_index - centre_rows[blob_index]
        across = col_index - centre_cols[blob_index]
        inside = down * down * 64 // (radius_rows[blob_index] * radius_rows[blob_index]) + across * across * 64 // (radius_cols[blob_index] * radius_cols[blob_index]) <= 64
        covered = covered | inside
    holes = jax.random.randint(subkeys[4], (SLIDES, NY, NX), 0, 8) != 0
    result = covered & holes
    result = result | (row_index == centre_rows[0]) & (col_index == centre_cols[0])
    result = result & jnp.logical_not((row_index == 0) & (col_index == 0))
    return result.astype(jnp.int32)


def block_levels(stream_key, extent, shards, low, largest):
    def one(dim, shards_of):
        steps = jax.random.uniform(jax.random.fold_in(jax.random.fold_in(stream_key, 6), dim), (shards_of,), jnp.float32, low / len(shards), largest / len(shards))
        return jnp.repeat(jnp.exp(steps), extent[dim] // shards_of).reshape((-1,) + (1,) * (len(extent) - dim - 1))

    gain = one(*shards[0])
    for cut in shards[1:]:
        gain = gain * one(*cut)
    return gain


def normal_values(stream_key, shape, spread, reach, pieces=(), dtype=jnp.bfloat16):
    values = jax.random.normal(stream_key, shape, jnp.float32) * spread
    if len(pieces) > 0:
        values = block_levels(stream_key, shape, pieces, -0.22, 0.18) * values
    return jnp.clip(values, min=-reach, max=reach).astype(dtype)


def setup_inputs(seed: int = 0) -> dict:
    keys = jax.random.split(jax.random.key(seed), 6)
    return {
        "tokens": draw_tokens(jax.random.fold_in(keys[5], 71), 0),
        "weights": draw_weights(jax.random.fold_in(keys[5], 71), 0),
        "norm_gain": jnp.clip(1.0 + 0.15 * jax.random.normal(keys[2], (D,), jnp.float32), 0.25, 1.75),
        "tissue": draw_tissue(jax.random.fold_in(keys[5], 71), 0),
        "cotangent": normal_values(keys[4], (SLIDES, NY, NX, D), 1.0, 6.0, ((0, 4), (1, 2), (2, 4))),
    }


EPSILON = 1e-06

def contract(pattern, left_operand, second):
    return jnp.einsum(pattern, left_operand.astype(jnp.float32), second.astype(jnp.float32))

def into_blocks(array, blocks_down, blocks_across, head_dim):
    shaped = array.reshape(blocks_down, 8, blocks_across, 8, HEADS, head_dim)
    return shaped.transpose(0, 2, 1, 3, 4, 5).reshape(blocks_down * blocks_across, 64, HEADS, head_dim)

def from_blocks(array, blocks_down, blocks_across):
    model_width = array.shape[2] * array.shape[3]
    shaped = array.reshape(blocks_down, blocks_across, 8, 8, model_width)
    return shaped.transpose(0, 2, 1, 3, 4).reshape(blocks_down * 8, blocks_across * 8, model_width)

def stack_windows(array, blocks_count):
    return jnp.stack([array[offset:offset + blocks_count] for offset in range(3)], axis=1)

def tile_attention(queries, key_values, grad_attn, row_valid, col_valid):
    tile_rows, tile_cols, model_width = queries.shape
    head_dim = model_width // HEADS
    blocks_down = tile_rows // 8
    blocks_across = tile_cols // 8
    block_count = blocks_down * blocks_across
    window_edge = 8 + 2 * RADIUS
    window_size = window_edge * window_edge
    extra_rows = 16 - 2 * RADIUS
    channels = key_values.shape[2]
    padded = jnp.pad(key_values, ((0, extra_rows), (0, extra_rows), (0, 0)))
    block_grid = padded.reshape(blocks_down + 2, 8, blocks_across + 2, 8, channels)
    row_stack = stack_windows(block_grid, blocks_down)
    full_stack = jnp.stack([row_stack[:, :, :, offset:offset + blocks_across] for offset in range(3)], axis=4)
    windows = full_stack.reshape(blocks_down, 24, blocks_across, 24, channels)[:, :window_edge, :, :window_edge]
    windows = windows.transpose(0, 2, 1, 3, 4).reshape(block_count, window_size, channels)
    row_padded = jnp.pad(row_valid, (0, extra_rows)).reshape(blocks_down + 2, 8)
    row_window = stack_windows(row_padded, blocks_down).reshape(blocks_down, 24)[:, :window_edge]
    col_padded = jnp.pad(col_valid, (0, extra_rows)).reshape(blocks_across + 2, 8)
    col_window = stack_windows(col_padded, blocks_across).reshape(blocks_across, 24)[:, :window_edge]
    query_slot = jnp.arange(64)
    key_slot = jnp.arange(window_size)
    query_row = (query_slot // 8)[:, None]
    query_col = (query_slot % 8)[:, None]
    key_row = (key_slot // window_edge)[None, :]
    key_col = (key_slot % window_edge)[None, :]
    nearby = (key_row >= query_row) & (key_row <= query_row + 2 * RADIUS)
    nearby = nearby & (key_col >= query_col) & (key_col <= query_col + 2 * RADIUS)
    in_grid = (row_window[:, None, :, None] & col_window[None, :, None, :]).reshape(block_count, 1, 1, window_size)
    allowed = nearby[None, None] & in_grid
    query_blocks = into_blocks(queries, blocks_down, blocks_across, head_dim)
    grad_blocks = into_blocks(grad_attn, blocks_down, blocks_across, head_dim)
    key_blocks = windows[:, :, :model_width].reshape(block_count, window_size, HEADS, head_dim)
    value_blocks = windows[:, :, model_width:].reshape(block_count, window_size, HEADS, head_dim)
    scaling = 1.0 / math.sqrt(head_dim)
    scores = contract('nqhd,nkhd->nhqk', query_blocks, key_blocks) * scaling
    scores = jnp.where(allowed, scores, -1e+30)
    row_max = lax.optimization_barrier(jnp.max(scores, axis=-1, keepdims=True))
    exponent = jnp.exp(scores - row_max)
    attn_probs = exponent / lax.optimization_barrier(jnp.sum(exponent, axis=-1, keepdims=True))
    probs_bf = attn_probs.astype(jnp.bfloat16)
    attended = contract('nhqk,nkhd->nqhd', probs_bf, value_blocks).astype(jnp.bfloat16)
    grad_probs = contract('nqhd,nkhd->nhqk', grad_blocks, value_blocks)
    centred = grad_probs - lax.optimization_barrier(jnp.sum(attn_probs * grad_probs, axis=-1, keepdims=True))
    grad_scores = (attn_probs * centred * scaling).astype(jnp.bfloat16)
    grad_queries = contract('nhqk,nkhd->nqhd', grad_scores, key_blocks).astype(jnp.bfloat16)
    grad_keys = contract('nhqk,nqhd->nkhd', grad_scores, query_blocks)
    grad_values = contract('nhqk,nqhd->nkhd', probs_bf, grad_blocks)
    grad_windows = jnp.concatenate([grad_keys.reshape(block_count, window_size, model_width), grad_values.reshape(block_count, window_size, model_width)], axis=-1)
    grad_windows = grad_windows.reshape(blocks_down, blocks_across, window_edge, window_edge, channels)
    grad_windows = jnp.pad(grad_windows, ((0, 0), (0, 0), (0, 24 - window_edge), (0, 24 - window_edge), (0, 0)))
    grad_windows = grad_windows.reshape(blocks_down, blocks_across, 3, 8, 3, 8, channels)
    accumulated = jnp.zeros((blocks_down + 2, 8, blocks_across + 2, 8, channels), jnp.float32)
    for offset_down in range(3):
        for offset_across in range(3):
            window_part = grad_windows[:, :, offset_down, :, offset_across].transpose(0, 2, 1, 3, 4)
            accumulated = accumulated.at[offset_down:offset_down + blocks_down, :, offset_across:offset_across + blocks_across].add(window_part)
    accumulated = accumulated.reshape(8 * (blocks_down + 2), 8 * (blocks_across + 2), channels)
    accumulated = accumulated[:tile_rows + 2 * RADIUS, :tile_cols + 2 * RADIUS]
    return (from_blocks(attended, blocks_down, blocks_across), from_blocks(grad_queries, blocks_down, blocks_across), accumulated)

def one_slide(slide_tokens, weights, norm_gain, slide_tissue, slide_cot):
    weight_in = weights[:, :3 * D]
    weight_out = weights[:, 3 * D:]
    tokens_float = slide_tokens.astype(jnp.float32)
    row_mean = lax.optimization_barrier(jnp.mean(tokens_float, axis=-1, keepdims=True))
    centered = tokens_float - row_mean
    variance = lax.optimization_barrier(jnp.mean(centered * centered, axis=-1, keepdims=True))
    inverse = lax.rsqrt(variance + EPSILON)
    normalized = centered * inverse
    normed = (normalized * norm_gain).astype(jnp.bfloat16)
    normed_flat = normed.reshape(NY * NX, D)
    projected = jnp.dot(normed_flat, weight_in, preferred_element_type=jnp.float32).astype(jnp.bfloat16).reshape(NY, NX, 3 * D)
    queries = projected[:, :, :D]
    key_values = projected[:, :, D:]
    tissue_mask = slide_tissue.astype(jnp.float32)[:, :, None]
    upstream = slide_cot.astype(jnp.float32)
    branch_grad = (tissue_mask * upstream).astype(jnp.bfloat16)
    branch_flat = branch_grad.reshape(NY * NX, D)
    grad_attn = jnp.dot(branch_flat, weight_out.T, preferred_element_type=jnp.float32).astype(jnp.bfloat16).reshape(NY, NX, D)
    padded_kv = jnp.pad(key_values, ((RADIUS, RADIUS), (RADIUS, RADIUS), (0, 0)))
    row_coord = jnp.arange(NY + 2 * RADIUS)
    row_valid = (row_coord >= RADIUS) & (row_coord < NY + RADIUS)
    col_coord = jnp.arange(NX + 2 * RADIUS)
    col_valid = (col_coord >= RADIUS) & (col_coord < NX + RADIUS)

    def strip_step(strip_index, carry):
        attended_all, grad_query_all, grad_padded_all = carry
        top_row = (strip_index * 8).astype(jnp.int32)
        query_strip = lax.dynamic_slice_in_dim(queries, top_row, 8, 0)
        kv_strip = lax.dynamic_slice_in_dim(padded_kv, top_row, 8 + 2 * RADIUS, 0)
        grad_strip = lax.dynamic_slice_in_dim(grad_attn, top_row, 8, 0)
        valid_strip = lax.dynamic_slice_in_dim(row_valid, top_row, 8 + 2 * RADIUS, 0)
        attended, grad_queries, grad_padded = tile_attention(query_strip, kv_strip, grad_strip, valid_strip, col_valid)
        attended_all = lax.dynamic_update_slice_in_dim(attended_all, attended, top_row, 0)
        grad_query_all = lax.dynamic_update_slice_in_dim(grad_query_all, grad_queries, top_row, 0)
        previous = lax.dynamic_slice_in_dim(grad_padded_all, top_row, 8 + 2 * RADIUS, 0)
        grad_padded_all = lax.dynamic_update_slice_in_dim(grad_padded_all, previous + grad_padded, top_row, 0)
        return (attended_all, grad_query_all, grad_padded_all)
    start_carry = (jnp.zeros((NY, NX, D), jnp.bfloat16), jnp.zeros((NY, NX, D), jnp.bfloat16), jnp.zeros((NY + 2 * RADIUS, NX + 2 * RADIUS, 2 * D), jnp.float32))
    attended_all, grad_query_all, grad_padded_all = lax.fori_loop(0, NY // 8, strip_step, start_carry)
    grad_kv = grad_padded_all[RADIUS:RADIUS + NY, RADIUS:RADIUS + NX].astype(jnp.bfloat16)
    grad_projected = jnp.concatenate([grad_query_all, grad_kv], axis=-1).reshape(NY * NX, 3 * D)
    attended_flat = attended_all.reshape(NY * NX, D)
    projection = jnp.dot(attended_flat, weight_out, preferred_element_type=jnp.float32).reshape(NY, NX, D)
    block_output = (tokens_float + tissue_mask * projection).astype(jnp.bfloat16)
    grad_normed = jnp.dot(grad_projected, weight_in.T, preferred_element_type=jnp.float32).reshape(NY, NX, D)
    scaled = grad_normed * norm_gain
    first_mean = lax.optimization_barrier(jnp.mean(scaled, axis=-1, keepdims=True))
    second_mean = lax.optimization_barrier(jnp.mean(scaled * normalized, axis=-1, keepdims=True))
    input_grad = (upstream + inverse * (scaled - first_mean - normalized * second_mean)).astype(jnp.bfloat16)
    grad_in = jnp.dot(normed_flat.T, grad_projected, preferred_element_type=jnp.float32)
    grad_out = jnp.dot(attended_flat.T, branch_flat, preferred_element_type=jnp.float32)
    return (block_output, input_grad, jnp.concatenate([grad_in, grad_out], axis=1))

def reference(tokens, weights, norm_gain, tissue, cotangent):
    outputs_list = []
    grads_list = []
    grad_total = jnp.zeros((D, 4 * D), jnp.float32)
    for slide_index in range(SLIDES):
        block_output, input_grad, slide_grads = one_slide(tokens[slide_index], weights, norm_gain, tissue[slide_index], cotangent[slide_index])
        outputs_list.append(block_output)
        grads_list.append(input_grad)
        grad_total = grad_total + slide_grads
    inv_root = 1.0 / math.sqrt(ALL_TOKENS)
    return (jnp.stack(outputs_list), jnp.stack(grads_list), grad_total * inv_root)
```

```python
import functools
import math

import jax
import jax.numpy as jnp
from jax import lax
from jax.experimental import pallas as pl
from jax.experimental.pallas import tpu as pltpu
from jax.sharding import PartitionSpec as P

HEADS = 16
RADIUS = 6
EPSILON = 1e-06
STRIP = 4
GROUP = 4
SIDE = 8
BF = jnp.bfloat16
F32 = jnp.float32


def swapped(array, axis, by):
    count = lax.axis_size(axis)
    return lax.ppermute(array, axis, [(i, i ^ by) for i in range(count)])


def moved(array, axis, by):
    count = lax.axis_size(axis)
    pairs = [(i, i + by) for i in range(count) if 0 <= i + by < count]
    return lax.ppermute(array, axis, pairs)


def row_halo(block, mine):
    rows_count = lax.axis_size("gy")
    if rows_count == 2:
        at_top = lax.axis_index("gy") == 0
        other = swapped(jnp.where(at_top, block[-RADIUS:], block[:RADIUS]), "gy", 1)
        zero = jnp.zeros((), block.dtype)
        top, bottom = jnp.where(at_top, zero, other), jnp.where(at_top, other, zero)
    else:
        top = moved(block[-RADIUS:], "gy", 1)
        bottom = moved(block[:RADIUS], "gy", -1)
    return jnp.concatenate([top, mine, bottom], axis=0)


def column_halo(block):
    right = moved(block[:, :SIDE], "gx", -1)
    left = moved(block[:, -SIDE:], "gx", 1)
    return jnp.concatenate([block, right, left], axis=1)


def spread_heads(block, head_dim):
    lane_head = lax.broadcasted_iota(jnp.int32, block.shape, 1) // head_dim
    zero = jnp.zeros_like(block)
    return jnp.concatenate(
        [jnp.where(lane_head == head, block, zero) for head in range(GROUP)], axis=0
    )


def gather_heads(full, count, head_dim):
    lane_head = lax.broadcasted_iota(jnp.int32, (count, full.shape[1]), 1) // head_dim
    result = full[:count]
    for head in range(1, GROUP):
        result = jnp.where(lane_head == head, full[head * count : (head + 1) * count], result)
    return result


def times(left, right):
    return jnp.dot(left, right, preferred_element_type=F32)


def times_t(left, right):
    return lax.dot_general(left, right, (((1,), (1,)), ((), ())), preferred_element_type=F32)


def fill_bias(place_ref, bias_ref, tile_rows, tile_cols):
    strips, count, window = bias_ref.shape
    slots = tile_cols + 2 * SIDE
    own = lax.broadcasted_iota(jnp.int32, (count, window), 0)
    near = lax.broadcasted_iota(jnp.int32, (count, window), 1)
    own_row, own_col = own // tile_cols, own % tile_cols
    near_row, slot = near // slots, near % slots
    near_col = jnp.where(slot < tile_cols + SIDE, slot, slot - slots)
    row_gap = near_row - RADIUS - own_row
    col_gap = near_col - own_col
    col = place_ref[1] + near_col
    allowed = (jnp.abs(row_gap) <= RADIUS) & (jnp.abs(col_gap) <= RADIUS)
    allowed = allowed & (col >= 0) & (col < place_ref[3])
    for strip in range(strips):
        row = place_ref[0] + strip * STRIP + near_row - RADIUS
        kept = allowed & (row >= 0) & (row < place_ref[2])
        bias_ref[strip] = jnp.where(kept, 0.0, -1e30).astype(F32)


def query_pass(
    head_dim, tile, place_ref, q_ref, g_ref, k_ref, v_ref, out_ref, dq_ref, stat_ref, bias_ref
):
    scaling = 1.0 / math.sqrt(head_dim)
    strips, count, window = bias_ref.shape
    step = (tile[1] + 2 * SIDE) * STRIP
    group = pl.program_id(0)

    @pl.when(group == 0)
    def _():
        fill_bias(place_ref, bias_ref, *tile)
        stat_ref[...] = jnp.zeros_like(stat_ref)

    lane = lax.broadcasted_iota(jnp.int32, (count, 128), 1) - group * (2 * GROUP)
    for strip in range(strips):
        own = pl.ds(strip * count, count)
        near = pl.ds(strip * step, window)
        queries = spread_heads(q_ref[own, :] * jnp.asarray(scaling, BF), head_dim)
        grads = spread_heads(g_ref[own, :], head_dim)
        keys = k_ref[near, :]
        values = v_ref[near, :]
        scores = times_t(queries, keys)
        grad_probs = times_t(grads, values)
        stats = stat_ref[own, :]
        probs_parts, grad_parts = [], []
        for head in range(GROUP):
            part = slice(head * count, (head + 1) * count)
            masked = scores[part] + bias_ref[strip]
            row_max = jnp.max(masked, axis=1, keepdims=True)
            exponent = jnp.exp(masked - row_max)
            grad_part = grad_probs[part]
            total = jnp.sum(exponent, axis=1, keepdims=True)
            share = 1.0 / total
            delta = jnp.sum(exponent * grad_part, axis=1, keepdims=True) * share
            probs = exponent * share
            probs_parts.append(probs.astype(BF))
            grad_parts.append((probs * (grad_part - delta)).astype(BF))
            stats = jnp.where(lane == 2 * head, row_max + jnp.log(total), stats)
            stats = jnp.where(lane == 2 * head + 1, delta, stats)
        attended = times(jnp.concatenate(probs_parts, axis=0), values)
        grad_queries = times(jnp.concatenate(grad_parts, axis=0), keys)
        out_ref[own, :] = gather_heads(attended, count, head_dim).astype(BF)
        dq_ref[own, :] = (gather_heads(grad_queries, count, head_dim) * scaling).astype(BF)
        stat_ref[own, :] = stats


def key_pass(
    head_dim,
    tile,
    first,
    place_ref,
    k_ref,
    v_ref,
    q_ref,
    g_ref,
    stat_ref,
    dk_ref,
    dv_ref,
    bias_ref,
    turned,
):
    scaling = 1.0 / math.sqrt(head_dim)
    strips, count, window = bias_ref.shape
    slots = tile[1] + 2 * SIDE
    step = slots * STRIP
    group = pl.program_id(0)

    @pl.when(group == 0)
    def _():
        fill_bias(place_ref, bias_ref, *tile)
        turned[...] = stat_ref[...].T

    rows = pl.ds(pl.multiple_of((group + first) * (2 * GROUP), 2 * GROUP), 2 * GROUP)

    def own_tokens(ref, strip):
        starts = [(RADIUS + strip * STRIP + row) * slots for row in range(STRIP)]
        return jnp.concatenate([ref[pl.ds(start, tile[1]), :] for start in starts], axis=0)

    for strip in range(strips):
        own = pl.ds(strip * count, count)
        near = pl.ds(strip * step, window)
        keys = spread_heads(own_tokens(k_ref, strip) * jnp.asarray(scaling, BF), head_dim)
        values = spread_heads(own_tokens(v_ref, strip), head_dim)
        queries = q_ref[near, :]
        grads = g_ref[near, :]
        scores = times_t(keys, queries)
        grad_probs = times_t(values, grads)
        stats = turned[rows, near]
        probs_parts, grad_parts = [], []
        for head in range(GROUP):
            part = slice(head * count, (head + 1) * count)
            masked = scores[part] + bias_ref[strip]
            probs = jnp.exp(masked - stats[2 * head : 2 * head + 1])
            centred = grad_probs[part] - stats[2 * head + 1 : 2 * head + 2]
            probs_parts.append(probs.astype(BF))
            grad_parts.append((probs * centred).astype(BF))
        grad_values = times(jnp.concatenate(probs_parts, axis=0), grads)
        grad_keys = times(jnp.concatenate(grad_parts, axis=0), queries)
        dv_ref[own, :] = gather_heads(grad_values, count, head_dim).astype(BF)
        dk_ref[own, :] = (gather_heads(grad_keys, count, head_dim) * scaling).astype(BF)


def whole(shape):
    return pl.BlockSpec(shape, lambda group: (0,) * len(shape))


def columns(rows, width, first=0):
    return pl.BlockSpec((rows, width), lambda group: (0, first + group))


PARAMS = dict(vmem_limit_bytes=24 * 1024 * 1024)


def window_shape(tile):
    return (tile[0] // STRIP, STRIP * tile[1], (STRIP + 2 * RADIUS) * (tile[1] + 2 * SIDE))


def attention_cost(tile, groups, part):
    strips, count, window = window_shape(tile)
    flops = 4 * 2 * groups * strips * GROUP * count * window * part
    return pl.CostEstimate(flops=flops, bytes_accessed=4 * 1024 * 1024, transcendentals=0)


SCALARS = pl.BlockSpec(memory_space=pltpu.SMEM)


def run_queries(place, queries, grads, keys, values, head_dim, tile):
    tokens, width = queries.shape
    ext = keys.shape[0]
    part = GROUP * head_dim
    groups = width // part
    return pl.pallas_call(
        functools.partial(query_pass, head_dim, tile),
        grid=(groups,),
        in_specs=[
            SCALARS,
            columns(tokens, part),
            columns(tokens, part),
            columns(ext, part),
            columns(ext, part),
        ],
        out_specs=[columns(tokens, part), columns(tokens, part), whole((tokens, 128))],
        out_shape=[
            jax.ShapeDtypeStruct((tokens, width), BF),
            jax.ShapeDtypeStruct((tokens, width), BF),
            jax.ShapeDtypeStruct((tokens, 128), F32),
        ],
        scratch_shapes=[pltpu.VMEM(window_shape(tile), F32)],
        compiler_params=pltpu.CompilerParams(**PARAMS),
        cost_estimate=attention_cost(tile, groups, part),
        name="query_pass",
    )(place, queries, grads, keys, values)


def run_keys(place, keys, values, queries, grads, stats, head_dim, tile, first, groups):
    tokens = tile[0] * tile[1]
    ext = queries.shape[0]
    part = GROUP * head_dim
    return pl.pallas_call(
        functools.partial(key_pass, head_dim, tile, first),
        grid=(groups,),
        in_specs=[SCALARS] + [columns(ext, part, first)] * 4 + [whole(stats.shape)],
        out_specs=[columns(tokens, part), columns(tokens, part)],
        out_shape=[
            jax.ShapeDtypeStruct((tokens, groups * part), BF),
            jax.ShapeDtypeStruct((tokens, groups * part), BF),
        ],
        scratch_shapes=[pltpu.VMEM(window_shape(tile), F32), pltpu.VMEM((128, ext), F32)],
        compiler_params=pltpu.CompilerParams(**PARAMS),
        cost_estimate=attention_cost(tile, groups, part),
        name="key_pass",
    )(place, keys, values, queries, grads, stats)


def own_part(array, index, axis):
    return lax.dynamic_index_in_dim(array, index, axis, keepdims=False)


def product_t(left, right):
    return lax.dot_general(left, right, (((0,), (0,)), ((), ())), preferred_element_type=F32)


def slide_swap(array, high):
    return swapped(array, "slide", lax.axis_size("slide") // 2 if high else 1)


def partners(across_slides):
    if across_slides:
        index = lax.axis_index("slide") // 2
        return index, [(1, 1 - index)]
    index = lax.axis_index("gy")
    return index, [(by, index ^ by) for by in range(1, lax.axis_size("gy"))]


def sent(block, across_slides, by):
    return slide_swap(block, True) if across_slides else swapped(block, "gy", by)


def pick_rows(left, index, across_slides):
    half = left.shape[1] // 2
    if across_slides:
        return lax.dynamic_slice_in_dim(left, index * half, half, axis=1)
    rest = half // lax.axis_size("gy")
    parts = [
        lax.dynamic_slice_in_dim(left, high * half + index * rest, rest, axis=1)
        for high in range(2)
    ]
    return jnp.concatenate(parts, axis=1)


def first_halving(left, right, across_slides):
    index, others = partners(across_slides)
    arrived = []
    for by, target in others:
        block = product_t(pick_rows(left, target, across_slides), right).astype(BF)
        arrived.append(sent(block, across_slides, by))
    mine = product_t(pick_rows(left, index, across_slides), right)
    for block in arrived:
        mine = mine + block.astype(F32)
    return mine


def second_halving(part, across_slides):
    index, others = partners(across_slides)
    rows = part.shape[0] // (len(others) + 1)
    mine = lax.dynamic_slice_in_dim(part, index * rows, rows, axis=0)
    for by, target in others:
        block = lax.dynamic_slice_in_dim(part, target * rows, rows, axis=0).astype(BF)
        mine = mine + sent(block, across_slides, by).astype(F32)
    return mine


def reduce_columns(part):
    count = lax.axis_size("gx")
    index = lax.axis_index("gx")
    rows = part.shape[0] // count
    mine = lax.dynamic_slice_in_dim(part, index * rows, rows, axis=0)
    arrived = []
    for by in range(count - 1, 0, -1):
        block = lax.dynamic_slice_in_dim(part, (index ^ by) * rows, rows, axis=0)
        arrived.append(swapped(block.astype(BF), "gx", by))
    for block in arrived:
        mine = mine + block.astype(F32)
    return mine


def later_halvings(one, two):
    one = second_halving(one, False)
    two = second_halving(two, True)
    return reduce_columns(jnp.concatenate([one, two], axis=1))


def after(array, *earlier):
    return lax.optimization_barrier((array, *earlier))[0]


def local(tokens, weights, norm_gain, tissue, cotangent):
    tile_tokens = tokens[0]
    tile_rows, tile_cols, model_width = tile_tokens.shape
    tile = (tile_rows, tile_cols)
    head_dim = model_width // HEADS
    token_count = tile_rows * tile_cols
    slides = lax.axis_size("slide")
    rows_count = lax.axis_size("gy")
    cols_count = lax.axis_size("gx")
    weight_in = weights[:, : 3 * model_width]
    weight_out = weights[:, 3 * model_width :]
    place = jnp.stack(
        [
            lax.axis_index("gy") * tile_rows,
            lax.axis_index("gx") * tile_cols,
            jnp.int32(tile_rows * rows_count),
            jnp.int32(tile_cols * cols_count),
        ]
    ).astype(jnp.int32)

    token_rows = row_halo(tile_tokens, tile_tokens)
    tissue_mask = tissue[0].astype(F32)[:, :, None]
    upstream = cotangent[0].astype(F32)
    branch_grad = (tissue_mask * upstream).astype(BF)
    branch_flat = branch_grad.reshape(token_count, model_width)

    def normalize(array):
        array = array.astype(F32)
        centered = array - jnp.mean(array, axis=-1, keepdims=True)
        variance = jnp.mean(centered * centered, axis=-1, keepdims=True)
        inverse = lax.rsqrt(variance + EPSILON)
        return centered * inverse, inverse

    normalized, inverse = normalize(tile_tokens.reshape(token_count, model_width))
    normed = (normalized * norm_gain).astype(BF)
    grad_attn = times_t(branch_flat, weight_out).astype(BF)
    queries = times(normed, weight_in[:, :model_width]).astype(BF)

    core = lax.axis_index("slide") % 2

    def half_swap(array):
        rows = model_width // slides

        def half(which):
            parts = [
                lax.dynamic_slice_in_dim(array, (2 * high + which) * rows, rows, axis=1)
                for high in range(slides // 2)
            ]
            return jnp.concatenate(parts, axis=1)

        return jnp.concatenate([half(core), slide_swap(half(1 - core), False)], axis=0)

    def whole_swap(array):
        return jnp.concatenate([array, slide_swap(array, False)], axis=0)

    token_ext = column_halo(token_rows)
    ext_rows, ext_cols = token_ext.shape[:2]
    branch_first = after(branch_grad, token_rows)
    branch_rows = row_halo(branch_first, branch_grad)
    token_ext = token_ext.reshape(ext_rows * ext_cols, model_width)
    normed_ext = (normalize(token_ext)[0] * norm_gain).astype(BF)
    key_ext = times(normed_ext, weight_in[:, model_width : 2 * model_width]).astype(BF)
    value_ext = times(normed_ext, weight_in[:, 2 * model_width :]).astype(BF)
    branch_ext = column_halo(branch_rows).reshape(ext_rows * ext_cols, model_width)

    attended, grad_queries, stats = run_queries(
        place, queries, grad_attn, key_ext, value_ext, head_dim, tile
    )

    stats_tile = stats.reshape(tile_rows, tile_cols, -1)
    stats_ext = column_halo(row_halo(stats_tile, stats_tile))
    stats_ext = stats_ext.reshape(ext_rows * ext_cols, -1)

    normed_pair = half_swap(normed)
    branch_pair = whole_swap(branch_flat)
    one = first_halving(normed_pair, whole_swap(grad_queries), True)
    two = first_halving(half_swap(attended), branch_pair, False)

    normed_late, branch_late = lax.optimization_barrier((normed_ext, branch_ext, stats))[:2]
    query_ext = times(normed_late, weight_in[:, :model_width]).astype(BF)
    grad_ext = times_t(branch_late, weight_out).astype(BF)

    projection = times(attended, weight_out).reshape(tile_tokens.shape)
    block_output = (tile_tokens.astype(F32) + tissue_mask * projection).astype(BF)

    stats_ext, one, two = lax.optimization_barrier((stats_ext, one, two))
    groups = HEADS // GROUP
    grad_keys, grad_values = run_keys(
        place, key_ext, value_ext, query_ext, grad_ext, stats_ext, head_dim, tile, 0, groups
    )
    first_sums = later_halvings(one, two)
    second_sums = later_halvings(
        first_halving(normed_pair, whole_swap(grad_keys), True),
        first_halving(normed_pair, whole_swap(grad_values), False),
    )

    grad_projected = jnp.concatenate([grad_queries, grad_keys, grad_values], axis=-1)
    scaled = times_t(grad_projected, weight_in) * norm_gain
    first_mean = jnp.mean(scaled, axis=-1, keepdims=True)
    second_mean = jnp.mean(scaled * normalized, axis=-1, keepdims=True)
    input_grad = inverse * (scaled - first_mean - normalized * second_mean)
    input_grad = (upstream + input_grad.reshape(tile_tokens.shape)).astype(BF)

    inv_root = 1.0 / math.sqrt(slides * rows_count * cols_count * token_count)
    width = model_width
    weight_grads = jnp.concatenate(
        [first_sums[:, :width], second_sums, first_sums[:, width:]], axis=1
    )
    return (block_output[None], input_grad[None], weight_grads * inv_root)


def solution(mesh):
    tile = P("slide", "gy", "gx", None)
    return jax.shard_map(
        local,
        mesh=mesh,
        in_specs=(tile, P(), P(), P("slide", "gy", "gx"), tile),
        out_specs=(tile, tile, P(("slide", "gy", "gx"), None)),
        check_vma=False,
    )
```

```python
import functools
import math

import jax
import jax.numpy as jnp
from jax import lax
from jax.experimental import pallas as pl
from jax.experimental.pallas import tpu as pltpu
from jax.sharding import PartitionSpec as P

HEADS = 16
RADIUS = 6
EPSILON = 1e-06
STRIP = 4
GROUP = 4
SIDE = 8
BF = jnp.bfloat16
F32 = jnp.float32


def swapped(array, axis, by):
    count = lax.axis_size(axis)
    return lax.ppermute(array, axis, [(i, i ^ by) for i in range(count)])


def moved(array, axis, by):
    count = lax.axis_size(axis)
    pairs = [(i, i + by) for i in range(count) if 0 <= i + by < count]
    return lax.ppermute(array, axis, pairs)


def rows_around(block, facing=None):
    rows_count = lax.axis_size("gy")
    if rows_count == 2:
        at_top = lax.axis_index("gy") == 0
        if facing is None:
            facing = jnp.where(at_top, block[-RADIUS:], block[:RADIUS])
        return (swapped(facing, "gy", 1),)
    return (moved(block[-RADIUS:], "gy", 1), moved(block[:RADIUS], "gy", -1))


def with_rows(block, rows):
    if len(rows) == 1:
        at_top = lax.axis_index("gy") == 0
        zero = jnp.zeros((), block.dtype)
        rows = (jnp.where(at_top, zero, rows[0]), jnp.where(at_top, rows[0], zero))
    return jnp.concatenate([rows[0], block, rows[1]], axis=0)


def column_halo(block):
    right = moved(block[:, :SIDE], "gx", -1)
    left = moved(block[:, -SIDE:], "gx", 1)
    return jnp.concatenate([block, right, left], axis=1)


def prepare(place_ref, x_ref, c_ref, t_ref, gain_ref, both_ref, face_ref, moment_ref):
    block, width = x_ref.shape
    step = pl.program_id(0)
    rows = pl.ds(pl.multiple_of(step * block, block), block)
    x = x_ref[...].astype(F32)
    mean = jnp.sum(x, axis=1, keepdims=True) * (1.0 / width)
    centered = x - mean
    variance = jnp.sum(centered * centered, axis=1, keepdims=True) * (1.0 / width)
    inverse = lax.rsqrt(variance + EPSILON)
    both_ref[rows, :width] = (centered * inverse * gain_ref[...]).astype(BF)
    both_ref[rows, width:] = (c_ref[...].astype(F32) * t_ref[...]).astype(BF)
    lane = lax.broadcasted_iota(jnp.int32, moment_ref.shape, 1)
    moment_ref[...] = jnp.where(lane == 0, mean, inverse)

    @pl.when(step == pl.num_programs(0) - 1)
    def _():
        first = pl.multiple_of(place_ref[4], 16)
        face_ref[...] = both_ref[pl.ds(first, face_ref.shape[0]), :]


def run_prepare(place, tokens, cotangent, tissue, gain, face):
    count, width = tokens.shape
    block = min(count, 64)
    part = lambda columns: pl.BlockSpec((block, columns), lambda step: (step, 0))
    return pl.pallas_call(
        prepare,
        grid=(count // block,),
        in_specs=[SCALARS, part(width), part(width), part(1), whole((1, width))],
        out_specs=[whole((count, 2 * width)), whole((face, 2 * width)), part(128)],
        out_shape=[
            jax.ShapeDtypeStruct((count, 2 * width), BF),
            jax.ShapeDtypeStruct((face, 2 * width), BF),
            jax.ShapeDtypeStruct((count, 128), F32),
        ],
        compiler_params=pltpu.CompilerParams(**PARAMS),
        cost_estimate=pl.CostEstimate(flops=0, bytes_accessed=3 * 1024 * 1024, transcendentals=0),
        name="prepare",
    )(place, tokens, cotangent, tissue, gain)


def spread_heads(block, head_dim):
    lane_head = lax.broadcasted_iota(jnp.int32, block.shape, 1) // head_dim
    zero = jnp.zeros_like(block)
    return jnp.concatenate(
        [jnp.where(lane_head == head, block, zero) for head in range(GROUP)], axis=0
    )


def gather_heads(full, count, head_dim):
    lane_head = lax.broadcasted_iota(jnp.int32, (count, full.shape[1]), 1) // head_dim
    result = full[:count]
    for head in range(1, GROUP):
        result = jnp.where(lane_head == head, full[head * count : (head + 1) * count], result)
    return result


def times(left, right):
    return jnp.dot(left, right, preferred_element_type=F32)


def times_t(left, right):
    return lax.dot_general(left, right, (((1,), (1,)), ((), ())), preferred_element_type=F32)


def fill_bias(place_ref, bias_ref, tile_rows, tile_cols):
    strips, count, window = bias_ref.shape
    slots = tile_cols + 2 * SIDE
    own = lax.broadcasted_iota(jnp.int32, (count, window), 0)
    near = lax.broadcasted_iota(jnp.int32, (count, window), 1)
    own_row, own_col = own // tile_cols, own % tile_cols
    near_row, slot = near // slots, near % slots
    near_col = jnp.where(slot < tile_cols + SIDE, slot, slot - slots)
    row_gap = near_row - RADIUS - own_row
    col_gap = near_col - own_col
    col = place_ref[1] + near_col
    allowed = (jnp.abs(row_gap) <= RADIUS) & (jnp.abs(col_gap) <= RADIUS)
    allowed = allowed & (col >= 0) & (col < place_ref[3])
    for strip in range(strips):
        row = place_ref[0] + strip * STRIP + near_row - RADIUS
        kept = allowed & (row >= 0) & (row < place_ref[2])
        bias_ref[strip] = jnp.where(kept, 0.0, -1e30).astype(F32)


def query_pass(
    head_dim, tile, place_ref, q_ref, g_ref, k_ref, v_ref, out_ref, stat_ref, bias_ref
):
    scaling = 1.0 / math.sqrt(head_dim)
    strips, count, window = bias_ref.shape
    step = (tile[1] + 2 * SIDE) * STRIP
    group = pl.program_id(0)

    @pl.when(group == 0)
    def _():
        fill_bias(place_ref, bias_ref, *tile)
        stat_ref[...] = jnp.zeros_like(stat_ref)

    lane = lax.broadcasted_iota(jnp.int32, (count, 128), 1) - group * (2 * GROUP)
    for strip in range(strips):
        own = pl.ds(strip * count, count)
        near = pl.ds(strip * step, window)
        queries = spread_heads(q_ref[own, :] * jnp.asarray(scaling, BF), head_dim)
        grads = spread_heads(g_ref[own, :], head_dim)
        keys = k_ref[near, :]
        values = v_ref[near, :]
        scores = times_t(queries, keys)
        grad_probs = times_t(grads, values)
        stats = stat_ref[own, :]
        probs_parts, grad_parts = [], []
        for head in range(GROUP):
            part = slice(head * count, (head + 1) * count)
            masked = scores[part] + bias_ref[strip]
            row_max = jnp.max(masked, axis=1, keepdims=True)
            exponent = jnp.exp(masked - row_max)
            grad_part = grad_probs[part]
            total = jnp.sum(exponent, axis=1, keepdims=True)
            share = 1.0 / total
            delta = jnp.sum(exponent * grad_part, axis=1, keepdims=True) * share
            probs = exponent * share
            probs_parts.append(probs.astype(BF))
            grad_parts.append((probs * (grad_part - delta)).astype(BF))
            stats = jnp.where(lane == 2 * head, row_max + jnp.log(total), stats)
            stats = jnp.where(lane == 2 * head + 1, delta, stats)
        attended = times(jnp.concatenate(probs_parts, axis=0), values)
        grad_queries = times(jnp.concatenate(grad_parts, axis=0), keys)
        out_ref[0, own, :] = gather_heads(attended, count, head_dim).astype(BF)
        out_ref[1, own, :] = (gather_heads(grad_queries, count, head_dim) * scaling).astype(BF)
        stat_ref[own, :] = stats


def key_pass(
    head_dim,
    tile,
    first,
    place_ref,
    k_ref,
    v_ref,
    q_ref,
    g_ref,
    stat_ref,
    out_ref,
    bias_ref,
    turned,
):
    scaling = 1.0 / math.sqrt(head_dim)
    strips, count, window = bias_ref.shape
    slots = tile[1] + 2 * SIDE
    step = slots * STRIP
    group = pl.program_id(0)

    @pl.when(group == 0)
    def _():
        fill_bias(place_ref, bias_ref, *tile)
        turned[...] = stat_ref[...].T

    rows = pl.ds(pl.multiple_of((group + first) * (2 * GROUP), 2 * GROUP), 2 * GROUP)

    def own_tokens(ref, strip):
        starts = [(RADIUS + strip * STRIP + row) * slots for row in range(STRIP)]
        return jnp.concatenate([ref[pl.ds(start, tile[1]), :] for start in starts], axis=0)

    for strip in range(strips):
        own = pl.ds(strip * count, count)
        near = pl.ds(strip * step, window)
        keys = spread_heads(own_tokens(k_ref, strip) * jnp.asarray(scaling, BF), head_dim)
        values = spread_heads(own_tokens(v_ref, strip), head_dim)
        queries = q_ref[near, :]
        grads = g_ref[near, :]
        scores = times_t(keys, queries)
        grad_probs = times_t(values, grads)
        stats = turned[rows, near]
        probs_parts, grad_parts = [], []
        for head in range(GROUP):
            part = slice(head * count, (head + 1) * count)
            masked = scores[part] + bias_ref[strip]
            probs = jnp.exp(masked - stats[2 * head : 2 * head + 1])
            centred = grad_probs[part] - stats[2 * head + 1 : 2 * head + 2]
            probs_parts.append(probs.astype(BF))
            grad_parts.append((probs * centred).astype(BF))
        grad_values = times(jnp.concatenate(probs_parts, axis=0), grads)
        grad_keys = times(jnp.concatenate(grad_parts, axis=0), queries)
        out_ref[1, own, :] = gather_heads(grad_values, count, head_dim).astype(BF)
        out_ref[0, own, :] = (gather_heads(grad_keys, count, head_dim) * scaling).astype(BF)


def whole(shape):
    return pl.BlockSpec(shape, lambda group: (0,) * len(shape))


def columns(rows, width, first=0):
    return pl.BlockSpec((rows, width), lambda group: (0, first + group))


def pair_columns(rows, width):
    return pl.BlockSpec((2, rows, width), lambda group: (0, 0, group))


SCALARS = pl.BlockSpec(memory_space=pltpu.SMEM)
PARAMS = dict(vmem_limit_bytes=24 * 1024 * 1024)


def window_shape(tile):
    return (tile[0] // STRIP, STRIP * tile[1], (STRIP + 2 * RADIUS) * (tile[1] + 2 * SIDE))


def attention_cost(tile, groups, part):
    strips, count, window = window_shape(tile)
    flops = 4 * 2 * groups * strips * GROUP * count * window * part
    return pl.CostEstimate(flops=flops, bytes_accessed=4 * 1024 * 1024, transcendentals=0)


def run_queries(place, queries, grads, keys, values, head_dim, tile):
    tokens, width = queries.shape
    ext = keys.shape[0]
    part = GROUP * head_dim
    groups = width // part
    return pl.pallas_call(
        functools.partial(query_pass, head_dim, tile),
        grid=(groups,),
        in_specs=[
            SCALARS,
            columns(tokens, part),
            columns(tokens, part),
            columns(ext, part),
            columns(ext, part),
        ],
        out_specs=[pair_columns(tokens, part), whole((tokens, 128))],
        out_shape=[
            jax.ShapeDtypeStruct((2, tokens, width), BF),
            jax.ShapeDtypeStruct((tokens, 128), F32),
        ],
        scratch_shapes=[pltpu.VMEM(window_shape(tile), F32)],
        compiler_params=pltpu.CompilerParams(**PARAMS),
        cost_estimate=attention_cost(tile, groups, part),
        name="query_pass",
    )(place, queries, grads, keys, values)


def run_keys(place, keys, values, queries, grads, stats, head_dim, tile, first, groups):
    tokens = tile[0] * tile[1]
    ext = queries.shape[0]
    part = GROUP * head_dim
    return pl.pallas_call(
        functools.partial(key_pass, head_dim, tile, first),
        grid=(groups,),
        in_specs=[SCALARS] + [columns(ext, part, first)] * 4 + [whole(stats.shape)],
        out_specs=pair_columns(tokens, part),
        out_shape=jax.ShapeDtypeStruct((2, tokens, groups * part), BF),
        scratch_shapes=[pltpu.VMEM(window_shape(tile), F32), pltpu.VMEM((128, ext), F32)],
        compiler_params=pltpu.CompilerParams(**PARAMS),
        cost_estimate=attention_cost(tile, groups, part),
        name="key_pass",
    )(place, keys, values, queries, grads, stats)


def own_part(array, index, axis):
    return lax.dynamic_index_in_dim(array, index, axis, keepdims=False)


def product_t(left, right):
    return lax.dot_general(left, right, (((0,), (0,)), ((), ())), preferred_element_type=F32)


def slide_swap(array, high):
    return swapped(array, "slide", lax.axis_size("slide") // 2 if high else 1)


def partners(across_slides):
    if across_slides:
        index = lax.axis_index("slide") // 2
        return index, [(1, 1 - index)]
    index = lax.axis_index("gy")
    return index, [(by, index ^ by) for by in range(1, lax.axis_size("gy"))]


def sent(block, across_slides, by):
    return slide_swap(block, True) if across_slides else swapped(block, "gy", by)


def pick_rows(array, index, across_slides):
    rows = array.shape[1] // lax.axis_size("slide")
    core = lax.axis_index("slide") % 2
    if across_slides:
        return lax.dynamic_slice_in_dim(array, (2 * index + core) * rows, rows, axis=1)
    rest = rows // lax.axis_size("gy")
    parts = [
        lax.dynamic_slice_in_dim(array, (2 * high + core) * rows + index * rest, rest, axis=1)
        for high in range(lax.axis_size("slide") // 2)
    ]
    return jnp.concatenate(parts, axis=1)


def pair_product(lefts, rights, index, across_slides):
    total = None
    for left, right in zip(lefts, rights):
        term = product_t(pick_rows(left, index, across_slides), right)
        total = term if total is None else total + term
    return total


def first_blocks(lefts, rights, across_slides):
    return [
        pair_product(lefts, rights, target, across_slides).astype(BF)
        for _, target in partners(across_slides)[1]
    ]


def first_halving(blocks, lefts, rights, across_slides):
    index, others = partners(across_slides)
    arrived = [sent(block, across_slides, by) for block, (by, _) in zip(blocks, others)]
    mine = pair_product(lefts, rights, index, across_slides)
    for block in arrived:
        mine = mine + block.astype(F32)
    return mine


def second_halving(part, across_slides):
    index, others = partners(across_slides)
    rows = part.shape[0] // (len(others) + 1)
    mine = lax.dynamic_slice_in_dim(part, index * rows, rows, axis=0)
    for by, target in others:
        block = lax.dynamic_slice_in_dim(part, target * rows, rows, axis=0).astype(BF)
        mine = mine + sent(block, across_slides, by).astype(F32)
    return mine


def reduce_columns(part):
    count = lax.axis_size("gx")
    index = lax.axis_index("gx")
    rows = part.shape[0] // count
    mine = lax.dynamic_slice_in_dim(part, index * rows, rows, axis=0)
    arrived = []
    for by in range(count - 1, 0, -1):
        block = lax.dynamic_slice_in_dim(part, (index ^ by) * rows, rows, axis=0)
        arrived.append(swapped(block.astype(BF), "gx", by))
    for block in arrived:
        mine = mine + block.astype(F32)
    return mine


def second_halvings(one, two):
    return jnp.concatenate([second_halving(one, False), second_halving(two, True)], axis=1)


def after(array, *earlier):
    return lax.optimization_barrier((array, *earlier))[0]


def local(tokens, weights, norm_gain, tissue, cotangent):
    tile_tokens = tokens[0]
    tile_rows, tile_cols, model_width = tile_tokens.shape
    tile = (tile_rows, tile_cols)
    head_dim = model_width // HEADS
    token_count = tile_rows * tile_cols
    slides = lax.axis_size("slide")
    rows_count = lax.axis_size("gy")
    cols_count = lax.axis_size("gx")
    weight_in = weights[:, : 3 * model_width]
    weight_out = weights[:, 3 * model_width :]
    face = RADIUS * tile_cols
    at_top = lax.axis_index("gy") == 0
    place = jnp.stack(
        [
            lax.axis_index("gy") * tile_rows,
            lax.axis_index("gx") * tile_cols,
            jnp.int32(tile_rows * rows_count),
            jnp.int32(tile_cols * cols_count),
            jnp.where(at_top, token_count - face, 0),
        ]
    ).astype(jnp.int32)

    flat = (token_count, model_width)
    grid = (tile_rows, tile_cols, model_width)
    tissue_mask = tissue[0].astype(F32).reshape(token_count, 1)
    tokens_flat = tile_tokens.reshape(flat)
    cot_flat = cotangent[0].reshape(flat)
    both, facing, moments = run_prepare(
        place, tokens_flat, cot_flat, tissue_mask, norm_gain.reshape(1, model_width), face
    )
    both_tile = both.reshape(tile_rows, tile_cols, 2 * model_width)
    rows = rows_around(both_tile, facing.reshape(RADIUS, tile_cols, 2 * model_width))
    middle = column_halo(both_tile)
    both_ext = with_rows(middle, [column_halo(row) for row in rows])
    ext_rows, ext_cols = both_ext.shape[:2]
    ext = (ext_rows * ext_cols, -1)
    normed_ext = both_ext[:, :, :model_width].reshape(ext)
    branch_ext = both_ext[:, :, model_width:].reshape(ext)

    normed, branch_flat = both[:, :model_width], both[:, model_width:]
    both_other = slide_swap(both, False)
    normed_pair = (normed, both_other[:, :model_width])
    branch_pair = (branch_flat, both_other[:, model_width:])
    grad_attn = times_t(branch_flat, weight_out).astype(BF)
    queries = times(normed, weight_in[:, :model_width]).astype(BF)
    key_ext = times(normed_ext, weight_in[:, model_width : 2 * model_width]).astype(BF)
    value_ext = times(normed_ext, weight_in[:, 2 * model_width :]).astype(BF)

    found, stats = run_queries(place, queries, grad_attn, key_ext, value_ext, head_dim, tile)
    attended, grad_queries = found[0], found[1]

    found_other = slide_swap(found, False)
    attended_pair = (attended, found_other[0])
    grad_query_pair = (grad_queries, found_other[1])
    first_sent = first_blocks(normed_pair, grad_query_pair, True)
    second_sent = first_blocks(attended_pair, branch_pair, False)

    stats_tile = stats.reshape(tile_rows, tile_cols, -1)
    stats_rows = with_rows(stats_tile, rows_around(stats_tile))
    stats_rows = after(stats_rows, *first_sent, *second_sent)
    stats_ext = column_halo(stats_rows).reshape(ext)
    one = first_halving(first_sent, normed_pair, grad_query_pair, True)
    two = first_halving(second_sent, attended_pair, branch_pair, False)

    normed_late, branch_late, _ = lax.optimization_barrier((normed_ext, branch_ext, stats_rows))
    query_ext = times(normed_late, weight_in[:, :model_width]).astype(BF)
    grad_ext = times_t(branch_late, weight_out).astype(BF)

    stats_ext, one, two = lax.optimization_barrier((stats_ext, one, two))
    groups = HEADS // GROUP
    owed = run_keys(
        place, key_ext, value_ext, query_ext, grad_ext, stats_ext, head_dim, tile, 0, groups
    )
    grad_keys, grad_values = owed[0], owed[1]
    owed_other = slide_swap(owed, False)
    grad_key_pair = (grad_keys, owed_other[0])
    grad_value_pair = (grad_values, owed_other[1])
    third_sent = first_blocks(normed_pair, grad_key_pair, True)
    fourth_sent = first_blocks(normed_pair, grad_value_pair, False)
    first_part = second_halvings(one, two)
    three = first_halving(third_sent, normed_pair, grad_key_pair, True)
    four = first_halving(fourth_sent, normed_pair, grad_value_pair, False)
    first_sums = reduce_columns(after(first_part, *third_sent, *fourth_sent))
    second_sums = reduce_columns(second_halvings(three, four))

    late = lax.optimization_barrier((attended, grad_keys, grad_values, third_sent, fourth_sent))
    attended_late, keys_late, values_late = late[:3]
    projection = times(attended_late, weight_out)
    block_output = (tokens_flat.astype(F32) + tissue_mask * projection).astype(BF)

    grad_projected = jnp.concatenate([grad_queries, keys_late, values_late], axis=-1)
    scaled = times_t(grad_projected, weight_in) * norm_gain
    inverse = moments[:, 1:2]
    normalized = (tokens_flat.astype(F32) - moments[:, :1]) * inverse
    first_mean = jnp.mean(scaled, axis=-1, keepdims=True)
    second_mean = jnp.mean(scaled * normalized, axis=-1, keepdims=True)
    input_grad = inverse * (scaled - first_mean - normalized * second_mean)
    input_grad = (cot_flat.astype(F32) + input_grad).astype(BF)

    inv_root = 1.0 / math.sqrt(slides * rows_count * cols_count * token_count)
    width = model_width
    weight_grads = jnp.concatenate(
        [first_sums[:, :width], second_sums, first_sums[:, width:]], axis=1
    )
    return (
        block_output.reshape((1,) + grid),
        input_grad.reshape((1,) + grid),
        weight_grads * inv_root,
    )


def solution(mesh):
    tile = P("slide", "gy", "gx", None)
    return jax.shard_map(
        local,
        mesh=mesh,
        in_specs=(tile, P(), P(), P("slide", "gy", "gx"), tile),
        out_specs=(tile, tile, P(("slide", "gy", "gx"), None)),
        check_vma=False,
    )
```

```python
import functools
import math

import jax
import jax.numpy as jnp
from jax import lax
from jax.experimental import pallas as pl
from jax.experimental.pallas import tpu as pltpu
from jax.sharding import PartitionSpec as P

HEADS = 16
RADIUS = 6
EPSILON = 1e-06
STRIP = 4
GROUP = 4
SIDE = 8
BF = jnp.bfloat16
F32 = jnp.float32


def swapped(array, axis, by):
    count = lax.axis_size(axis)
    return lax.ppermute(array, axis, [(i, i ^ by) for i in range(count)])


def moved(array, axis, by):
    count = lax.axis_size(axis)
    pairs = [(i, i + by) for i in range(count) if 0 <= i + by < count]
    return lax.ppermute(array, axis, pairs)


def rows_around(block, facing=None):
    rows_count = lax.axis_size("gy")
    if rows_count == 2:
        at_top = lax.axis_index("gy") == 0
        if facing is None:
            facing = jnp.where(at_top, block[-RADIUS:], block[:RADIUS])
        return (swapped(facing, "gy", 1),)
    return (moved(block[-RADIUS:], "gy", 1), moved(block[:RADIUS], "gy", -1))


def with_rows(block, rows):
    if len(rows) == 1:
        at_top = lax.axis_index("gy") == 0
        zero = jnp.zeros((), block.dtype)
        rows = (jnp.where(at_top, zero, rows[0]), jnp.where(at_top, rows[0], zero))
    return jnp.concatenate([rows[0], block, rows[1]], axis=0)


def column_halo(block):
    count = lax.axis_size("gx")
    even = lax.axis_index("gx") % 2 == 0
    first, last = block[:, :SIDE], block[:, -SIDE:]
    pairs = []
    for start in range(2):
        for low in range(start, count - 1, 2):
            pairs += [(start, low, low + 1), (start, low + 1, low)]
    one = lax.ppermute(jnp.where(even, last, first), "gx", [p[1:] for p in pairs if p[0] == 0])
    two = lax.ppermute(jnp.where(even, first, last), "gx", [p[1:] for p in pairs if p[0] == 1])
    right, left = jnp.where(even, one, two), jnp.where(even, two, one)
    return jnp.concatenate([block, right, left], axis=1)


def prepare(place_ref, x_ref, c_ref, t_ref, gain_ref, both_ref, face_ref, moment_ref):
    block, width = x_ref.shape
    step = pl.program_id(0)
    rows = pl.ds(pl.multiple_of(step * block, block), block)
    x = x_ref[...].astype(F32)
    mean = jnp.sum(x, axis=1, keepdims=True) * (1.0 / width)
    centered = x - mean
    variance = jnp.sum(centered * centered, axis=1, keepdims=True) * (1.0 / width)
    inverse = lax.rsqrt(variance + EPSILON)
    both_ref[rows, :width] = (centered * inverse * gain_ref[...]).astype(BF)
    both_ref[rows, width:] = (c_ref[...].astype(F32) * t_ref[...]).astype(BF)
    lane = lax.broadcasted_iota(jnp.int32, moment_ref.shape, 1)
    moment_ref[...] = jnp.where(lane == 0, mean, inverse)

    @pl.when(step == pl.num_programs(0) - 1)
    def _():
        first = pl.multiple_of(place_ref[4], 16)
        face_ref[...] = both_ref[pl.ds(first, face_ref.shape[0]), :]


def run_prepare(place, tokens, cotangent, tissue, gain, face):
    count, width = tokens.shape
    block = min(count, 64)
    part = lambda columns: pl.BlockSpec((block, columns), lambda step: (step, 0))
    return pl.pallas_call(
        prepare,
        grid=(count // block,),
        in_specs=[SCALARS, part(width), part(width), part(1), whole((1, width))],
        out_specs=[whole((count, 2 * width)), whole((face, 2 * width)), part(128)],
        out_shape=[
            jax.ShapeDtypeStruct((count, 2 * width), BF),
            jax.ShapeDtypeStruct((face, 2 * width), BF),
            jax.ShapeDtypeStruct((count, 128), F32),
        ],
        compiler_params=pltpu.CompilerParams(**PARAMS),
        cost_estimate=pl.CostEstimate(flops=0, bytes_accessed=3 * 1024 * 1024, transcendentals=0),
        name="prepare",
    )(place, tokens, cotangent, tissue, gain)


def spread_heads(block, head_dim):
    lane_head = lax.broadcasted_iota(jnp.int32, block.shape, 1) // head_dim
    zero = jnp.zeros_like(block)
    return jnp.concatenate(
        [jnp.where(lane_head == head, block, zero) for head in range(GROUP)], axis=0
    )


def gather_heads(full, count, head_dim):
    lane_head = lax.broadcasted_iota(jnp.int32, (count, full.shape[1]), 1) // head_dim
    result = full[:count]
    for head in range(1, GROUP):
        result = jnp.where(lane_head == head, full[head * count : (head + 1) * count], result)
    return result


def times(left, right):
    return jnp.dot(left, right, preferred_element_type=F32)


def times_t(left, right):
    return lax.dot_general(left, right, (((1,), (1,)), ((), ())), preferred_element_type=F32)


def fill_bias(place_ref, bias_ref, tile_rows, tile_cols):
    strips, count, window = bias_ref.shape
    slots = tile_cols + 2 * SIDE
    own = lax.broadcasted_iota(jnp.int32, (count, window), 0)
    near = lax.broadcasted_iota(jnp.int32, (count, window), 1)
    own_row, own_col = own // tile_cols, own % tile_cols
    near_row, slot = near // slots, near % slots
    near_col = jnp.where(slot < tile_cols + SIDE, slot, slot - slots)
    row_gap = near_row - RADIUS - own_row
    col_gap = near_col - own_col
    col = place_ref[1] + near_col
    allowed = (jnp.abs(row_gap) <= RADIUS) & (jnp.abs(col_gap) <= RADIUS)
    allowed = allowed & (col >= 0) & (col < place_ref[3])
    for strip in range(strips):
        row = place_ref[0] + strip * STRIP + near_row - RADIUS
        kept = allowed & (row >= 0) & (row < place_ref[2])
        bias_ref[strip] = jnp.where(kept, 0.0, -1e30).astype(F32)


def query_pass(
    head_dim,
    tile,
    place_ref,
    q_ref,
    g_ref,
    normed_ref,
    key_w_ref,
    value_w_ref,
    out_ref,
    stat_ref,
    k_ref,
    v_ref,
    bias_ref,
):
    scaling = 1.0 / math.sqrt(head_dim)
    strips, count, window = bias_ref.shape
    step = (tile[1] + 2 * SIDE) * STRIP
    group = pl.program_id(0)

    @pl.when(group == 0)
    def _():
        fill_bias(place_ref, bias_ref, *tile)
        stat_ref[...] = jnp.zeros_like(stat_ref)

    k_ref[...] = times(normed_ref[...], key_w_ref[...]).astype(BF)
    v_ref[...] = times(normed_ref[...], value_w_ref[...]).astype(BF)
    lane = lax.broadcasted_iota(jnp.int32, (count, 128), 1) - group * (2 * GROUP)

    def dots(strip):
        own = pl.ds(strip * count, count)
        near = pl.ds(strip * step, window)
        queries = spread_heads(q_ref[own, :] * jnp.asarray(scaling, BF), head_dim)
        grads = spread_heads(g_ref[own, :], head_dim)
        return times_t(queries, k_ref[near, :]), times_t(grads, v_ref[near, :])

    ahead = dots(0)
    for strip in range(strips):
        own = pl.ds(strip * count, count)
        near = pl.ds(strip * step, window)
        scores, grad_probs = ahead
        if strip + 1 < strips:
            ahead = dots(strip + 1)
        stats = stat_ref[own, :]
        probs_parts, grad_parts = [], []
        for head in range(GROUP):
            part = slice(head * count, (head + 1) * count)
            masked = scores[part] + bias_ref[strip]
            row_max = jnp.max(masked, axis=1, keepdims=True)
            exponent = jnp.exp(masked - row_max)
            grad_part = grad_probs[part]
            total = jnp.sum(exponent, axis=1, keepdims=True)
            share = 1.0 / total
            delta = jnp.sum(exponent * grad_part, axis=1, keepdims=True) * share
            probs = exponent * share
            probs_parts.append(probs.astype(BF))
            grad_parts.append((probs * (grad_part - delta)).astype(BF))
            stats = jnp.where(lane == 2 * head, row_max + jnp.log(total), stats)
            stats = jnp.where(lane == 2 * head + 1, delta, stats)
        attended = times(jnp.concatenate(probs_parts, axis=0), v_ref[near, :])
        grad_queries = times(jnp.concatenate(grad_parts, axis=0), k_ref[near, :])
        out_ref[0, own, :] = gather_heads(attended, count, head_dim).astype(BF)
        out_ref[1, own, :] = (gather_heads(grad_queries, count, head_dim) * scaling).astype(BF)
        stat_ref[own, :] = stats


def key_pass(
    head_dim,
    tile,
    first,
    place_ref,
    k_ref,
    v_ref,
    q_ref,
    g_ref,
    stat_ref,
    out_ref,
    bias_ref,
    turned,
):
    scaling = 1.0 / math.sqrt(head_dim)
    strips, count, window = bias_ref.shape
    slots = tile[1] + 2 * SIDE
    step = slots * STRIP
    group = pl.program_id(0)

    @pl.when(group == 0)
    def _():
        fill_bias(place_ref, bias_ref, *tile)
        turned[...] = stat_ref[...].T

    part_width = q_ref.shape[1]
    keys_at = pl.multiple_of(group * part_width, part_width)
    values_at = pl.multiple_of((group + pl.num_programs(0)) * part_width, part_width)
    rows = pl.ds(pl.multiple_of((group + first) * (2 * GROUP), 2 * GROUP), 2 * GROUP)

    def own_tokens(ref, strip):
        starts = [(RADIUS + strip * STRIP + row) * slots for row in range(STRIP)]
        return jnp.concatenate([ref[pl.ds(start, tile[1]), :] for start in starts], axis=0)

    def dots(strip):
        near = pl.ds(strip * step, window)
        keys = spread_heads(own_tokens(k_ref, strip) * jnp.asarray(scaling, BF), head_dim)
        values = spread_heads(own_tokens(v_ref, strip), head_dim)
        return times_t(keys, q_ref[near, :]), times_t(values, g_ref[near, :])

    def finish(strip, probs, grads):
        own = pl.ds(strip * count, count)
        near = pl.ds(strip * step, window)
        grad_values = gather_heads(times(probs, g_ref[near, :]), count, head_dim)
        grad_keys = gather_heads(times(grads, q_ref[near, :]), count, head_dim) * scaling
        out_ref[own, pl.ds(values_at, part_width)] = grad_values.astype(BF)
        out_ref[own, pl.ds(keys_at, part_width)] = grad_keys.astype(BF)

    ahead = dots(0)
    behind = None
    for strip in range(strips):
        near = pl.ds(strip * step, window)
        scores, grad_probs = ahead
        if strip + 1 < strips:
            ahead = dots(strip + 1)
        stats = turned[rows, near]
        probs_parts, grad_parts = [], []
        for head in range(GROUP):
            part = slice(head * count, (head + 1) * count)
            masked = scores[part] + bias_ref[strip]
            probs = jnp.exp(masked - stats[2 * head : 2 * head + 1])
            centred = grad_probs[part] - stats[2 * head + 1 : 2 * head + 2]
            probs_parts.append(probs.astype(BF))
            grad_parts.append((probs * centred).astype(BF))
        if strip > 0:
            finish(strip - 1, *behind)
        behind = (jnp.concatenate(probs_parts, axis=0), jnp.concatenate(grad_parts, axis=0))
    finish(strips - 1, *behind)


def whole(shape):
    return pl.BlockSpec(shape, lambda group: (0,) * len(shape))


def columns(rows, width, first=0):
    return pl.BlockSpec((rows, width), lambda group: (0, first + group))


def pair_columns(rows, width):
    return pl.BlockSpec((2, rows, width), lambda group: (0, 0, group))


SCALARS = pl.BlockSpec(memory_space=pltpu.SMEM)
PARAMS = dict(vmem_limit_bytes=24 * 1024 * 1024)


def window_shape(tile):
    return (tile[0] // STRIP, STRIP * tile[1], (STRIP + 2 * RADIUS) * (tile[1] + 2 * SIDE))


def attention_cost(tile, groups, part):
    strips, count, window = window_shape(tile)
    flops = 4 * 2 * groups * strips * GROUP * count * window * part
    return pl.CostEstimate(flops=flops, bytes_accessed=4 * 1024 * 1024, transcendentals=0)


def run_queries(place, queries, grads, normed_ext, weights, head_dim, tile):
    tokens, width = queries.shape
    ext = normed_ext.shape[0]
    part = GROUP * head_dim
    groups = width // part
    return pl.pallas_call(
        functools.partial(query_pass, head_dim, tile),
        grid=(groups,),
        in_specs=[
            SCALARS,
            columns(tokens, part),
            columns(tokens, part),
            whole(normed_ext.shape),
            columns(width, part, groups),
            columns(width, part, 2 * groups),
        ],
        out_specs=[
            pair_columns(tokens, part),
            whole((tokens, 128)),
            columns(ext, part),
            columns(ext, part),
        ],
        out_shape=[
            jax.ShapeDtypeStruct((2, tokens, width), BF),
            jax.ShapeDtypeStruct((tokens, 128), F32),
            jax.ShapeDtypeStruct((ext, width), BF),
            jax.ShapeDtypeStruct((ext, width), BF),
        ],
        scratch_shapes=[pltpu.VMEM(window_shape(tile), F32)],
        compiler_params=pltpu.CompilerParams(**PARAMS),
        cost_estimate=attention_cost(tile, groups, part),
        name="query_pass",
    )(place, queries, grads, normed_ext, weights, weights)


def run_keys(place, keys, values, queries, grads, stats, head_dim, tile, first, groups):
    tokens = tile[0] * tile[1]
    ext = queries.shape[0]
    part = GROUP * head_dim
    return pl.pallas_call(
        functools.partial(key_pass, head_dim, tile, first),
        grid=(groups,),
        in_specs=[SCALARS] + [columns(ext, part, first)] * 4 + [whole(stats.shape)],
        out_specs=whole((tokens, 2 * groups * part)),
        out_shape=jax.ShapeDtypeStruct((tokens, 2 * groups * part), BF),
        scratch_shapes=[pltpu.VMEM(window_shape(tile), F32), pltpu.VMEM((128, ext), F32)],
        compiler_params=pltpu.CompilerParams(**PARAMS),
        cost_estimate=attention_cost(tile, groups, part),
        name="key_pass",
    )(place, keys, values, queries, grads, stats)


def own_part(array, index, axis):
    return lax.dynamic_index_in_dim(array, index, axis, keepdims=False)


def product_t(left, right):
    return lax.dot_general(left, right, (((0,), (0,)), ((), ())), preferred_element_type=F32)


def slide_swap(array, high):
    return swapped(array, "slide", lax.axis_size("slide") // 2 if high else 1)


def partners(across_slides):
    if across_slides:
        index = lax.axis_index("slide") // 2
        return index, [(1, 1 - index)]
    index = lax.axis_index("gy")
    return index, [(by, index ^ by) for by in range(1, lax.axis_size("gy"))]


def sent(block, across_slides, by):
    return slide_swap(block, True) if across_slides else swapped(block, "gy", by)


def pick_rows(array, index, across_slides, width):
    rows = width // lax.axis_size("slide")
    core = lax.axis_index("slide") % 2
    if across_slides:
        return lax.dynamic_slice_in_dim(array, (2 * index + core) * rows, rows, axis=1)
    rest = rows // lax.axis_size("gy")
    parts = [
        lax.dynamic_slice_in_dim(array, (2 * high + core) * rows + index * rest, rest, axis=1)
        for high in range(lax.axis_size("slide") // 2)
    ]
    return jnp.concatenate(parts, axis=1)


def pair_product(lefts, rights, index, across_slides):
    total = None
    for left, right in zip(lefts, rights):
        term = product_t(pick_rows(left, index, across_slides, right.shape[1]), right)
        total = term if total is None else total + term
    return total


def first_blocks(lefts, rights, across_slides):
    return [
        pair_product(lefts, rights, target, across_slides).astype(BF)
        for _, target in partners(across_slides)[1]
    ]


def first_halving(blocks, lefts, rights, across_slides):
    index, others = partners(across_slides)
    arrived = [sent(block, across_slides, by) for block, (by, _) in zip(blocks, others)]
    mine = pair_product(lefts, rights, index, across_slides)
    for block in arrived:
        mine = mine + block.astype(F32)
    return mine


def second_halving(part, across_slides):
    index, others = partners(across_slides)
    rows = part.shape[0] // (len(others) + 1)
    mine = lax.dynamic_slice_in_dim(part, index * rows, rows, axis=0)
    for by, target in others:
        block = lax.dynamic_slice_in_dim(part, target * rows, rows, axis=0).astype(BF)
        mine = mine + sent(block, across_slides, by).astype(F32)
    return mine


def reduce_columns(part):
    count = lax.axis_size("gx")
    index = lax.axis_index("gx")
    rows = part.shape[0] // count
    mine = lax.dynamic_slice_in_dim(part, index * rows, rows, axis=0)
    arrived = []
    for by in range(count - 1, 0, -1):
        block = lax.dynamic_slice_in_dim(part, (index ^ by) * rows, rows, axis=0)
        arrived.append(swapped(block.astype(BF), "gx", by))
    for block in arrived:
        mine = mine + block.astype(F32)
    return mine


def second_halvings(one, two):
    return jnp.concatenate([second_halving(one, False), second_halving(two, True)], axis=1)


def after(array, *earlier):
    return lax.optimization_barrier((array, *earlier))[0]


def local(tokens, weights, norm_gain, tissue, cotangent):
    tile_tokens = tokens[0]
    tile_rows, tile_cols, model_width = tile_tokens.shape
    tile = (tile_rows, tile_cols)
    head_dim = model_width // HEADS
    token_count = tile_rows * tile_cols
    slides = lax.axis_size("slide")
    rows_count = lax.axis_size("gy")
    cols_count = lax.axis_size("gx")
    weight_in = weights[:, : 3 * model_width]
    weight_out = weights[:, 3 * model_width :]
    face = RADIUS * tile_cols
    at_top = lax.axis_index("gy") == 0
    place = jnp.stack(
        [
            lax.axis_index("gy") * tile_rows,
            lax.axis_index("gx") * tile_cols,
            jnp.int32(tile_rows * rows_count),
            jnp.int32(tile_cols * cols_count),
            jnp.where(at_top, token_count - face, 0),
        ]
    ).astype(jnp.int32)

    flat = (token_count, model_width)
    grid = (tile_rows, tile_cols, model_width)
    tissue_mask = tissue[0].astype(F32).reshape(token_count, 1)
    tokens_flat = tile_tokens.reshape(flat)
    cot_flat = cotangent[0].reshape(flat)
    both, facing, moments = run_prepare(
        place, tokens_flat, cot_flat, tissue_mask, norm_gain.reshape(1, model_width), face
    )
    both_tile = both.reshape(tile_rows, tile_cols, 2 * model_width)
    rows = rows_around(both_tile, facing.reshape(RADIUS, tile_cols, 2 * model_width))
    middle = column_halo(both_tile)
    both_ext = with_rows(middle, [column_halo(row) for row in rows])
    ext_rows, ext_cols = both_ext.shape[:2]
    ext = (ext_rows * ext_cols, -1)
    normed_ext = both_ext[:, :, :model_width].reshape(ext)
    branch_ext = both_ext[:, :, model_width:].reshape(ext)

    normed, branch_flat = both[:, :model_width], both[:, model_width:]
    both_other = slide_swap(both, False)
    normed_pair = (both, both_other)
    branch_pair = (branch_flat, both_other[:, model_width:])
    grad_attn = times_t(branch_flat, weight_out).astype(BF)
    queries = times(normed, weight_in[:, :model_width]).astype(BF)

    found, stats, key_ext, value_ext = run_queries(
        place, queries, grad_attn, normed_ext, weights, head_dim, tile
    )
    attended, grad_queries = found[0], found[1]

    found_other = slide_swap(found, False)
    attended_pair = (attended, found_other[0])
    grad_query_pair = (grad_queries, found_other[1])
    first_sent = first_blocks(normed_pair, grad_query_pair, True)
    second_sent = first_blocks(attended_pair, branch_pair, False)

    stats_tile = stats.reshape(tile_rows, tile_cols, -1)
    stats_rows = with_rows(stats_tile, rows_around(stats_tile))
    stats_rows = after(stats_rows, *first_sent, *second_sent)
    stats_ext = column_halo(stats_rows).reshape(ext)
    one = first_halving(first_sent, normed_pair, grad_query_pair, True)
    two = first_halving(second_sent, attended_pair, branch_pair, False)

    normed_late, branch_late, _ = lax.optimization_barrier((normed_ext, branch_ext, stats_rows))
    query_ext = times(normed_late, weight_in[:, :model_width]).astype(BF)
    grad_ext = times_t(branch_late, weight_out).astype(BF)

    stats_ext, one, two = lax.optimization_barrier((stats_ext, one, two))
    half = HEADS // GROUP // 2
    held = (key_ext, value_ext, query_ext, grad_ext)
    owed_low = run_keys(place, *held, stats_ext, head_dim, tile, 0, half)
    first_part, stats_late = lax.optimization_barrier((second_halvings(one, two), stats_ext))
    owed_high = run_keys(place, *held, stats_late, head_dim, tile, half, half)
    low_other = slide_swap(owed_low, False)
    low_pair = lax.optimization_barrier((owed_low, low_other, owed_high))[:2]
    high_pair = (owed_high, slide_swap(owed_high, False))
    third_sent = first_blocks(normed_pair, low_pair, True)
    fourth_sent = first_blocks(normed_pair, high_pair, False)
    three = first_halving(third_sent, normed_pair, low_pair, True)
    four = first_halving(fourth_sent, normed_pair, high_pair, False)
    first_sums = reduce_columns(after(first_part, *third_sent, *fourth_sent))
    second_sums = reduce_columns(second_halvings(three, four))

    late = lax.optimization_barrier((attended, owed_low, owed_high, third_sent, fourth_sent))
    attended_late, low_late, high_late = late[:3]
    projection = times(attended_late, weight_out)
    block_output = (tokens_flat.astype(F32) + tissue_mask * projection).astype(BF)

    cut = model_width // 2
    grad_projected = jnp.concatenate(
        [grad_queries, low_late[:, :cut], high_late[:, :cut], low_late[:, cut:], high_late[:, cut:]],
        axis=-1,
    )
    scaled = times_t(grad_projected, weight_in) * norm_gain
    inverse = moments[:, 1:2]
    normalized = (tokens_flat.astype(F32) - moments[:, :1]) * inverse
    first_mean = jnp.mean(scaled, axis=-1, keepdims=True)
    second_mean = jnp.mean(scaled * normalized, axis=-1, keepdims=True)
    input_grad = inverse * (scaled - first_mean - normalized * second_mean)
    input_grad = (cot_flat.astype(F32) + input_grad).astype(BF)

    inv_root = 1.0 / math.sqrt(slides * rows_count * cols_count * token_count)
    width = model_width
    weight_grads = jnp.concatenate(
        [
            first_sums[:, :width],
            second_sums[:, :cut],
            second_sums[:, width : width + cut],
            second_sums[:, cut:width],
            second_sums[:, width + cut :],
            first_sums[:, width:],
        ],
        axis=1,
    )
    return (
        block_output.reshape((1,) + grid),
        input_grad.reshape((1,) + grid),
        weight_grads * inv_root,
    )


def solution(mesh):
    tile = P("slide", "gy", "gx", None)
    return jax.shard_map(
        local,
        mesh=mesh,
        in_specs=(tile, P(), P(), P("slide", "gy", "gx"), tile),
        out_specs=(tile, tile, P(("slide", "gy", "gx"), None)),
        check_vma=False,
    )
```

```python
import functools
import math

import jax
import jax.numpy as jnp
from jax import lax
from jax.experimental import pallas as pl
from jax.experimental.pallas import tpu as pltpu
from jax.sharding import PartitionSpec as P

HEADS = 16
RADIUS = 6
EPSILON = 1e-06
STRIP = 4
GROUP = 4
SIDE = 8
BF = jnp.bfloat16
F32 = jnp.float32


def swapped(array, axis, by):
    count = lax.axis_size(axis)
    return lax.ppermute(array, axis, [(i, i ^ by) for i in range(count)])


def moved(array, axis, by):
    count = lax.axis_size(axis)
    pairs = [(i, i + by) for i in range(count) if 0 <= i + by < count]
    return lax.ppermute(array, axis, pairs)


def rows_around(block, facing=None):
    rows_count = lax.axis_size("gy")
    if rows_count == 2:
        at_top = lax.axis_index("gy") == 0
        if facing is None:
            facing = jnp.where(at_top, block[-RADIUS:], block[:RADIUS])
        return (swapped(facing, "gy", 1),)
    return (moved(block[-RADIUS:], "gy", 1), moved(block[:RADIUS], "gy", -1))


def with_rows(block, rows):
    if len(rows) == 1:
        at_top = lax.axis_index("gy") == 0
        zero = jnp.zeros((), block.dtype)
        rows = (jnp.where(at_top, zero, rows[0]), jnp.where(at_top, rows[0], zero))
    return jnp.concatenate([rows[0], block, rows[1]], axis=0)


def column_halo(block):
    count = lax.axis_size("gx")
    even = lax.axis_index("gx") % 2 == 0
    first, last = block[:, :SIDE], block[:, -SIDE:]
    pairs = []
    for start in range(2):
        for low in range(start, count - 1, 2):
            pairs += [(start, low, low + 1), (start, low + 1, low)]
    one = lax.ppermute(jnp.where(even, last, first), "gx", [p[1:] for p in pairs if p[0] == 0])
    two = lax.ppermute(jnp.where(even, first, last), "gx", [p[1:] for p in pairs if p[0] == 1])
    right, left = jnp.where(even, one, two), jnp.where(even, two, one)
    return jnp.concatenate([block, right, left], axis=1)


def in_hbm(array):
    return pltpu.with_memory_space_constraint(array, pltpu.HBM)


def prepare(place_ref, x_ref, c_ref, t_ref, gain_ref, both_ref, face_ref, moment_ref):
    block, width = x_ref.shape
    step = pl.program_id(0)
    rows = pl.ds(pl.multiple_of(step * block, block), block)
    x = x_ref[...].astype(F32)
    mean = jnp.sum(x, axis=1, keepdims=True) * (1.0 / width)
    centered = x - mean
    variance = jnp.sum(centered * centered, axis=1, keepdims=True) * (1.0 / width)
    inverse = lax.rsqrt(variance + EPSILON)
    both_ref[rows, :width] = (centered * inverse * gain_ref[...]).astype(BF)
    both_ref[rows, width:] = (c_ref[...].astype(F32) * t_ref[...]).astype(BF)
    lane = lax.broadcasted_iota(jnp.int32, moment_ref.shape, 1)
    moment_ref[...] = jnp.where(lane == 0, mean, inverse)

    @pl.when(step == pl.num_programs(0) - 1)
    def _():
        first = pl.multiple_of(place_ref[4], 16)
        face_ref[...] = both_ref[pl.ds(first, face_ref.shape[0]), :]


def run_prepare(place, tokens, cotangent, tissue, gain, face):
    count, width = tokens.shape
    block = min(count, 64)
    part = lambda columns: pl.BlockSpec((block, columns), lambda step: (step, 0))
    return pl.pallas_call(
        prepare,
        grid=(count // block,),
        in_specs=[SCALARS, part(width), part(width), part(1), whole((1, width))],
        out_specs=[whole((count, 2 * width)), whole((face, 2 * width)), part(128)],
        out_shape=[
            jax.ShapeDtypeStruct((count, 2 * width), BF),
            jax.ShapeDtypeStruct((face, 2 * width), BF),
            jax.ShapeDtypeStruct((count, 128), F32),
        ],
        compiler_params=pltpu.CompilerParams(**PARAMS),
        cost_estimate=pl.CostEstimate(flops=0, bytes_accessed=3 * 1024 * 1024, transcendentals=0),
        name="prepare",
    )(place, in_hbm(tokens), in_hbm(cotangent), tissue, in_hbm(gain))


def spread_heads(block, head_dim):
    lane_head = lax.broadcasted_iota(jnp.int32, block.shape, 1) // head_dim
    zero = jnp.zeros_like(block)
    return jnp.concatenate(
        [jnp.where(lane_head == head, block, zero) for head in range(GROUP)], axis=0
    )


def gather_heads(full, count, head_dim):
    lane_head = lax.broadcasted_iota(jnp.int32, (count, full.shape[1]), 1) // head_dim
    result = full[:count]
    for head in range(1, GROUP):
        result = jnp.where(lane_head == head, full[head * count : (head + 1) * count], result)
    return result


def times(left, right):
    return jnp.dot(left, right, preferred_element_type=F32)


def times_t(left, right):
    return lax.dot_general(left, right, (((1,), (1,)), ((), ())), preferred_element_type=F32)


def fill_bias(place_ref, bias_ref, tile_rows, tile_cols):
    strips, count, window = bias_ref.shape
    slots = tile_cols + 2 * SIDE
    own = lax.broadcasted_iota(jnp.int32, (count, window), 0)
    near = lax.broadcasted_iota(jnp.int32, (count, window), 1)
    own_row, own_col = own // tile_cols, own % tile_cols
    near_row, slot = near // slots, near % slots
    near_col = jnp.where(slot < tile_cols + SIDE, slot, slot - slots)
    row_gap = near_row - RADIUS - own_row
    col_gap = near_col - own_col
    col = place_ref[1] + near_col
    allowed = (jnp.abs(row_gap) <= RADIUS) & (jnp.abs(col_gap) <= RADIUS)
    allowed = allowed & (col >= 0) & (col < place_ref[3])
    for strip in range(strips):
        row = place_ref[0] + strip * STRIP + near_row - RADIUS
        kept = allowed & (row >= 0) & (row < place_ref[2])
        bias_ref[strip] = jnp.where(kept, 0.0, -1e30).astype(F32)


def query_pass(
    head_dim,
    tile,
    place_ref,
    q_ref,
    g_ref,
    normed_ref,
    key_w_ref,
    value_w_ref,
    out_ref,
    stat_ref,
    k_ref,
    v_ref,
    bias_ref,
):
    scaling = 1.0 / math.sqrt(head_dim)
    strips, count, window = bias_ref.shape
    step = (tile[1] + 2 * SIDE) * STRIP
    group = pl.program_id(0)

    @pl.when(group == 0)
    def _():
        fill_bias(place_ref, bias_ref, *tile)
        stat_ref[...] = jnp.zeros_like(stat_ref)

    k_ref[...] = times(normed_ref[...], key_w_ref[...]).astype(BF)
    v_ref[...] = times(normed_ref[...], value_w_ref[...]).astype(BF)
    lane = lax.broadcasted_iota(jnp.int32, (count, 128), 1) - group * (2 * GROUP)

    def dots(strip):
        own = pl.ds(strip * count, count)
        near = pl.ds(strip * step, window)
        queries = spread_heads(q_ref[own, :] * jnp.asarray(scaling, BF), head_dim)
        grads = spread_heads(g_ref[own, :], head_dim)
        return times_t(queries, k_ref[near, :]), times_t(grads, v_ref[near, :])

    ahead = dots(0)
    for strip in range(strips):
        own = pl.ds(strip * count, count)
        near = pl.ds(strip * step, window)
        scores, grad_probs = ahead
        if strip + 1 < strips:
            ahead = dots(strip + 1)
        stats = stat_ref[own, :]
        probs_parts, grad_parts = [], []
        for head in range(GROUP):
            part = slice(head * count, (head + 1) * count)
            masked = scores[part] + bias_ref[strip]
            row_max = jnp.max(masked, axis=1, keepdims=True)
            exponent = jnp.exp(masked - row_max)
            grad_part = grad_probs[part]
            total = jnp.sum(exponent, axis=1, keepdims=True)
            share = 1.0 / total
            delta = jnp.sum(exponent * grad_part, axis=1, keepdims=True) * share
            probs = exponent * share
            probs_parts.append(probs.astype(BF))
            grad_parts.append((probs * (grad_part - delta)).astype(BF))
            stats = jnp.where(lane == 2 * head, row_max + jnp.log(total), stats)
            stats = jnp.where(lane == 2 * head + 1, delta, stats)
        attended = times(jnp.concatenate(probs_parts, axis=0), v_ref[near, :])
        grad_queries = times(jnp.concatenate(grad_parts, axis=0), k_ref[near, :])
        out_ref[0, own, :] = gather_heads(attended, count, head_dim).astype(BF)
        out_ref[1, own, :] = (gather_heads(grad_queries, count, head_dim) * scaling).astype(BF)
        stat_ref[own, :] = stats


def key_pass(
    head_dim,
    tile,
    first,
    place_ref,
    k_ref,
    v_ref,
    q_ref,
    g_ref,
    stat_ref,
    out_ref,
    bias_ref,
    turned,
):
    scaling = 1.0 / math.sqrt(head_dim)
    strips, count, window = bias_ref.shape
    slots = tile[1] + 2 * SIDE
    step = slots * STRIP
    group = pl.program_id(0)

    @pl.when(group == 0)
    def _():
        fill_bias(place_ref, bias_ref, *tile)
        turned[...] = stat_ref[...].T

    part_width = q_ref.shape[1]
    keys_at = pl.multiple_of(group * part_width, part_width)
    values_at = pl.multiple_of((group + pl.num_programs(0)) * part_width, part_width)
    rows = pl.ds(pl.multiple_of((group + first) * (2 * GROUP), 2 * GROUP), 2 * GROUP)

    def own_tokens(ref, strip):
        starts = [(RADIUS + strip * STRIP + row) * slots for row in range(STRIP)]
        return jnp.concatenate([ref[pl.ds(start, tile[1]), :] for start in starts], axis=0)

    def dots(strip):
        near = pl.ds(strip * step, window)
        keys = spread_heads(own_tokens(k_ref, strip) * jnp.asarray(scaling, BF), head_dim)
        values = spread_heads(own_tokens(v_ref, strip), head_dim)
        return times_t(keys, q_ref[near, :]), times_t(values, g_ref[near, :])

    def finish(strip, probs, grads):
        own = pl.ds(strip * count, count)
        near = pl.ds(strip * step, window)
        grad_values = gather_heads(times(probs, g_ref[near, :]), count, head_dim)
        grad_keys = gather_heads(times(grads, q_ref[near, :]), count, head_dim) * scaling
        out_ref[own, pl.ds(values_at, part_width)] = grad_values.astype(BF)
        out_ref[own, pl.ds(keys_at, part_width)] = grad_keys.astype(BF)

    ahead = dots(0)
    behind = None
    for strip in range(strips):
        near = pl.ds(strip * step, window)
        scores, grad_probs = ahead
        if strip + 1 < strips:
            ahead = dots(strip + 1)
        stats = turned[rows, near]
        probs_parts, grad_parts = [], []
        for head in range(GROUP):
            part = slice(head * count, (head + 1) * count)
            masked = scores[part] + bias_ref[strip]
            probs = jnp.exp(masked - stats[2 * head : 2 * head + 1])
            centred = grad_probs[part] - stats[2 * head + 1 : 2 * head + 2]
            probs_parts.append(probs.astype(BF))
            grad_parts.append((probs * centred).astype(BF))
        if strip > 0:
            finish(strip - 1, *behind)
        behind = (jnp.concatenate(probs_parts, axis=0), jnp.concatenate(grad_parts, axis=0))
    finish(strips - 1, *behind)


def whole(shape):
    return pl.BlockSpec(shape, lambda group: (0,) * len(shape))


def columns(rows, width, first=0):
    return pl.BlockSpec((rows, width), lambda group: (0, first + group))


def pair_columns(rows, width):
    return pl.BlockSpec((2, rows, width), lambda group: (0, 0, group))


SCALARS = pl.BlockSpec(memory_space=pltpu.SMEM)
PARAMS = dict(vmem_limit_bytes=24 * 1024 * 1024)


def window_shape(tile):
    return (tile[0] // STRIP, STRIP * tile[1], (STRIP + 2 * RADIUS) * (tile[1] + 2 * SIDE))


def attention_cost(tile, groups, part):
    strips, count, window = window_shape(tile)
    flops = 4 * 2 * groups * strips * GROUP * count * window * part
    return pl.CostEstimate(flops=flops, bytes_accessed=4 * 1024 * 1024, transcendentals=0)


def run_queries(place, queries, grads, normed_ext, weights, head_dim, tile):
    tokens, width = queries.shape
    ext = normed_ext.shape[0]
    part = GROUP * head_dim
    groups = width // part
    return pl.pallas_call(
        functools.partial(query_pass, head_dim, tile),
        grid=(groups,),
        in_specs=[
            SCALARS,
            columns(tokens, part),
            columns(tokens, part),
            whole(normed_ext.shape),
            columns(width, part, groups),
            columns(width, part, 2 * groups),
        ],
        out_specs=[
            pair_columns(tokens, part),
            whole((tokens, 128)),
            columns(ext, part),
            columns(ext, part),
        ],
        out_shape=[
            jax.ShapeDtypeStruct((2, tokens, width), BF),
            jax.ShapeDtypeStruct((tokens, 128), F32),
            jax.ShapeDtypeStruct((ext, width), BF),
            jax.ShapeDtypeStruct((ext, width), BF),
        ],
        scratch_shapes=[pltpu.VMEM(window_shape(tile), F32)],
        compiler_params=pltpu.CompilerParams(**PARAMS),
        cost_estimate=attention_cost(tile, groups, part),
        name="query_pass",
    )(place, queries, grads, normed_ext, in_hbm(weights), in_hbm(weights))


def run_keys(place, keys, values, queries, grads, stats, head_dim, tile, first, groups):
    tokens = tile[0] * tile[1]
    ext = queries.shape[0]
    part = GROUP * head_dim
    return pl.pallas_call(
        functools.partial(key_pass, head_dim, tile, first),
        grid=(groups,),
        in_specs=[SCALARS] + [columns(ext, part, first)] * 4 + [whole(stats.shape)],
        out_specs=whole((tokens, 2 * groups * part)),
        out_shape=jax.ShapeDtypeStruct((tokens, 2 * groups * part), BF),
        scratch_shapes=[pltpu.VMEM(window_shape(tile), F32), pltpu.VMEM((128, ext), F32)],
        compiler_params=pltpu.CompilerParams(**PARAMS),
        cost_estimate=attention_cost(tile, groups, part),
        name="key_pass",
    )(place, keys, values, queries, grads, stats)


def own_part(array, index, axis):
    return lax.dynamic_index_in_dim(array, index, axis, keepdims=False)


def product_t(left, right):
    return lax.dot_general(left, right, (((0,), (0,)), ((), ())), preferred_element_type=F32)


def slide_swap(array, high):
    return swapped(array, "slide", lax.axis_size("slide") // 2 if high else 1)


def partners(across_slides):
    if across_slides:
        index = lax.axis_index("slide") // 2
        return index, [(1, 1 - index)]
    index = lax.axis_index("gy")
    return index, [(by, index ^ by) for by in range(1, lax.axis_size("gy"))]


def sent(block, across_slides, by):
    return slide_swap(block, True) if across_slides else swapped(block, "gy", by)


def pick_rows(array, index, across_slides, width):
    rows = width // lax.axis_size("slide")
    core = lax.axis_index("slide") % 2
    if across_slides:
        return lax.dynamic_slice_in_dim(array, (2 * index + core) * rows, rows, axis=1)
    rest = rows // lax.axis_size("gy")
    parts = [
        lax.dynamic_slice_in_dim(array, (2 * high + core) * rows + index * rest, rest, axis=1)
        for high in range(lax.axis_size("slide") // 2)
    ]
    return jnp.concatenate(parts, axis=1)


def pair_product(lefts, rights, index, across_slides):
    total = None
    for left, right in zip(lefts, rights):
        term = product_t(pick_rows(left, index, across_slides, right.shape[1]), right)
        total = term if total is None else total + term
    return total


def first_blocks(lefts, rights, across_slides):
    return [
        pair_product(lefts, rights, target, across_slides).astype(BF)
        for _, target in partners(across_slides)[1]
    ]


def first_halving(blocks, lefts, rights, across_slides):
    index, others = partners(across_slides)
    arrived = [sent(block, across_slides, by) for block, (by, _) in zip(blocks, others)]
    mine = pair_product(lefts, rights, index, across_slides)
    for block in arrived:
        mine = mine + block.astype(F32)
    return mine


def second_halving(part, across_slides):
    index, others = partners(across_slides)
    rows = part.shape[0] // (len(others) + 1)
    mine = lax.dynamic_slice_in_dim(part, index * rows, rows, axis=0)
    for by, target in others:
        block = lax.dynamic_slice_in_dim(part, target * rows, rows, axis=0).astype(BF)
        mine = mine + sent(block, across_slides, by).astype(F32)
    return mine


def reduce_columns(part):
    count = lax.axis_size("gx")
    index = lax.axis_index("gx")
    rows = part.shape[0] // count
    mine = lax.dynamic_slice_in_dim(part, index * rows, rows, axis=0)
    arrived = []
    for by in range(count - 1, 0, -1):
        block = lax.dynamic_slice_in_dim(part, (index ^ by) * rows, rows, axis=0)
        arrived.append(swapped(block.astype(BF), "gx", by))
    for block in arrived:
        mine = mine + block.astype(F32)
    return mine


def second_halvings(one, two):
    return jnp.concatenate([second_halving(one, False), second_halving(two, True)], axis=1)


def after(array, *earlier):
    return lax.optimization_barrier((array, *earlier))[0]


def local(tokens, weights, norm_gain, tissue, cotangent):
    tile_tokens = tokens[0]
    tile_rows, tile_cols, model_width = tile_tokens.shape
    tile = (tile_rows, tile_cols)
    head_dim = model_width // HEADS
    token_count = tile_rows * tile_cols
    slides = lax.axis_size("slide")
    rows_count = lax.axis_size("gy")
    cols_count = lax.axis_size("gx")
    weight_in = weights[:, : 3 * model_width]
    weight_out = weights[:, 3 * model_width :]
    face = RADIUS * tile_cols
    at_top = lax.axis_index("gy") == 0
    place = jnp.stack(
        [
            lax.axis_index("gy") * tile_rows,
            lax.axis_index("gx") * tile_cols,
            jnp.int32(tile_rows * rows_count),
            jnp.int32(tile_cols * cols_count),
            jnp.where(at_top, token_count - face, 0),
        ]
    ).astype(jnp.int32)

    flat = (token_count, model_width)
    grid = (tile_rows, tile_cols, model_width)
    tissue_mask = tissue[0].astype(F32).reshape(token_count, 1)
    tokens_flat = tile_tokens.reshape(flat)
    cot_flat = cotangent[0].reshape(flat)
    both, facing, moments = run_prepare(
        place, tokens_flat, cot_flat, tissue_mask, norm_gain.reshape(1, model_width), face
    )
    both_tile = both.reshape(tile_rows, tile_cols, 2 * model_width)
    rows = rows_around(both_tile, facing.reshape(RADIUS, tile_cols, 2 * model_width))
    middle = column_halo(both_tile)
    both_ext = with_rows(middle, [column_halo(row) for row in rows])
    ext_rows, ext_cols = both_ext.shape[:2]
    ext = (ext_rows * ext_cols, -1)
    normed_ext = both_ext[:, :, :model_width].reshape(ext)
    branch_ext = both_ext[:, :, model_width:].reshape(ext)

    normed, branch_flat = both[:, :model_width], both[:, model_width:]
    both_other = slide_swap(both, False)
    normed_pair = (both, both_other)
    branch_pair = (branch_flat, both_other[:, model_width:])
    grad_attn = times_t(branch_flat, weight_out).astype(BF)
    queries = times(normed, weight_in[:, :model_width]).astype(BF)

    found, stats, key_ext, value_ext = run_queries(
        place, queries, grad_attn, normed_ext, weights, head_dim, tile
    )
    attended, grad_queries = found[0], found[1]

    found_other = slide_swap(found, False)
    attended_pair = (attended, found_other[0])
    grad_query_pair = (grad_queries, found_other[1])
    first_sent = first_blocks(normed_pair, grad_query_pair, True)
    second_sent = first_blocks(attended_pair, branch_pair, False)

    stats_tile = stats.reshape(tile_rows, tile_cols, -1)
    stats_rows = with_rows(stats_tile, rows_around(stats_tile))
    stats_rows = after(stats_rows, *first_sent, *second_sent)
    stats_ext = column_halo(stats_rows).reshape(ext)
    one = first_halving(first_sent, normed_pair, grad_query_pair, True)
    two = first_halving(second_sent, attended_pair, branch_pair, False)

    normed_late, branch_late, _ = lax.optimization_barrier((normed_ext, branch_ext, stats_rows))
    query_ext = times(normed_late, weight_in[:, :model_width]).astype(BF)
    grad_ext = times_t(branch_late, weight_out).astype(BF)

    stats_ext, one, two = lax.optimization_barrier((stats_ext, one, two))
    half = HEADS // GROUP // 2
    held = (key_ext, value_ext, query_ext, grad_ext)
    owed_low = run_keys(place, *held, stats_ext, head_dim, tile, 0, half)
    first_part, stats_late = lax.optimization_barrier((second_halvings(one, two), stats_ext))
    owed_high = run_keys(place, *held, stats_late, head_dim, tile, half, half)
    low_other = slide_swap(owed_low, False)
    low_pair = lax.optimization_barrier((owed_low, low_other, owed_high))[:2]
    high_pair = (owed_high, slide_swap(owed_high, False))
    third_sent = first_blocks(normed_pair, low_pair, True)
    fourth_sent = first_blocks(normed_pair, high_pair, False)
    three = first_halving(third_sent, normed_pair, low_pair, True)
    four = first_halving(fourth_sent, normed_pair, high_pair, False)
    first_sums = reduce_columns(after(first_part, *third_sent, *fourth_sent))
    second_sums = reduce_columns(second_halvings(three, four))

    late = lax.optimization_barrier((attended, owed_low, owed_high, third_sent, fourth_sent))
    attended_late, low_late, high_late = late[:3]
    projection = times(attended_late, weight_out)
    block_output = (tokens_flat.astype(F32) + tissue_mask * projection).astype(BF)

    cut = model_width // 2
    grad_projected = jnp.concatenate(
        [grad_queries, low_late[:, :cut], high_late[:, :cut], low_late[:, cut:], high_late[:, cut:]],
        axis=-1,
    )
    scaled = times_t(grad_projected, weight_in) * norm_gain
    inverse = moments[:, 1:2]
    normalized = (tokens_flat.astype(F32) - moments[:, :1]) * inverse
    first_mean = jnp.mean(scaled, axis=-1, keepdims=True)
    second_mean = jnp.mean(scaled * normalized, axis=-1, keepdims=True)
    input_grad = inverse * (scaled - first_mean - normalized * second_mean)
    input_grad = (cot_flat.astype(F32) + input_grad).astype(BF)

    inv_root = 1.0 / math.sqrt(slides * rows_count * cols_count * token_count)
    width = model_width
    weight_grads = jnp.concatenate(
        [
            first_sums[:, :width],
            second_sums[:, :cut],
            second_sums[:, width : width + cut],
            second_sums[:, cut:width],
            second_sums[:, width + cut :],
            first_sums[:, width:],
        ],
        axis=1,
    )
    return (
        block_output.reshape((1,) + grid),
        input_grad.reshape((1,) + grid),
        weight_grads * inv_root,
    )


def solution(mesh):
    tile = P("slide", "gy", "gx", None)
    return jax.shard_map(
        local,
        mesh=mesh,
        in_specs=(tile, P(), P(), P("slide", "gy", "gx"), tile),
        out_specs=(tile, tile, P(("slide", "gy", "gx"), None)),
        check_vma=False,
    )
```

```python
import functools
import math

import jax
import jax.numpy as jnp
from jax import lax
from jax.experimental import pallas as pl
from jax.experimental.pallas import tpu as pltpu
from jax.sharding import PartitionSpec as P

HEADS = 16
RADIUS = 6
EPSILON = 1e-06
STRIP = 4
GROUP = 4
SIDE = 8
BF = jnp.bfloat16
F32 = jnp.float32


def swapped(array, axis, by):
    count = lax.axis_size(axis)
    return lax.ppermute(array, axis, [(i, i ^ by) for i in range(count)])


def moved(array, axis, by):
    count = lax.axis_size(axis)
    pairs = [(i, i + by) for i in range(count) if 0 <= i + by < count]
    return lax.ppermute(array, axis, pairs)


def rows_around(block, facing=None):
    rows_count = lax.axis_size("gy")
    if rows_count == 2:
        at_top = lax.axis_index("gy") == 0
        if facing is None:
            facing = jnp.where(at_top, block[-RADIUS:], block[:RADIUS])
        return (swapped(facing, "gy", 1),)
    return (moved(block[-RADIUS:], "gy", 1), moved(block[:RADIUS], "gy", -1))


def with_rows(block, rows):
    if len(rows) == 1:
        at_top = lax.axis_index("gy") == 0
        zero = jnp.zeros((), block.dtype)
        rows = (jnp.where(at_top, zero, rows[0]), jnp.where(at_top, rows[0], zero))
    return jnp.concatenate([rows[0], block, rows[1]], axis=0)


def facing_columns(to_right, to_left):
    even = lax.axis_index("gx") % 2 == 0
    return jnp.where(even, to_right, to_left), jnp.where(even, to_left, to_right)


def exchange_columns(out_one, out_two):
    count = lax.axis_size("gx")
    even = lax.axis_index("gx") % 2 == 0
    first, second = [], []
    for low in range(count - 1):
        pairs = second if low % 2 else first
        pairs += [(low, low + 1), (low + 1, low)]
    one = lax.ppermute(out_one, "gx", first)
    two = lax.ppermute(out_two, "gx", second)
    return jnp.where(even, two, one), jnp.where(even, one, two)


def column_halo(block):
    left, right = exchange_columns(*facing_columns(block[:, -SIDE:], block[:, :SIDE]))
    return jnp.concatenate([block, right, left], axis=1)


def owed_columns(grid):
    cols = grid.shape[2] - 2 * SIDE
    return facing_columns(grid[:, :, cols : cols + SIDE], grid[:, :, cols + SIDE :])


def return_columns(grid, out_one, out_two):
    cols = grid.shape[2] - 2 * SIDE
    from_left, from_right = exchange_columns(out_one, out_two)
    return grid[:, :, :cols].astype(F32) + jnp.concatenate([from_left, from_right], axis=2)


def owed_rows(grid):
    top, bottom = grid[:, :RADIUS].astype(BF), grid[:, -RADIUS:].astype(BF)
    if lax.axis_size("gy") == 2:
        return (jnp.where(lax.axis_index("gy") == 0, bottom, top),)
    return (top, bottom)


def return_rows(grid, outward):
    own = grid[:, RADIUS:-RADIUS]
    if len(outward) == 1:
        at_top = lax.axis_index("gy") == 0
        other = swapped(outward[0], "gy", 1)
        zero = jnp.zeros((), BF)
        above, below = jnp.where(at_top, zero, other), jnp.where(at_top, other, zero)
    else:
        above = moved(outward[1], "gy", 1)
        below = moved(outward[0], "gy", -1)
    rest = ((0, 0), (0, own.shape[1] - RADIUS), (0, 0), (0, 0))
    above = jnp.pad(above, rest)
    below = jnp.pad(below, (rest[0], rest[1][::-1], rest[2], rest[3]))
    return own + above.astype(F32) + below.astype(F32)


def in_hbm(array):
    return pltpu.with_memory_space_constraint(array, pltpu.HBM)


def prepare(
    place_ref, x_ref, c_ref, t_ref, gain_ref, normed_ref, branch_ref, face_ref, moment_ref
):
    block, width = x_ref.shape
    step = pl.program_id(0)
    rows = pl.ds(pl.multiple_of(step * block, block), block)
    x = x_ref[...].astype(F32)
    mean = jnp.sum(x, axis=1, keepdims=True) * (1.0 / width)
    centered = x - mean
    variance = jnp.sum(centered * centered, axis=1, keepdims=True) * (1.0 / width)
    inverse = lax.rsqrt(variance + EPSILON)
    normed_ref[rows, :] = (centered * inverse * gain_ref[...]).astype(BF)
    branch_ref[...] = (c_ref[...].astype(F32) * t_ref[...]).astype(BF)
    lane = lax.broadcasted_iota(jnp.int32, moment_ref.shape, 1)
    moment_ref[...] = jnp.where(lane == 0, mean, inverse)

    @pl.when(step == pl.num_programs(0) - 1)
    def _():
        first = pl.multiple_of(place_ref[4], 16)
        face_ref[...] = normed_ref[pl.ds(first, face_ref.shape[0]), :]


def run_prepare(place, tokens, cotangent, tissue, gain, face):
    count, width = tokens.shape
    block = min(count, 64)
    part = lambda columns: pl.BlockSpec((block, columns), lambda step: (step, 0))
    return pl.pallas_call(
        prepare,
        grid=(count // block,),
        in_specs=[SCALARS, part(width), part(width), part(1), whole((1, width))],
        out_specs=[whole((count, width)), part(width), whole((face, width)), part(128)],
        out_shape=[
            jax.ShapeDtypeStruct((count, width), BF),
            jax.ShapeDtypeStruct((count, width), BF),
            jax.ShapeDtypeStruct((face, width), BF),
            jax.ShapeDtypeStruct((count, 128), F32),
        ],
        compiler_params=pltpu.CompilerParams(**PARAMS),
        cost_estimate=pl.CostEstimate(flops=0, bytes_accessed=3 * 1024 * 1024, transcendentals=0),
        name="prepare",
    )(place, in_hbm(tokens), in_hbm(cotangent), tissue, in_hbm(gain))


def spread_heads(block, head_dim):
    lane_head = lax.broadcasted_iota(jnp.int32, block.shape, 1) // head_dim
    zero = jnp.zeros_like(block)
    return jnp.concatenate(
        [jnp.where(lane_head == head, block, zero) for head in range(GROUP)], axis=0
    )


def gather_heads(full, count, head_dim):
    lane_head = lax.broadcasted_iota(jnp.int32, (count, full.shape[1]), 1) // head_dim
    result = full[:count]
    for head in range(1, GROUP):
        result = jnp.where(lane_head == head, full[head * count : (head + 1) * count], result)
    return result


def times(left, right):
    return jnp.dot(left, right, preferred_element_type=F32)


def times_t(left, right):
    return lax.dot_general(left, right, (((1,), (1,)), ((), ())), preferred_element_type=F32)


def fill_bias(place_ref, bias_ref, tile_rows, tile_cols):
    strips, count, window = bias_ref.shape
    slots = tile_cols + 2 * SIDE
    own = lax.broadcasted_iota(jnp.int32, (count, window), 0)
    near = lax.broadcasted_iota(jnp.int32, (count, window), 1)
    own_row, own_col = own // tile_cols, own % tile_cols
    near_row, slot = near // slots, near % slots
    near_col = jnp.where(slot < tile_cols + SIDE, slot, slot - slots)
    row_gap = near_row - RADIUS - own_row
    col_gap = near_col - own_col
    col = place_ref[1] + near_col
    allowed = (jnp.abs(row_gap) <= RADIUS) & (jnp.abs(col_gap) <= RADIUS)
    allowed = allowed & (col >= 0) & (col < place_ref[3])
    for strip in range(strips):
        row = place_ref[0] + strip * STRIP + near_row - RADIUS
        kept = allowed & (row >= 0) & (row < place_ref[2])
        bias_ref[strip] = jnp.where(kept, 0.0, -1e30).astype(F32)


def query_pass(
    head_dim,
    tile,
    place_ref,
    q_ref,
    g_ref,
    normed_ref,
    key_w_ref,
    value_w_ref,
    out_ref,
    owed_ref,
    bias_ref,
    k_ref,
    v_ref,
    dk_ref,
    dv_ref,
):
    scaling = 1.0 / math.sqrt(head_dim)
    strips, count, window = bias_ref.shape
    step = (tile[1] + 2 * SIDE) * STRIP
    group = pl.program_id(0)

    @pl.when(group == 0)
    def _():
        fill_bias(place_ref, bias_ref, *tile)

    k_ref[...] = times(normed_ref[...], key_w_ref[...]).astype(BF)
    v_ref[...] = times(normed_ref[...], value_w_ref[...]).astype(BF)
    dk_ref[...] = jnp.zeros_like(dk_ref)
    dv_ref[...] = jnp.zeros_like(dv_ref)

    def dots(strip):
        own = pl.ds(strip * count, count)
        near = pl.ds(strip * step, window)
        queries = spread_heads(q_ref[own, :] * jnp.asarray(scaling, BF), head_dim)
        grads = spread_heads(g_ref[own, :], head_dim)
        scores = times_t(queries, k_ref[near, :])
        return queries, grads, scores, times_t(grads, v_ref[near, :])

    ahead = dots(0)
    for strip in range(strips):
        own = pl.ds(strip * count, count)
        near = pl.ds(strip * step, window)
        queries, grads, scores, grad_probs = ahead
        if strip + 1 < strips:
            ahead = dots(strip + 1)
        probs_parts, grad_parts = [], []
        for head in range(GROUP):
            part = slice(head * count, (head + 1) * count)
            masked = scores[part] + bias_ref[strip]
            row_max = jnp.max(masked, axis=1, keepdims=True)
            exponent = jnp.exp(masked - row_max)
            grad_part = grad_probs[part]
            total = jnp.sum(exponent, axis=1, keepdims=True)
            share = 1.0 / total
            delta = jnp.sum(exponent * grad_part, axis=1, keepdims=True) * share
            probs = exponent * share
            probs_parts.append(probs.astype(BF))
            grad_parts.append((probs * (grad_part - delta)).astype(BF))
        probs = jnp.concatenate(probs_parts, axis=0)
        grad_scores = jnp.concatenate(grad_parts, axis=0)
        attended = times(probs, v_ref[near, :])
        grad_queries = times(grad_scores, k_ref[near, :])
        out_ref[0, own, :] = gather_heads(attended, count, head_dim).astype(BF)
        out_ref[1, own, :] = (gather_heads(grad_queries, count, head_dim) * scaling).astype(BF)
        dk_ref[near, :] += product_t(grad_scores, queries)
        dv_ref[near, :] += product_t(probs, grads)
    owed_ref[0] = dk_ref[...].astype(BF)
    owed_ref[1] = dv_ref[...].astype(BF)


def whole(shape):
    return pl.BlockSpec(shape, lambda group: (0,) * len(shape))


def columns(rows, width, first=0):
    return pl.BlockSpec((rows, width), lambda group: (0, first + group))


def pair_columns(rows, width):
    return pl.BlockSpec((2, rows, width), lambda group: (0, 0, group))


SCALARS = pl.BlockSpec(memory_space=pltpu.SMEM)
PARAMS = dict(vmem_limit_bytes=24 * 1024 * 1024)


def window_shape(tile):
    return (tile[0] // STRIP, STRIP * tile[1], (STRIP + 2 * RADIUS) * (tile[1] + 2 * SIDE))


def attention_cost(tile, groups, part):
    strips, count, window = window_shape(tile)
    flops = 4 * 2 * groups * strips * GROUP * count * window * part
    return pl.CostEstimate(flops=flops, bytes_accessed=4 * 1024 * 1024, transcendentals=0)


def run_queries(place, queries, grads, normed_ext, weights, head_dim, tile):
    tokens, width = queries.shape
    ext = normed_ext.shape[0]
    part = GROUP * head_dim
    groups = width // part
    return pl.pallas_call(
        functools.partial(query_pass, head_dim, tile),
        grid=(groups,),
        in_specs=[
            SCALARS,
            columns(tokens, part),
            columns(tokens, part),
            whole(normed_ext.shape),
            columns(width, part, groups),
            columns(width, part, 2 * groups),
        ],
        out_specs=[pair_columns(tokens, part), pair_columns(ext, part)],
        out_shape=[
            jax.ShapeDtypeStruct((2, tokens, width), BF),
            jax.ShapeDtypeStruct((2, ext, width), BF),
        ],
        scratch_shapes=[pltpu.VMEM(window_shape(tile), F32)]
        + [pltpu.VMEM((ext, part), BF)] * 2
        + [pltpu.VMEM((ext, part), F32)] * 2,
        compiler_params=pltpu.CompilerParams(**PARAMS),
        cost_estimate=attention_cost(tile, groups, part),
        name="query_pass",
    )(place, queries, grads, normed_ext, in_hbm(weights), in_hbm(weights))


def own_part(array, index, axis):
    return lax.dynamic_index_in_dim(array, index, axis, keepdims=False)


def product_t(left, right):
    return lax.dot_general(left, right, (((0,), (0,)), ((), ())), preferred_element_type=F32)


def slide_swap(array, high):
    return swapped(array, "slide", lax.axis_size("slide") // 2 if high else 1)


def partners(across_slides):
    if across_slides:
        index = lax.axis_index("slide") // 2
        return index, [(1, 1 - index)]
    index = lax.axis_index("gy")
    return index, [(by, index ^ by) for by in range(1, lax.axis_size("gy"))]


def sent(block, across_slides, by):
    return slide_swap(block, True) if across_slides else swapped(block, "gy", by)


def pick_rows(array, index, across_slides, width):
    rows = width // lax.axis_size("slide")
    core = lax.axis_index("slide") % 2
    if across_slides:
        return lax.dynamic_slice_in_dim(array, (2 * index + core) * rows, rows, axis=1)
    rest = rows // lax.axis_size("gy")
    parts = [
        lax.dynamic_slice_in_dim(array, (2 * high + core) * rows + index * rest, rest, axis=1)
        for high in range(lax.axis_size("slide") // 2)
    ]
    return jnp.concatenate(parts, axis=1)


def pair_product(lefts, rights, index, across_slides):
    total = None
    for left, right in zip(lefts, rights):
        term = product_t(pick_rows(left, index, across_slides, right.shape[1]), right)
        total = term if total is None else total + term
    return total


def partner_half(left, right):
    rows = left.shape[1] // lax.axis_size("slide")
    other = 1 - lax.axis_index("slide") % 2
    parts = [
        lax.dynamic_slice_in_dim(left, (2 * high + other) * rows, rows, axis=1)
        for high in range(lax.axis_size("slide") // 2)
    ]
    return product_t(jnp.concatenate(parts, axis=1), right).astype(BF)


def halved_product(left, right, arrived, index, across_slides):
    rows = arrived.shape[0] // 2
    if across_slides:
        match = lax.dynamic_slice_in_dim(arrived, index * rows, rows, axis=0)
    else:
        rest = rows // lax.axis_size("gy")
        match = jnp.concatenate(
            [
                lax.dynamic_slice_in_dim(arrived, high * rows + index * rest, rest, axis=0)
                for high in range(2)
            ],
            axis=0,
        )
    return product_t(pick_rows(left, index, across_slides, left.shape[1]), right) + match.astype(F32)


def blocks_of(product, across_slides):
    index, others = partners(across_slides)
    return [product(target).astype(BF) for _, target in others], lambda: product(index)


def first_halving(blocks, mine, across_slides):
    others = partners(across_slides)[1]
    arrived = [sent(block, across_slides, by) for block, (by, _) in zip(blocks, others)]
    total = mine()
    for block in arrived:
        total = total + block.astype(F32)
    return total


def second_halving(part, across_slides):
    index, others = partners(across_slides)
    rows = part.shape[0] // (len(others) + 1)
    mine = lax.dynamic_slice_in_dim(part, index * rows, rows, axis=0)
    for by, target in others:
        block = lax.dynamic_slice_in_dim(part, target * rows, rows, axis=0).astype(BF)
        mine = mine + sent(block, across_slides, by).astype(F32)
    return mine


def reduce_columns(part):
    count = lax.axis_size("gx")
    index = lax.axis_index("gx")
    rows = part.shape[0] // count
    mine = lax.dynamic_slice_in_dim(part, index * rows, rows, axis=0)
    arrived = []
    for by in range(count - 1, 0, -1):
        block = lax.dynamic_slice_in_dim(part, (index ^ by) * rows, rows, axis=0)
        arrived.append(swapped(block.astype(BF), "gx", by))
    for block in arrived:
        mine = mine + block.astype(F32)
    return mine


def second_halvings(one, two):
    return jnp.concatenate([second_halving(one, False), second_halving(two, True)], axis=1)


def after(array, *earlier):
    return lax.optimization_barrier((array, *earlier))[0]


def local(tokens, weights, norm_gain, tissue, cotangent):
    tile_tokens = tokens[0]
    tile_rows, tile_cols, model_width = tile_tokens.shape
    tile = (tile_rows, tile_cols)
    head_dim = model_width // HEADS
    token_count = tile_rows * tile_cols
    slides = lax.axis_size("slide")
    rows_count = lax.axis_size("gy")
    cols_count = lax.axis_size("gx")
    weight_in = weights[:, : 3 * model_width]
    weight_out = weights[:, 3 * model_width :]
    face = RADIUS * tile_cols
    at_top = lax.axis_index("gy") == 0
    place = jnp.stack(
        [
            lax.axis_index("gy") * tile_rows,
            lax.axis_index("gx") * tile_cols,
            jnp.int32(tile_rows * rows_count),
            jnp.int32(tile_cols * cols_count),
            jnp.where(at_top, token_count - face, 0),
        ]
    ).astype(jnp.int32)

    flat = (token_count, model_width)
    grid = (tile_rows, tile_cols, model_width)
    tissue_mask = tissue[0].astype(F32).reshape(token_count, 1)
    tokens_flat = tile_tokens.reshape(flat)
    cot_flat = cotangent[0].reshape(flat)
    normed, branch_flat, facing, moments = run_prepare(
        place, tokens_flat, cot_flat, tissue_mask, norm_gain.reshape(1, model_width), face
    )
    normed_tile = normed.reshape(grid)
    rows = rows_around(normed_tile, facing.reshape(RADIUS, tile_cols, model_width))
    middle = column_halo(normed_tile)
    normed_ext = with_rows(middle, [column_halo(row) for row in rows])
    ext_rows, ext_cols = normed_ext.shape[:2]
    normed_ext = normed_ext.reshape(ext_rows * ext_cols, model_width)

    grad_attn = times_t(branch_flat, weight_out).astype(BF)
    queries = times(normed, weight_in[:, :model_width]).astype(BF)
    normed_pair = (normed, slide_swap(normed, False))
    branch_pair = (branch_flat, slide_swap(branch_flat, False))

    found, owed = run_queries(place, queries, grad_attn, normed_ext, weights, head_dim, tile)
    attended, grad_queries = found[0], found[1]

    found_other = slide_swap(found, False)
    key_half = partner_half(normed_ext, owed[0])
    value_half = partner_half(normed_ext, owed[1])
    key_arrived, value_arrived = slide_swap(key_half, False), slide_swap(value_half, False)
    found_other = after(found_other, key_half, value_half)
    query_sent, query_kept = blocks_of(
        lambda index: pair_product(normed_pair, (grad_queries, found_other[1]), index, True), True
    )
    out_sent, out_kept = blocks_of(
        lambda index: pair_product((attended, found_other[0]), branch_pair, index, False), False
    )

    owed_grid = after(owed, *query_sent, *out_sent)
    owed_grid = owed_grid.reshape(2, ext_rows, ext_cols, model_width)
    outward = owed_columns(owed_grid)
    key_sent, key_kept = blocks_of(
        lambda index: halved_product(normed_ext, owed[0], key_arrived, index, True), True
    )
    value_sent, value_kept = blocks_of(
        lambda index: halved_product(normed_ext, owed[1], value_arrived, index, False), False
    )

    first_kept = lax.optimization_barrier((query_kept(), out_kept(), key_sent, value_sent))[:2]
    one = first_halving(query_sent, lambda: first_kept[0], True)
    two = first_halving(out_sent, lambda: first_kept[1], False)
    second_kept = lax.optimization_barrier((key_kept(), value_kept(), one, two))[:2]
    three = first_halving(key_sent, lambda: second_kept[0], True)
    four = first_halving(value_sent, lambda: second_kept[1], False)
    owed_cols = return_columns(owed_grid, *outward)
    owed_up = owed_rows(owed_cols)
    second_sums = reduce_columns(after(second_halvings(three, four), *owed_up))
    first_sums = reduce_columns(second_halvings(one, two))
    owed_sum = return_rows(owed_cols, owed_up).astype(BF).reshape((2,) + flat)

    attended_late = after(attended, *key_sent, *value_sent)
    projection = times(attended_late, weight_out)
    block_output = (tokens_flat.astype(F32) + tissue_mask * projection).astype(BF)

    grad_projected = jnp.concatenate([grad_queries, owed_sum[0], owed_sum[1]], axis=-1)
    scaled = times_t(grad_projected, weight_in) * norm_gain
    inverse = moments[:, 1:2]
    normalized = (tokens_flat.astype(F32) - moments[:, :1]) * inverse
    first_mean = jnp.mean(scaled, axis=-1, keepdims=True)
    second_mean = jnp.mean(scaled * normalized, axis=-1, keepdims=True)
    input_grad = inverse * (scaled - first_mean - normalized * second_mean)
    input_grad = (cot_flat.astype(F32) + input_grad).astype(BF)

    inv_root = 1.0 / math.sqrt(slides * rows_count * cols_count * token_count)
    width = model_width
    weight_grads = jnp.concatenate(
        [first_sums[:, :width], second_sums, first_sums[:, width:]], axis=1
    )
    return (
        block_output.reshape((1,) + grid),
        input_grad.reshape((1,) + grid),
        weight_grads * inv_root,
    )


def solution(mesh):
    tile = P("slide", "gy", "gx", None)
    return jax.shard_map(
        local,
        mesh=mesh,
        in_specs=(tile, P(), P(), P("slide", "gy", "gx"), tile),
        out_specs=(tile, tile, P(("slide", "gy", "gx"), None)),
        check_vma=False,
    )
```

```python
import functools
import math

import jax
import jax.numpy as jnp
from jax import lax
from jax.experimental import pallas as pl
from jax.experimental.pallas import tpu as pltpu
from jax.sharding import PartitionSpec as P

HEADS = 16
RADIUS = 6
EPSILON = 1e-06
STRIP = 4
GROUP = 4
SIDE = 8
BF = jnp.bfloat16
F32 = jnp.float32


def swapped(array, axis, by):
    count = lax.axis_size(axis)
    return lax.ppermute(array, axis, [(i, i ^ by) for i in range(count)])


def moved(array, axis, by):
    count = lax.axis_size(axis)
    pairs = [(i, i + by) for i in range(count) if 0 <= i + by < count]
    return lax.ppermute(array, axis, pairs)


def rows_around(block, facing=None):
    rows_count = lax.axis_size("gy")
    if rows_count == 2:
        at_top = lax.axis_index("gy") == 0
        if facing is None:
            facing = jnp.where(at_top, block[-RADIUS:], block[:RADIUS])
        return (swapped(facing, "gy", 1),)
    return (moved(block[-RADIUS:], "gy", 1), moved(block[:RADIUS], "gy", -1))


def with_rows(block, rows):
    if len(rows) == 1:
        at_top = lax.axis_index("gy") == 0
        zero = jnp.zeros((), block.dtype)
        rows = (jnp.where(at_top, zero, rows[0]), jnp.where(at_top, rows[0], zero))
    return jnp.concatenate([rows[0], block, rows[1]], axis=0)


def facing_columns(to_right, to_left):
    even = lax.axis_index("gx") % 2 == 0
    return jnp.where(even, to_left, to_right), jnp.where(even, to_right, to_left)


def exchange_columns(out_one, out_two):
    count = lax.axis_size("gx")
    even = lax.axis_index("gx") % 2 == 0
    first, second = [], []
    for low in range(count - 1):
        pairs = first if low % 2 else second
        pairs += [(low, low + 1), (low + 1, low)]
    one = lax.ppermute(out_one, "gx", first)
    two = lax.ppermute(out_two, "gx", second)
    return jnp.where(even, one, two), jnp.where(even, two, one)


def column_halo(block):
    left, right = exchange_columns(*facing_columns(block[:, -SIDE:], block[:, :SIDE]))
    return jnp.concatenate([block, right, left], axis=1)


def owed_columns(grid):
    cols = grid.shape[2] - 2 * SIDE
    return facing_columns(grid[:, :, cols : cols + SIDE], grid[:, :, cols + SIDE :])


def return_columns(grid, out_one, out_two):
    cols = grid.shape[2] - 2 * SIDE
    from_left, from_right = exchange_columns(out_one, out_two)
    return grid[:, :, :cols].astype(F32) + jnp.concatenate([from_left, from_right], axis=2)


def owed_rows(grid):
    top, bottom = grid[:, :RADIUS].astype(BF), grid[:, -RADIUS:].astype(BF)
    if lax.axis_size("gy") == 2:
        return (jnp.where(lax.axis_index("gy") == 0, bottom, top),)
    return (top, bottom)


def return_rows(grid, outward):
    own = grid[:, RADIUS:-RADIUS]
    if len(outward) == 1:
        at_top = lax.axis_index("gy") == 0
        other = swapped(outward[0], "gy", 1)
        zero = jnp.zeros((), BF)
        above, below = jnp.where(at_top, zero, other), jnp.where(at_top, other, zero)
    else:
        above = moved(outward[1], "gy", 1)
        below = moved(outward[0], "gy", -1)
    rest = ((0, 0), (0, own.shape[1] - RADIUS), (0, 0), (0, 0))
    above = jnp.pad(above, rest)
    below = jnp.pad(below, (rest[0], rest[1][::-1], rest[2], rest[3]))
    return own + above.astype(F32) + below.astype(F32)


def in_hbm(array):
    return pltpu.with_memory_space_constraint(array, pltpu.HBM)


def prepare(
    place_ref, x_ref, c_ref, t_ref, gain_ref, normed_ref, branch_ref, face_ref, moment_ref
):
    block, width = x_ref.shape
    step = pl.program_id(0)
    rows = pl.ds(pl.multiple_of(step * block, block), block)
    x = x_ref[...].astype(F32)
    mean = jnp.sum(x, axis=1, keepdims=True) * (1.0 / width)
    centered = x - mean
    variance = jnp.sum(centered * centered, axis=1, keepdims=True) * (1.0 / width)
    inverse = lax.rsqrt(variance + EPSILON)
    normed_ref[rows, :] = (centered * inverse * gain_ref[...]).astype(BF)
    branch_ref[...] = (c_ref[...].astype(F32) * t_ref[...]).astype(BF)
    lane = lax.broadcasted_iota(jnp.int32, moment_ref.shape, 1)
    moment_ref[...] = jnp.where(lane == 0, mean, inverse)

    @pl.when(step == pl.num_programs(0) - 1)
    def _():
        first = pl.multiple_of(place_ref[4], 16)
        face_ref[...] = normed_ref[pl.ds(first, face_ref.shape[0]), :]


def run_prepare(place, tokens, cotangent, tissue, gain, face):
    count, width = tokens.shape
    block = min(count, 64)
    part = lambda columns: pl.BlockSpec((block, columns), lambda step: (step, 0))
    return pl.pallas_call(
        prepare,
        grid=(count // block,),
        in_specs=[SCALARS, part(width), part(width), part(1), whole((1, width))],
        out_specs=[whole((count, width)), part(width), whole((face, width)), part(128)],
        out_shape=[
            jax.ShapeDtypeStruct((count, width), BF),
            jax.ShapeDtypeStruct((count, width), BF),
            jax.ShapeDtypeStruct((face, width), BF),
            jax.ShapeDtypeStruct((count, 128), F32),
        ],
        compiler_params=pltpu.CompilerParams(**PARAMS),
        cost_estimate=pl.CostEstimate(flops=0, bytes_accessed=3 * 1024 * 1024, transcendentals=0),
        name="prepare",
    )(place, in_hbm(tokens), in_hbm(cotangent), tissue, in_hbm(gain))


def spread_heads(block, head_dim):
    lane_head = lax.broadcasted_iota(jnp.int32, block.shape, 1) // head_dim
    zero = jnp.zeros_like(block)
    return jnp.concatenate(
        [jnp.where(lane_head == head, block, zero) for head in range(GROUP)], axis=0
    )


def gather_heads(full, count, head_dim):
    lane_head = lax.broadcasted_iota(jnp.int32, (count, full.shape[1]), 1) // head_dim
    result = full[:count]
    for head in range(1, GROUP):
        result = jnp.where(lane_head == head, full[head * count : (head + 1) * count], result)
    return result


def times(left, right):
    return jnp.dot(left, right, preferred_element_type=F32)


def times_t(left, right):
    return lax.dot_general(left, right, (((1,), (1,)), ((), ())), preferred_element_type=F32)


def fill_bias(place_ref, bias_ref, tile_rows, tile_cols):
    strips, count, window = bias_ref.shape
    slots = tile_cols + 2 * SIDE
    own = lax.broadcasted_iota(jnp.int32, (count, window), 0)
    near = lax.broadcasted_iota(jnp.int32, (count, window), 1)
    own_row, own_col = own // tile_cols, own % tile_cols
    near_row, slot = near // slots, near % slots
    near_col = jnp.where(slot < tile_cols + SIDE, slot, slot - slots)
    row_gap = near_row - RADIUS - own_row
    col_gap = near_col - own_col
    col = place_ref[1] + near_col
    allowed = (jnp.abs(row_gap) <= RADIUS) & (jnp.abs(col_gap) <= RADIUS)
    allowed = allowed & (col >= 0) & (col < place_ref[3])
    for strip in range(strips):
        row = place_ref[0] + strip * STRIP + near_row - RADIUS
        kept = allowed & (row >= 0) & (row < place_ref[2])
        bias_ref[strip] = jnp.where(kept, 0.0, -1e30).astype(F32)


def query_pass(
    head_dim,
    tile,
    place_ref,
    q_ref,
    g_ref,
    normed_ref,
    key_w_ref,
    value_w_ref,
    out_ref,
    owed_ref,
    bias_ref,
    k_ref,
    v_ref,
    dk_ref,
    dv_ref,
):
    scaling = 1.0 / math.sqrt(head_dim)
    strips, count, window = bias_ref.shape
    step = (tile[1] + 2 * SIDE) * STRIP
    group = pl.program_id(0)

    @pl.when(group == 0)
    def _():
        fill_bias(place_ref, bias_ref, *tile)

    k_ref[...] = times(normed_ref[...], key_w_ref[...]).astype(BF)
    v_ref[...] = times(normed_ref[...], value_w_ref[...]).astype(BF)
    dk_ref[...] = jnp.zeros_like(dk_ref)
    dv_ref[...] = jnp.zeros_like(dv_ref)

    def dots(strip):
        own = pl.ds(strip * count, count)
        near = pl.ds(strip * step, window)
        queries = spread_heads(q_ref[own, :] * jnp.asarray(scaling, BF), head_dim)
        grads = spread_heads(g_ref[own, :], head_dim)
        scores = times_t(queries, k_ref[near, :])
        return queries, grads, scores, times_t(grads, v_ref[near, :])

    ahead = dots(0)
    for strip in range(strips):
        own = pl.ds(strip * count, count)
        near = pl.ds(strip * step, window)
        queries, grads, scores, grad_probs = ahead
        if strip + 1 < strips:
            ahead = dots(strip + 1)
        probs_parts, grad_parts = [], []
        for head in range(GROUP):
            part = slice(head * count, (head + 1) * count)
            masked = scores[part] + bias_ref[strip]
            row_max = jnp.max(masked, axis=1, keepdims=True)
            exponent = jnp.exp(masked - row_max)
            grad_part = grad_probs[part]
            total = jnp.sum(exponent, axis=1, keepdims=True)
            share = 1.0 / total
            delta = jnp.sum(exponent * grad_part, axis=1, keepdims=True) * share
            probs = exponent * share
            probs_parts.append(probs.astype(BF))
            grad_parts.append((probs * (grad_part - delta)).astype(BF))
        probs = jnp.concatenate(probs_parts, axis=0)
        grad_scores = jnp.concatenate(grad_parts, axis=0)
        attended = times(probs, v_ref[near, :])
        grad_queries = times(grad_scores, k_ref[near, :])
        out_ref[0, own, :] = gather_heads(attended, count, head_dim).astype(BF)
        out_ref[1, own, :] = (gather_heads(grad_queries, count, head_dim) * scaling).astype(BF)
        dk_ref[near, :] += product_t(grad_scores, queries)
        dv_ref[near, :] += product_t(probs, grads)
    owed_ref[0] = dk_ref[...].astype(BF)
    owed_ref[1] = dv_ref[...].astype(BF)


def whole(shape):
    return pl.BlockSpec(shape, lambda group: (0,) * len(shape))


def columns(rows, width, first=0):
    return pl.BlockSpec((rows, width), lambda group: (0, first + group))


def pair_columns(rows, width):
    return pl.BlockSpec((2, rows, width), lambda group: (0, 0, group))


SCALARS = pl.BlockSpec(memory_space=pltpu.SMEM)
PARAMS = dict(vmem_limit_bytes=24 * 1024 * 1024)


def window_shape(tile):
    return (tile[0] // STRIP, STRIP * tile[1], (STRIP + 2 * RADIUS) * (tile[1] + 2 * SIDE))


def attention_cost(tile, groups, part):
    strips, count, window = window_shape(tile)
    flops = 4 * 2 * groups * strips * GROUP * count * window * part
    return pl.CostEstimate(flops=flops, bytes_accessed=4 * 1024 * 1024, transcendentals=0)


def run_queries(place, queries, grads, normed_ext, weights, head_dim, tile):
    tokens, width = queries.shape
    ext = normed_ext.shape[0]
    part = GROUP * head_dim
    groups = width // part
    return pl.pallas_call(
        functools.partial(query_pass, head_dim, tile),
        grid=(groups,),
        in_specs=[
            SCALARS,
            columns(tokens, part),
            columns(tokens, part),
            whole(normed_ext.shape),
            columns(width, part, groups),
            columns(width, part, 2 * groups),
        ],
        out_specs=[pair_columns(tokens, part), pair_columns(ext, part)],
        out_shape=[
            jax.ShapeDtypeStruct((2, tokens, width), BF),
            jax.ShapeDtypeStruct((2, ext, width), BF),
        ],
        scratch_shapes=[pltpu.VMEM(window_shape(tile), F32)]
        + [pltpu.VMEM((ext, part), BF)] * 2
        + [pltpu.VMEM((ext, part), F32)] * 2,
        compiler_params=pltpu.CompilerParams(**PARAMS),
        cost_estimate=attention_cost(tile, groups, part),
        name="query_pass",
    )(place, queries, grads, normed_ext, in_hbm(weights), in_hbm(weights))


def own_part(array, index, axis):
    return lax.dynamic_index_in_dim(array, index, axis, keepdims=False)


def product_t(left, right):
    return lax.dot_general(left, right, (((0,), (0,)), ((), ())), preferred_element_type=F32)


def slide_swap(array, high):
    return swapped(array, "slide", lax.axis_size("slide") // 2 if high else 1)


def partners(across_slides):
    if across_slides:
        index = lax.axis_index("slide") // 2
        return index, [(1, 1 - index)]
    index = lax.axis_index("gy")
    return index, [(by, index ^ by) for by in range(1, lax.axis_size("gy"))]


def sent(block, across_slides, by):
    return slide_swap(block, True) if across_slides else swapped(block, "gy", by)


def pick_rows(array, index, across_slides, width):
    rows = width // lax.axis_size("slide")
    core = lax.axis_index("slide") % 2
    if across_slides:
        return lax.dynamic_slice_in_dim(array, (2 * index + core) * rows, rows, axis=1)
    rest = rows // lax.axis_size("gy")
    parts = [
        lax.dynamic_slice_in_dim(array, (2 * high + core) * rows + index * rest, rest, axis=1)
        for high in range(lax.axis_size("slide") // 2)
    ]
    return jnp.concatenate(parts, axis=1)


def pair_product(lefts, rights, index, across_slides):
    total = None
    for left, right in zip(lefts, rights):
        term = product_t(pick_rows(left, index, across_slides, right.shape[1]), right)
        total = term if total is None else total + term
    return total


def partner_half(left, right):
    rows = left.shape[1] // lax.axis_size("slide")
    other = 1 - lax.axis_index("slide") % 2
    parts = [
        lax.dynamic_slice_in_dim(left, (2 * high + other) * rows, rows, axis=1)
        for high in range(lax.axis_size("slide") // 2)
    ]
    return product_t(jnp.concatenate(parts, axis=1), right).astype(BF)


def halved_product(left, right, arrived, index, across_slides):
    rows = arrived.shape[0] // 2
    if across_slides:
        match = lax.dynamic_slice_in_dim(arrived, index * rows, rows, axis=0)
    else:
        rest = rows // lax.axis_size("gy")
        match = jnp.concatenate(
            [
                lax.dynamic_slice_in_dim(arrived, high * rows + index * rest, rest, axis=0)
                for high in range(2)
            ],
            axis=0,
        )
    return product_t(pick_rows(left, index, across_slides, left.shape[1]), right) + match.astype(F32)


def blocks_of(product, across_slides):
    index, others = partners(across_slides)
    return [product(target).astype(BF) for _, target in others], lambda: product(index)


def first_halving(blocks, mine, across_slides):
    others = partners(across_slides)[1]
    arrived = [sent(block, across_slides, by) for block, (by, _) in zip(blocks, others)]
    total = mine()
    for block in arrived:
        total = total + block.astype(F32)
    return total


def second_halving(part, across_slides):
    index, others = partners(across_slides)
    rows = part.shape[0] // (len(others) + 1)
    mine = lax.dynamic_slice_in_dim(part, index * rows, rows, axis=0)
    for by, target in others:
        block = lax.dynamic_slice_in_dim(part, target * rows, rows, axis=0).astype(BF)
        mine = mine + sent(block, across_slides, by).astype(F32)
    return mine


def column_blocks(part):
    count = lax.axis_size("gx")
    index = lax.axis_index("gx")
    rows = part.shape[0] // count
    mine = lax.dynamic_slice_in_dim(part, index * rows, rows, axis=0)
    others = [
        lax.dynamic_slice_in_dim(part, (index ^ by) * rows, rows, axis=0).astype(BF)
        for by in range(count - 1, 0, -1)
    ]
    return mine, others


def reduce_columns(mine, others):
    count = lax.axis_size("gx")
    arrived = [
        swapped(block, "gx", by) for block, by in zip(others, range(count - 1, 0, -1))
    ]
    for block in arrived:
        mine = mine + block.astype(F32)
    return mine


def halve_columns(part):
    count, width = lax.axis_size("gx"), part.shape[1]
    index = lax.axis_index("gx")
    rows = part.shape[0] // count
    by = 1
    while by < count:
        bit = lax.rem(index // by, 2)
        blocks = part.reshape(-1, 2, rows, width)
        going = lax.dynamic_index_in_dim(blocks, 1 - bit, 1, keepdims=False).astype(BF)
        kept = lax.dynamic_index_in_dim(blocks, bit, 1, keepdims=False)
        part = (kept + swapped(going, "gx", by).astype(F32)).reshape(-1, width)
        by *= 2
    return part


def second_halvings(one, two):
    return jnp.concatenate([second_halving(one, False), second_halving(two, True)], axis=1)


def after(array, *earlier):
    return lax.optimization_barrier((array, *earlier))[0]


def local(tokens, weights, norm_gain, tissue, cotangent):
    tile_tokens = tokens[0]
    tile_rows, tile_cols, model_width = tile_tokens.shape
    tile = (tile_rows, tile_cols)
    head_dim = model_width // HEADS
    token_count = tile_rows * tile_cols
    slides = lax.axis_size("slide")
    rows_count = lax.axis_size("gy")
    cols_count = lax.axis_size("gx")
    weight_in = weights[:, : 3 * model_width]
    weight_out = weights[:, 3 * model_width :]
    face = RADIUS * tile_cols
    at_top = lax.axis_index("gy") == 0
    place = jnp.stack(
        [
            lax.axis_index("gy") * tile_rows,
            lax.axis_index("gx") * tile_cols,
            jnp.int32(tile_rows * rows_count),
            jnp.int32(tile_cols * cols_count),
            jnp.where(at_top, token_count - face, 0),
        ]
    ).astype(jnp.int32)

    flat = (token_count, model_width)
    grid = (tile_rows, tile_cols, model_width)
    tissue_mask = tissue[0].astype(F32).reshape(token_count, 1)
    tokens_flat = tile_tokens.reshape(flat)
    cot_flat = cotangent[0].reshape(flat)
    normed, branch_flat, facing, moments = run_prepare(
        place, tokens_flat, cot_flat, tissue_mask, norm_gain.reshape(1, model_width), face
    )
    normed_tile = normed.reshape(grid)
    rows = rows_around(normed_tile, facing.reshape(RADIUS, tile_cols, model_width))
    middle = column_halo(normed_tile)
    normed_ext = with_rows(middle, [column_halo(row) for row in rows])
    ext_rows, ext_cols = normed_ext.shape[:2]
    normed_ext = normed_ext.reshape(ext_rows * ext_cols, model_width)

    grad_attn = times_t(branch_flat, weight_out).astype(BF)
    queries = times(normed, weight_in[:, :model_width]).astype(BF)
    normed_pair = (normed, slide_swap(normed, False))
    branch_pair = (branch_flat, slide_swap(branch_flat, False))

    found, owed = run_queries(place, queries, grad_attn, normed_ext, weights, head_dim, tile)
    attended, grad_queries = found[0], found[1]

    found_other = slide_swap(found, False)
    key_half = partner_half(normed_ext, owed[0])
    value_half = partner_half(normed_ext, owed[1])
    key_arrived, value_arrived = slide_swap(key_half, False), slide_swap(value_half, False)
    found_other = after(found_other, key_half, value_half)
    query_sent, query_kept = blocks_of(
        lambda index: pair_product(normed_pair, (grad_queries, found_other[1]), index, True), True
    )
    out_sent, out_kept = blocks_of(
        lambda index: pair_product((attended, found_other[0]), branch_pair, index, False), False
    )

    owed_grid = after(owed, *query_sent, *out_sent)
    owed_grid = owed_grid.reshape(2, ext_rows, ext_cols, model_width)
    outward = owed_columns(owed_grid)
    key_sent, key_kept = blocks_of(
        lambda index: halved_product(normed_ext, owed[0], key_arrived, index, True), True
    )
    value_sent, value_kept = blocks_of(
        lambda index: halved_product(normed_ext, owed[1], value_arrived, index, False), False
    )

    first_kept = lax.optimization_barrier((query_kept(), out_kept(), key_sent, value_sent))[:2]
    one = first_halving(query_sent, lambda: first_kept[0], True)
    two = first_halving(out_sent, lambda: first_kept[1], False)
    second_kept = lax.optimization_barrier((key_kept(), value_kept(), one, two))[:2]
    three = first_halving(key_sent, lambda: second_kept[0], True)
    four = first_halving(value_sent, lambda: second_kept[1], False)
    owed_cols = return_columns(owed_grid, *outward)
    owed_up = owed_rows(owed_cols)
    mine, others = column_blocks(after(second_halvings(three, four), *owed_up))
    first_sums = reduce_columns(*column_blocks(second_halvings(one, two)))
    owed_sum = return_rows(owed_cols, owed_up).astype(BF).reshape((2,) + flat)

    attended_late = after(attended, *key_sent, *value_sent)
    projection = times(attended_late, weight_out)
    block_output = (tokens_flat.astype(F32) + tissue_mask * projection).astype(BF)

    grad_projected = jnp.concatenate([grad_queries, owed_sum[0], owed_sum[1]], axis=-1)
    scaled = times_t(grad_projected, weight_in) * norm_gain
    inverse = moments[:, 1:2]
    normalized = (tokens_flat.astype(F32) - moments[:, :1]) * inverse
    first_mean = jnp.mean(scaled, axis=-1, keepdims=True)
    second_mean = jnp.mean(scaled * normalized, axis=-1, keepdims=True)
    input_grad = inverse * (scaled - first_mean - normalized * second_mean)
    input_grad = (cot_flat.astype(F32) + input_grad).astype(BF)

    second_sums = reduce_columns(after(mine, input_grad), others)
    inv_root = 1.0 / math.sqrt(slides * rows_count * cols_count * token_count)
    width = model_width
    weight_grads = jnp.concatenate(
        [first_sums[:, :width], second_sums, first_sums[:, width:]], axis=1
    )
    return (
        block_output.reshape((1,) + grid),
        input_grad.reshape((1,) + grid),
        weight_grads * inv_root,
    )


def solution(mesh):
    tile = P("slide", "gy", "gx", None)
    return jax.shard_map(
        local,
        mesh=mesh,
        in_specs=(tile, P(), P(), P("slide", "gy", "gx"), tile),
        out_specs=(tile, tile, P(("slide", "gy", "gx"), None)),
        check_vma=False,
    )
```

```python
import functools
import math

import jax
import jax.numpy as jnp
from jax import lax
from jax.experimental import pallas as pl
from jax.experimental.pallas import tpu as pltpu
from jax.sharding import PartitionSpec as P

HEADS = 16
RADIUS = 6
EPSILON = 1e-06
STRIP = 4
GROUP = 4
SIDE = 8
BF = jnp.bfloat16
F32 = jnp.float32


def swapped(array, axis, by):
    count = lax.axis_size(axis)
    return lax.ppermute(array, axis, [(i, i ^ by) for i in range(count)])


def moved(array, axis, by):
    count = lax.axis_size(axis)
    pairs = [(i, i + by) for i in range(count) if 0 <= i + by < count]
    return lax.ppermute(array, axis, pairs)


def rows_around(block, facing=None):
    rows_count = lax.axis_size("gy")
    if rows_count == 2:
        at_top = lax.axis_index("gy") == 0
        if facing is None:
            facing = jnp.where(at_top, block[-RADIUS:], block[:RADIUS])
        return (swapped(facing, "gy", 1),)
    return (moved(block[-RADIUS:], "gy", 1), moved(block[:RADIUS], "gy", -1))


def with_rows(block, rows):
    if len(rows) == 1:
        at_top = lax.axis_index("gy") == 0
        zero = jnp.zeros((), block.dtype)
        rows = (jnp.where(at_top, zero, rows[0]), jnp.where(at_top, rows[0], zero))
    return jnp.concatenate([rows[0], block, rows[1]], axis=0)


def facing_columns(to_right, to_left):
    even = lax.axis_index("gx") % 2 == 0
    return jnp.where(even, to_left, to_right), jnp.where(even, to_right, to_left)


def exchange_columns(out_one, out_two):
    count = lax.axis_size("gx")
    even = lax.axis_index("gx") % 2 == 0
    first, second = [], []
    for low in range(count - 1):
        pairs = first if low % 2 else second
        pairs += [(low, low + 1), (low + 1, low)]
    one = lax.ppermute(out_one, "gx", first)
    two = lax.ppermute(out_two, "gx", second)
    return jnp.where(even, one, two), jnp.where(even, two, one)


def column_halo(block):
    left, right = exchange_columns(*facing_columns(block[:, -SIDE:], block[:, :SIDE]))
    return jnp.concatenate([block, right, left], axis=1)


def owed_columns(grid):
    cols = grid.shape[2] - 2 * SIDE
    return facing_columns(grid[:, :, cols : cols + SIDE], grid[:, :, cols + SIDE :])


def return_columns(grid, out_one, out_two):
    cols = grid.shape[2] - 2 * SIDE
    from_left, from_right = exchange_columns(out_one, out_two)
    return grid[:, :, :cols].astype(F32) + jnp.concatenate([from_left, from_right], axis=2)


def owed_rows(grid):
    top, bottom = grid[:, :RADIUS].astype(BF), grid[:, -RADIUS:].astype(BF)
    if lax.axis_size("gy") == 2:
        return (jnp.where(lax.axis_index("gy") == 0, bottom, top),)
    return (top, bottom)


def return_rows(grid, outward):
    own = grid[:, RADIUS:-RADIUS]
    if len(outward) == 1:
        at_top = lax.axis_index("gy") == 0
        other = swapped(outward[0], "gy", 1)
        zero = jnp.zeros((), BF)
        above, below = jnp.where(at_top, zero, other), jnp.where(at_top, other, zero)
    else:
        above = moved(outward[1], "gy", 1)
        below = moved(outward[0], "gy", -1)
    rest = ((0, 0), (0, own.shape[1] - RADIUS), (0, 0), (0, 0))
    above = jnp.pad(above, rest)
    below = jnp.pad(below, (rest[0], rest[1][::-1], rest[2], rest[3]))
    return own + above.astype(F32) + below.astype(F32)


def in_hbm(array):
    return pltpu.with_memory_space_constraint(array, pltpu.HBM)


def prepare(
    place_ref, x_ref, c_ref, t_ref, gain_ref, normed_ref, branch_ref, face_ref, moment_ref
):
    block, width = x_ref.shape
    step = pl.program_id(0)
    rows = pl.ds(pl.multiple_of(step * block, block), block)
    x = x_ref[...].astype(F32)
    mean = jnp.sum(x, axis=1, keepdims=True) * (1.0 / width)
    centered = x - mean
    variance = jnp.sum(centered * centered, axis=1, keepdims=True) * (1.0 / width)
    inverse = lax.rsqrt(variance + EPSILON)
    normed_ref[rows, :] = (centered * inverse * gain_ref[...]).astype(BF)
    branch_ref[...] = (c_ref[...].astype(F32) * t_ref[...]).astype(BF)
    lane = lax.broadcasted_iota(jnp.int32, moment_ref.shape, 1)
    moment_ref[...] = jnp.where(lane == 0, mean, inverse)

    @pl.when(step == pl.num_programs(0) - 1)
    def _():
        first = pl.multiple_of(place_ref[4], 16)
        face_ref[...] = normed_ref[pl.ds(first, face_ref.shape[0]), :]


def run_prepare(place, tokens, cotangent, tissue, gain, face):
    count, width = tokens.shape
    block = min(count, 64)
    part = lambda columns: pl.BlockSpec((block, columns), lambda step: (step, 0))
    return pl.pallas_call(
        prepare,
        grid=(count // block,),
        in_specs=[SCALARS, part(width), part(width), part(1), whole((1, width))],
        out_specs=[whole((count, width)), part(width), whole((face, width)), part(128)],
        out_shape=[
            jax.ShapeDtypeStruct((count, width), BF),
            jax.ShapeDtypeStruct((count, width), BF),
            jax.ShapeDtypeStruct((face, width), BF),
            jax.ShapeDtypeStruct((count, 128), F32),
        ],
        compiler_params=pltpu.CompilerParams(**PARAMS),
        cost_estimate=pl.CostEstimate(flops=0, bytes_accessed=3 * 1024 * 1024, transcendentals=0),
        name="prepare",
    )(place, in_hbm(tokens), in_hbm(cotangent), tissue, in_hbm(gain))


def spread_heads(block, head_dim):
    lane_head = lax.broadcasted_iota(jnp.int32, block.shape, 1) // head_dim
    zero = jnp.zeros_like(block)
    return jnp.concatenate(
        [jnp.where(lane_head == head, block, zero) for head in range(GROUP)], axis=0
    )


def gather_heads(full, count, head_dim):
    lane_head = lax.broadcasted_iota(jnp.int32, (count, full.shape[1]), 1) // head_dim
    result = full[:count]
    for head in range(1, GROUP):
        result = jnp.where(lane_head == head, full[head * count : (head + 1) * count], result)
    return result


def times(left, right):
    return jnp.dot(left, right, preferred_element_type=F32)


def times_t(left, right):
    return lax.dot_general(left, right, (((1,), (1,)), ((), ())), preferred_element_type=F32)


def fill_bias(place_ref, bias_ref, tile_rows, tile_cols):
    strips, count, window = bias_ref.shape
    slots = tile_cols + 2 * SIDE
    own = lax.broadcasted_iota(jnp.int32, (count, window), 0)
    near = lax.broadcasted_iota(jnp.int32, (count, window), 1)
    own_row, own_col = own // tile_cols, own % tile_cols
    near_row, slot = near // slots, near % slots
    near_col = jnp.where(slot < tile_cols + SIDE, slot, slot - slots)
    row_gap = near_row - RADIUS - own_row
    col_gap = near_col - own_col
    col = place_ref[1] + near_col
    allowed = (jnp.abs(row_gap) <= RADIUS) & (jnp.abs(col_gap) <= RADIUS)
    allowed = allowed & (col >= 0) & (col < place_ref[3])
    for strip in range(strips):
        row = place_ref[0] + strip * STRIP + near_row - RADIUS
        kept = allowed & (row >= 0) & (row < place_ref[2])
        bias_ref[strip] = jnp.where(kept, 0.0, -1e30).astype(F32)


def query_pass(
    head_dim,
    tile,
    place_ref,
    q_ref,
    g_ref,
    normed_ref,
    key_w_ref,
    value_w_ref,
    out_ref,
    owed_ref,
    bias_ref,
    k_ref,
    v_ref,
    dk_ref,
    dv_ref,
):
    scaling = 1.0 / math.sqrt(head_dim)
    strips, count, window = bias_ref.shape
    step = (tile[1] + 2 * SIDE) * STRIP
    group = pl.program_id(0)

    @pl.when(group == 0)
    def _():
        fill_bias(place_ref, bias_ref, *tile)

    k_ref[...] = times(normed_ref[...], key_w_ref[...]).astype(BF)
    v_ref[...] = times(normed_ref[...], value_w_ref[...]).astype(BF)
    dk_ref[...] = jnp.zeros_like(dk_ref)
    dv_ref[...] = jnp.zeros_like(dv_ref)

    def dots(strip):
        own = pl.ds(strip * count, count)
        near = pl.ds(strip * step, window)
        queries = spread_heads(q_ref[own, :] * jnp.asarray(scaling, BF), head_dim)
        grads = spread_heads(g_ref[own, :], head_dim)
        scores = times_t(queries, k_ref[near, :])
        return queries, grads, scores, times_t(grads, v_ref[near, :])

    ahead = dots(0)
    for strip in range(strips):
        own = pl.ds(strip * count, count)
        near = pl.ds(strip * step, window)
        queries, grads, scores, grad_probs = ahead
        if strip + 1 < strips:
            ahead = dots(strip + 1)
        probs_parts, grad_parts = [], []
        for head in range(GROUP):
            part = slice(head * count, (head + 1) * count)
            masked = scores[part] + bias_ref[strip]
            row_max = jnp.max(masked, axis=1, keepdims=True)
            exponent = jnp.exp(masked - row_max)
            grad_part = grad_probs[part]
            total = jnp.sum(exponent, axis=1, keepdims=True)
            share = 1.0 / total
            delta = jnp.sum(exponent * grad_part, axis=1, keepdims=True) * share
            probs = exponent * share
            probs_parts.append(probs.astype(BF))
            grad_parts.append((probs * (grad_part - delta)).astype(BF))
        probs = jnp.concatenate(probs_parts, axis=0)
        grad_scores = jnp.concatenate(grad_parts, axis=0)
        attended = times(probs, v_ref[near, :])
        grad_queries = times(grad_scores, k_ref[near, :])
        out_ref[0, own, :] = gather_heads(attended, count, head_dim).astype(BF)
        out_ref[1, own, :] = (gather_heads(grad_queries, count, head_dim) * scaling).astype(BF)
        dk_ref[near, :] += product_t(grad_scores, queries)
        dv_ref[near, :] += product_t(probs, grads)
    owed_ref[0] = dk_ref[...].astype(BF)
    owed_ref[1] = dv_ref[...].astype(BF)


def whole(shape):
    return pl.BlockSpec(shape, lambda group: (0,) * len(shape))


def columns(rows, width, first=0):
    return pl.BlockSpec((rows, width), lambda group: (0, first + group))


def pair_columns(rows, width):
    return pl.BlockSpec((2, rows, width), lambda group: (0, 0, group))


SCALARS = pl.BlockSpec(memory_space=pltpu.SMEM)
PARAMS = dict(vmem_limit_bytes=24 * 1024 * 1024)


def window_shape(tile):
    return (tile[0] // STRIP, STRIP * tile[1], (STRIP + 2 * RADIUS) * (tile[1] + 2 * SIDE))


def attention_cost(tile, groups, part):
    strips, count, window = window_shape(tile)
    flops = 4 * 2 * groups * strips * GROUP * count * window * part
    return pl.CostEstimate(flops=flops, bytes_accessed=4 * 1024 * 1024, transcendentals=0)


def run_queries(place, queries, grads, normed_ext, weights, head_dim, tile):
    tokens, width = queries.shape
    ext = normed_ext.shape[0]
    part = GROUP * head_dim
    groups = width // part
    return pl.pallas_call(
        functools.partial(query_pass, head_dim, tile),
        grid=(groups,),
        in_specs=[
            SCALARS,
            columns(tokens, part),
            columns(tokens, part),
            whole(normed_ext.shape),
            columns(width, part, groups),
            columns(width, part, 2 * groups),
        ],
        out_specs=[pair_columns(tokens, part), pair_columns(ext, part)],
        out_shape=[
            jax.ShapeDtypeStruct((2, tokens, width), BF),
            jax.ShapeDtypeStruct((2, ext, width), BF),
        ],
        scratch_shapes=[pltpu.VMEM(window_shape(tile), F32)]
        + [pltpu.VMEM((ext, part), BF)] * 2
        + [pltpu.VMEM((ext, part), F32)] * 2,
        compiler_params=pltpu.CompilerParams(**PARAMS),
        cost_estimate=attention_cost(tile, groups, part),
        name="query_pass",
    )(place, queries, grads, normed_ext, in_hbm(weights), in_hbm(weights))


def own_part(array, index, axis):
    return lax.dynamic_index_in_dim(array, index, axis, keepdims=False)


def product_t(left, right):
    return lax.dot_general(left, right, (((0,), (0,)), ((), ())), preferred_element_type=F32)


def slide_swap(array, high):
    return swapped(array, "slide", lax.axis_size("slide") // 2 if high else 1)


def partners(across_slides):
    if across_slides:
        index = lax.axis_index("slide") // 2
        return index, [(1, 1 - index)]
    index = lax.axis_index("gy")
    return index, [(by, index ^ by) for by in range(1, lax.axis_size("gy"))]


def sent(block, across_slides, by):
    return slide_swap(block, True) if across_slides else swapped(block, "gy", by)


def pick_rows(array, index, across_slides, width):
    rows = width // lax.axis_size("slide")
    core = lax.axis_index("slide") % 2
    if across_slides:
        return lax.dynamic_slice_in_dim(array, (2 * index + core) * rows, rows, axis=1)
    rest = rows // lax.axis_size("gy")
    parts = [
        lax.dynamic_slice_in_dim(array, (2 * high + core) * rows + index * rest, rest, axis=1)
        for high in range(lax.axis_size("slide") // 2)
    ]
    return jnp.concatenate(parts, axis=1)


def pair_product(lefts, rights, index, across_slides):
    total = None
    for left, right in zip(lefts, rights):
        term = product_t(pick_rows(left, index, across_slides, right.shape[1]), right)
        total = term if total is None else total + term
    return total


def partner_half(left, right):
    rows = left.shape[1] // lax.axis_size("slide")
    other = 1 - lax.axis_index("slide") % 2
    parts = [
        lax.dynamic_slice_in_dim(left, (2 * high + other) * rows, rows, axis=1)
        for high in range(lax.axis_size("slide") // 2)
    ]
    return product_t(jnp.concatenate(parts, axis=1), right).astype(BF)


def halved_product(left, right, arrived, index, across_slides):
    rows = arrived.shape[0] // 2
    if across_slides:
        match = lax.dynamic_slice_in_dim(arrived, index * rows, rows, axis=0)
    else:
        rest = rows // lax.axis_size("gy")
        match = jnp.concatenate(
            [
                lax.dynamic_slice_in_dim(arrived, high * rows + index * rest, rest, axis=0)
                for high in range(2)
            ],
            axis=0,
        )
    return product_t(pick_rows(left, index, across_slides, left.shape[1]), right) + match.astype(F32)


def blocks_of(product, across_slides):
    index, others = partners(across_slides)
    return [product(target).astype(BF) for _, target in others], lambda: product(index)


def first_halving(blocks, mine, across_slides):
    others = partners(across_slides)[1]
    arrived = [sent(block, across_slides, by) for block, (by, _) in zip(blocks, others)]
    total = mine()
    for block in arrived:
        total = total + block.astype(F32)
    return total


def second_halving(part, across_slides):
    index, others = partners(across_slides)
    rows = part.shape[0] // (len(others) + 1)
    mine = lax.dynamic_slice_in_dim(part, index * rows, rows, axis=0)
    for by, target in others:
        block = lax.dynamic_slice_in_dim(part, target * rows, rows, axis=0).astype(BF)
        mine = mine + sent(block, across_slides, by).astype(F32)
    return mine


def column_blocks(part):
    count = lax.axis_size("gx")
    index = lax.axis_index("gx")
    rows = part.shape[0] // count
    mine = lax.dynamic_slice_in_dim(part, index * rows, rows, axis=0)
    others = [
        lax.dynamic_slice_in_dim(part, (index ^ by) * rows, rows, axis=0).astype(BF)
        for by in range(count - 1, 0, -1)
    ]
    return mine, others


def reduce_columns(mine, others):
    count = lax.axis_size("gx")
    arrived = [
        swapped(block, "gx", by) for block, by in zip(others, range(count - 1, 0, -1))
    ]
    for block in arrived:
        mine = mine + block.astype(F32)
    return mine


def halve_columns(part):
    count, width = lax.axis_size("gx"), part.shape[1]
    index = lax.axis_index("gx")
    rows = part.shape[0] // count
    by = 1
    while by < count:
        bit = lax.rem(index // by, 2)
        blocks = part.reshape(-1, 2, rows, width)
        going = lax.dynamic_index_in_dim(blocks, 1 - bit, 1, keepdims=False).astype(BF)
        kept = lax.dynamic_index_in_dim(blocks, bit, 1, keepdims=False)
        part = (kept + swapped(going, "gx", by).astype(F32)).reshape(-1, width)
        by *= 2
    return part


def second_halvings(one, two):
    return jnp.concatenate([second_halving(one, False), second_halving(two, True)], axis=1)


def after(array, *earlier):
    return lax.optimization_barrier((array, *earlier))[0]


def local(tokens, weights, norm_gain, tissue, cotangent):
    tile_tokens = tokens[0]
    tile_rows, tile_cols, model_width = tile_tokens.shape
    tile = (tile_rows, tile_cols)
    head_dim = model_width // HEADS
    token_count = tile_rows * tile_cols
    slides = lax.axis_size("slide")
    rows_count = lax.axis_size("gy")
    cols_count = lax.axis_size("gx")
    weight_in = weights[:, : 3 * model_width]
    weight_out = weights[:, 3 * model_width :]
    face = RADIUS * tile_cols
    at_top = lax.axis_index("gy") == 0
    place = jnp.stack(
        [
            lax.axis_index("gy") * tile_rows,
            lax.axis_index("gx") * tile_cols,
            jnp.int32(tile_rows * rows_count),
            jnp.int32(tile_cols * cols_count),
            jnp.where(at_top, token_count - face, 0),
        ]
    ).astype(jnp.int32)

    flat = (token_count, model_width)
    grid = (tile_rows, tile_cols, model_width)
    tissue_mask = tissue[0].astype(F32).reshape(token_count, 1)
    tokens_flat = tile_tokens.reshape(flat)
    cot_flat = cotangent[0].reshape(flat)
    normed, branch_flat, facing, moments = run_prepare(
        place, tokens_flat, cot_flat, tissue_mask, norm_gain.reshape(1, model_width), face
    )
    normed_tile = normed.reshape(grid)
    rows = rows_around(normed_tile, facing.reshape(RADIUS, tile_cols, model_width))
    middle = column_halo(normed_tile)
    normed_ext = with_rows(middle, [column_halo(row) for row in rows])
    ext_rows, ext_cols = normed_ext.shape[:2]
    normed_ext = normed_ext.reshape(ext_rows * ext_cols, model_width)

    grad_attn = times_t(branch_flat, weight_out).astype(BF)
    queries = times(after(normed, *rows), weight_in[:, :model_width]).astype(BF)
    normed_late, branch_late, queries = lax.optimization_barrier((normed, branch_flat, queries))
    normed_pair = (normed, slide_swap(normed_late, False))
    branch_pair = (branch_flat, slide_swap(branch_late, False))

    found, owed = run_queries(place, queries, grad_attn, normed_ext, weights, head_dim, tile)
    attended, grad_queries = found[0], found[1]

    found_other = slide_swap(found, False)
    key_half = partner_half(normed_ext, owed[0])
    value_half = partner_half(normed_ext, owed[1])
    key_arrived, value_arrived = slide_swap(key_half, False), slide_swap(value_half, False)
    found_other = after(found_other, key_half, value_half)
    query_sent, query_kept = blocks_of(
        lambda index: pair_product(normed_pair, (grad_queries, found_other[1]), index, True), True
    )
    out_sent, out_kept = blocks_of(
        lambda index: pair_product((attended, found_other[0]), branch_pair, index, False), False
    )

    owed_grid = after(owed, *query_sent, *out_sent)
    owed_grid = owed_grid.reshape(2, ext_rows, ext_cols, model_width)
    outward = owed_columns(owed_grid)
    key_sent, key_kept = blocks_of(
        lambda index: halved_product(normed_ext, owed[0], key_arrived, index, True), True
    )
    value_sent, value_kept = blocks_of(
        lambda index: halved_product(normed_ext, owed[1], value_arrived, index, False), False
    )

    first_kept = lax.optimization_barrier((query_kept(), out_kept(), key_sent, value_sent))[:2]
    one = first_halving(query_sent, lambda: first_kept[0], True)
    two = first_halving(out_sent, lambda: first_kept[1], False)
    second_kept = lax.optimization_barrier((key_kept(), value_kept(), one, two))[:2]
    three = first_halving(key_sent, lambda: second_kept[0], True)
    four = first_halving(value_sent, lambda: second_kept[1], False)
    owed_cols = return_columns(owed_grid, *outward)
    owed_up = owed_rows(owed_cols)
    mine, others = column_blocks(after(second_halvings(three, four), *owed_up))
    first_sums = reduce_columns(*column_blocks(second_halvings(one, two)))
    owed_sum = return_rows(owed_cols, owed_up).astype(BF).reshape((2,) + flat)

    attended_late = after(attended, *key_sent, *value_sent)
    projection = times(attended_late, weight_out)
    block_output = (tokens_flat.astype(F32) + tissue_mask * projection).astype(BF)

    grad_projected = jnp.concatenate([grad_queries, owed_sum[0], owed_sum[1]], axis=-1)
    scaled = times_t(grad_projected, weight_in) * norm_gain
    inverse = moments[:, 1:2]
    normalized = (tokens_flat.astype(F32) - moments[:, :1]) * inverse
    first_mean = jnp.mean(scaled, axis=-1, keepdims=True)
    second_mean = jnp.mean(scaled * normalized, axis=-1, keepdims=True)
    input_grad = inverse * (scaled - first_mean - normalized * second_mean)
    input_grad = (cot_flat.astype(F32) + input_grad).astype(BF)

    second_sums = reduce_columns(after(mine, input_grad), others)
    inv_root = 1.0 / math.sqrt(slides * rows_count * cols_count * token_count)
    width = model_width
    weight_grads = jnp.concatenate(
        [first_sums[:, :width], second_sums, first_sums[:, width:]], axis=1
    )
    return (
        block_output.reshape((1,) + grid),
        input_grad.reshape((1,) + grid),
        weight_grads * inv_root,
    )


def solution(mesh):
    tile = P("slide", "gy", "gx", None)
    return jax.shard_map(
        local,
        mesh=mesh,
        in_specs=(tile, P(), P(), P("slide", "gy", "gx"), tile),
        out_specs=(tile, tile, P(("slide", "gy", "gx"), None)),
        check_vma=False,
    )
```

```python
import functools
import math

import jax
import jax.numpy as jnp
from jax import lax
from jax.experimental import pallas as pl
from jax.experimental.pallas import tpu as pltpu
from jax.sharding import PartitionSpec as P

HEADS = 16
RADIUS = 6
EPSILON = 1e-06
STRIP = 4
GROUP = 4
SIDE = 8
BF = jnp.bfloat16
F32 = jnp.float32


def swapped(array, axis, by):
    count = lax.axis_size(axis)
    return lax.ppermute(array, axis, [(i, i ^ by) for i in range(count)])


def moved(array, axis, by):
    count = lax.axis_size(axis)
    pairs = [(i, i + by) for i in range(count) if 0 <= i + by < count]
    return lax.ppermute(array, axis, pairs)


def rows_around(block, facing=None):
    rows_count = lax.axis_size("gy")
    if rows_count == 2:
        at_top = lax.axis_index("gy") == 0
        if facing is None:
            facing = jnp.where(at_top, block[-RADIUS:], block[:RADIUS])
        return (swapped(facing, "gy", 1),)
    return (moved(block[-RADIUS:], "gy", 1), moved(block[:RADIUS], "gy", -1))


def with_rows(block, rows):
    if len(rows) == 1:
        at_top = lax.axis_index("gy") == 0
        zero = jnp.zeros((), block.dtype)
        rows = (jnp.where(at_top, zero, rows[0]), jnp.where(at_top, rows[0], zero))
    return jnp.concatenate([rows[0], block, rows[1]], axis=0)


def facing_columns(to_right, to_left):
    even = lax.axis_index("gx") % 2 == 0
    return jnp.where(even, to_left, to_right), jnp.where(even, to_right, to_left)


def exchange_columns(out_one, out_two):
    count = lax.axis_size("gx")
    even = lax.axis_index("gx") % 2 == 0
    first, second = [], []
    for low in range(count - 1):
        pairs = first if low % 2 else second
        pairs += [(low, low + 1), (low + 1, low)]
    one = lax.ppermute(out_one, "gx", first)
    two = lax.ppermute(out_two, "gx", second)
    return jnp.where(even, one, two), jnp.where(even, two, one)


def column_halo(block):
    left, right = exchange_columns(*facing_columns(block[:, -SIDE:], block[:, :SIDE]))
    return jnp.concatenate([block, right, left], axis=1)


def owed_columns(grid):
    cols = grid.shape[2] - 2 * SIDE
    return facing_columns(grid[:, :, cols : cols + SIDE], grid[:, :, cols + SIDE :])


def return_columns(grid, out_one, out_two):
    cols = grid.shape[2] - 2 * SIDE
    from_left, from_right = exchange_columns(out_one, out_two)
    return grid[:, :, :cols].astype(F32) + jnp.concatenate([from_left, from_right], axis=2)


def owed_rows(grid):
    top, bottom = grid[:, :RADIUS].astype(BF), grid[:, -RADIUS:].astype(BF)
    if lax.axis_size("gy") == 2:
        return (jnp.where(lax.axis_index("gy") == 0, bottom, top),)
    return (top, bottom)


def return_rows(grid, outward):
    own = grid[:, RADIUS:-RADIUS]
    if len(outward) == 1:
        at_top = lax.axis_index("gy") == 0
        other = swapped(outward[0], "gy", 1)
        zero = jnp.zeros((), BF)
        above, below = jnp.where(at_top, zero, other), jnp.where(at_top, other, zero)
    else:
        above = moved(outward[1], "gy", 1)
        below = moved(outward[0], "gy", -1)
    rest = ((0, 0), (0, own.shape[1] - RADIUS), (0, 0), (0, 0))
    above = jnp.pad(above, rest)
    below = jnp.pad(below, (rest[0], rest[1][::-1], rest[2], rest[3]))
    return own + above.astype(F32) + below.astype(F32)


def in_hbm(array):
    return pltpu.with_memory_space_constraint(array, pltpu.HBM)


def prepare(
    place_ref, x_ref, c_ref, t_ref, gain_ref, normed_ref, branch_ref, face_ref, moment_ref
):
    block, width = x_ref.shape
    step = pl.program_id(0)
    rows = pl.ds(pl.multiple_of(step * block, block), block)
    x = x_ref[...].astype(F32)
    mean = jnp.sum(x, axis=1, keepdims=True) * (1.0 / width)
    centered = x - mean
    variance = jnp.sum(centered * centered, axis=1, keepdims=True) * (1.0 / width)
    inverse = lax.rsqrt(variance + EPSILON)
    normed_ref[rows, :] = (centered * inverse * gain_ref[...]).astype(BF)
    branch_ref[...] = (c_ref[...].astype(F32) * t_ref[...]).astype(BF)
    lane = lax.broadcasted_iota(jnp.int32, moment_ref.shape, 1)
    moment_ref[...] = jnp.where(lane == 0, mean, inverse)

    @pl.when(step == pl.num_programs(0) - 1)
    def _():
        first = pl.multiple_of(place_ref[4], 16)
        face_ref[...] = normed_ref[pl.ds(first, face_ref.shape[0]), :]


def run_prepare(place, tokens, cotangent, tissue, gain, face):
    count, width = tokens.shape
    block = min(count, 128)
    part = lambda columns: pl.BlockSpec((block, columns), lambda step: (step, 0))
    return pl.pallas_call(
        prepare,
        grid=(count // block,),
        in_specs=[SCALARS, part(width), part(width), part(1), whole((1, width))],
        out_specs=[whole((count, width)), part(width), whole((face, width)), part(128)],
        out_shape=[
            jax.ShapeDtypeStruct((count, width), BF),
            jax.ShapeDtypeStruct((count, width), BF),
            jax.ShapeDtypeStruct((face, width), BF),
            jax.ShapeDtypeStruct((count, 128), F32),
        ],
        compiler_params=pltpu.CompilerParams(**PARAMS),
        cost_estimate=pl.CostEstimate(flops=0, bytes_accessed=3 * 1024 * 1024, transcendentals=0),
        name="prepare",
    )(place, in_hbm(tokens), in_hbm(cotangent), tissue, in_hbm(gain))


def spread_heads(block, head_dim):
    lane_head = lax.broadcasted_iota(jnp.int32, block.shape, 1) // head_dim
    zero = jnp.zeros_like(block)
    return jnp.concatenate(
        [jnp.where(lane_head == head, block, zero) for head in range(GROUP)], axis=0
    )


def gather_heads(full, count, head_dim):
    lane_head = lax.broadcasted_iota(jnp.int32, (count, full.shape[1]), 1) // head_dim
    result = full[:count]
    for head in range(1, GROUP):
        result = jnp.where(lane_head == head, full[head * count : (head + 1) * count], result)
    return result


def times(left, right):
    return jnp.dot(left, right, preferred_element_type=F32)


def times_t(left, right):
    return lax.dot_general(left, right, (((1,), (1,)), ((), ())), preferred_element_type=F32)


def fill_bias(place_ref, bias_ref, tile_rows, tile_cols):
    strips, count, window = bias_ref.shape
    slots = tile_cols + 2 * SIDE
    own = lax.broadcasted_iota(jnp.int32, (count, window), 0)
    near = lax.broadcasted_iota(jnp.int32, (count, window), 1)
    own_row, own_col = own // tile_cols, own % tile_cols
    near_row, slot = near // slots, near % slots
    near_col = jnp.where(slot < tile_cols + SIDE, slot, slot - slots)
    row_gap = near_row - RADIUS - own_row
    col_gap = near_col - own_col
    col = place_ref[1] + near_col
    allowed = (jnp.abs(row_gap) <= RADIUS) & (jnp.abs(col_gap) <= RADIUS)
    allowed = allowed & (col >= 0) & (col < place_ref[3])
    for strip in range(strips):
        row = place_ref[0] + strip * STRIP + near_row - RADIUS
        kept = allowed & (row >= 0) & (row < place_ref[2])
        bias_ref[strip] = jnp.where(kept, 0.0, -1e30).astype(F32)


def query_pass(
    head_dim,
    tile,
    place_ref,
    q_ref,
    g_ref,
    normed_ref,
    key_w_ref,
    value_w_ref,
    out_ref,
    owed_ref,
    bias_ref,
    k_ref,
    v_ref,
    dk_ref,
    dv_ref,
):
    scaling = 1.0 / math.sqrt(head_dim)
    strips, count, window = bias_ref.shape
    step = (tile[1] + 2 * SIDE) * STRIP
    group = pl.program_id(0)

    @pl.when(group == 0)
    def _():
        fill_bias(place_ref, bias_ref, *tile)

    k_ref[...] = times(normed_ref[...], key_w_ref[...]).astype(BF)
    v_ref[...] = times(normed_ref[...], value_w_ref[...]).astype(BF)
    dk_ref[...] = jnp.zeros_like(dk_ref)
    dv_ref[...] = jnp.zeros_like(dv_ref)

    def dots(strip):
        own = pl.ds(strip * count, count)
        near = pl.ds(strip * step, window)
        queries = spread_heads(q_ref[own, :] * jnp.asarray(scaling, BF), head_dim)
        grads = spread_heads(g_ref[own, :], head_dim)
        scores = times_t(queries, k_ref[near, :])
        return queries, grads, scores, times_t(grads, v_ref[near, :])

    ahead = dots(0)
    for strip in range(strips):
        own = pl.ds(strip * count, count)
        near = pl.ds(strip * step, window)
        queries, grads, scores, grad_probs = ahead
        if strip + 1 < strips:
            ahead = dots(strip + 1)
        probs_parts, grad_parts = [], []
        for head in range(GROUP):
            part = slice(head * count, (head + 1) * count)
            masked = scores[part] + bias_ref[strip]
            row_max = jnp.max(masked, axis=1, keepdims=True)
            exponent = jnp.exp(masked - row_max)
            grad_part = grad_probs[part]
            total = jnp.sum(exponent, axis=1, keepdims=True)
            share = 1.0 / total
            delta = jnp.sum(exponent * grad_part, axis=1, keepdims=True) * share
            probs = exponent * share
            probs_parts.append(probs.astype(BF))
            grad_parts.append((probs * (grad_part - delta)).astype(BF))
        probs = jnp.concatenate(probs_parts, axis=0)
        grad_scores = jnp.concatenate(grad_parts, axis=0)
        attended = times(probs, v_ref[near, :])
        grad_queries = times(grad_scores, k_ref[near, :])
        out_ref[0, own, :] = gather_heads(attended, count, head_dim).astype(BF)
        out_ref[1, own, :] = (gather_heads(grad_queries, count, head_dim) * scaling).astype(BF)
        dk_ref[near, :] += product_t(grad_scores, queries)
        dv_ref[near, :] += product_t(probs, grads)
    owed_ref[0] = dk_ref[...].astype(BF)
    owed_ref[1] = dv_ref[...].astype(BF)


def whole(shape):
    return pl.BlockSpec(shape, lambda group: (0,) * len(shape))


def columns(rows, width, first=0):
    return pl.BlockSpec((rows, width), lambda group: (0, first + group))


def pair_columns(rows, width):
    return pl.BlockSpec((2, rows, width), lambda group: (0, 0, group))


SCALARS = pl.BlockSpec(memory_space=pltpu.SMEM)
PARAMS = dict(vmem_limit_bytes=24 * 1024 * 1024)


def window_shape(tile):
    return (tile[0] // STRIP, STRIP * tile[1], (STRIP + 2 * RADIUS) * (tile[1] + 2 * SIDE))


def attention_cost(tile, groups, part):
    strips, count, window = window_shape(tile)
    flops = 4 * 2 * groups * strips * GROUP * count * window * part
    return pl.CostEstimate(flops=flops, bytes_accessed=4 * 1024 * 1024, transcendentals=0)


def run_queries(place, queries, grads, normed_ext, weights, head_dim, tile):
    tokens, width = queries.shape
    ext = normed_ext.shape[0]
    part = GROUP * head_dim
    groups = width // part
    return pl.pallas_call(
        functools.partial(query_pass, head_dim, tile),
        grid=(groups,),
        in_specs=[
            SCALARS,
            columns(tokens, part),
            columns(tokens, part),
            pl.BlockSpec(normed_ext.shape, lambda group: (0, 0), pipeline_mode=pl.Buffered(1)),
            columns(width, part, groups),
            columns(width, part, 2 * groups),
        ],
        out_specs=[pair_columns(tokens, part), pair_columns(ext, part)],
        out_shape=[
            jax.ShapeDtypeStruct((2, tokens, width), BF),
            jax.ShapeDtypeStruct((2, ext, width), BF),
        ],
        scratch_shapes=[pltpu.VMEM(window_shape(tile), F32)]
        + [pltpu.VMEM((ext, part), BF)] * 2
        + [pltpu.VMEM((ext, part), F32)] * 2,
        compiler_params=pltpu.CompilerParams(**PARAMS),
        cost_estimate=attention_cost(tile, groups, part),
        name="query_pass",
    )(place, queries, grads, normed_ext, in_hbm(weights), in_hbm(weights))


def own_part(array, index, axis):
    return lax.dynamic_index_in_dim(array, index, axis, keepdims=False)


def product_t(left, right):
    return lax.dot_general(left, right, (((0,), (0,)), ((), ())), preferred_element_type=F32)


def slide_swap(array, high):
    return swapped(array, "slide", lax.axis_size("slide") // 2 if high else 1)


def partners(across_slides):
    if across_slides:
        index = lax.axis_index("slide") // 2
        return index, [(1, 1 - index)]
    index = lax.axis_index("gy")
    return index, [(by, index ^ by) for by in range(1, lax.axis_size("gy"))]


def sent(block, across_slides, by):
    return slide_swap(block, True) if across_slides else swapped(block, "gy", by)


def pick_rows(array, index, across_slides, width):
    rows = width // lax.axis_size("slide")
    core = lax.axis_index("slide") % 2
    if across_slides:
        return lax.dynamic_slice_in_dim(array, (2 * index + core) * rows, rows, axis=1)
    rest = rows // lax.axis_size("gy")
    parts = [
        lax.dynamic_slice_in_dim(array, (2 * high + core) * rows + index * rest, rest, axis=1)
        for high in range(lax.axis_size("slide") // 2)
    ]
    return jnp.concatenate(parts, axis=1)


def pair_product(lefts, rights, index, across_slides):
    total = None
    for left, right in zip(lefts, rights):
        term = product_t(pick_rows(left, index, across_slides, right.shape[1]), right)
        total = term if total is None else total + term
    return total


def partner_half(left, right):
    rows = left.shape[1] // lax.axis_size("slide")
    other = 1 - lax.axis_index("slide") % 2
    parts = [
        lax.dynamic_slice_in_dim(left, (2 * high + other) * rows, rows, axis=1)
        for high in range(lax.axis_size("slide") // 2)
    ]
    return product_t(jnp.concatenate(parts, axis=1), right).astype(BF)


def halved_product(left, right, arrived, index, across_slides):
    rows = arrived.shape[0] // 2
    if across_slides:
        match = lax.dynamic_slice_in_dim(arrived, index * rows, rows, axis=0)
    else:
        rest = rows // lax.axis_size("gy")
        match = jnp.concatenate(
            [
                lax.dynamic_slice_in_dim(arrived, high * rows + index * rest, rest, axis=0)
                for high in range(2)
            ],
            axis=0,
        )
    return product_t(pick_rows(left, index, across_slides, left.shape[1]), right) + match.astype(F32)


def blocks_of(product, across_slides):
    index, others = partners(across_slides)
    return [product(target).astype(BF) for _, target in others], lambda: product(index)


def first_halving(blocks, mine, across_slides):
    others = partners(across_slides)[1]
    arrived = [sent(block, across_slides, by) for block, (by, _) in zip(blocks, others)]
    total = mine()
    for block in arrived:
        total = total + block.astype(F32)
    return total


def second_halving(part, across_slides):
    index, others = partners(across_slides)
    rows = part.shape[0] // (len(others) + 1)
    mine = lax.dynamic_slice_in_dim(part, index * rows, rows, axis=0)
    for by, target in others:
        block = lax.dynamic_slice_in_dim(part, target * rows, rows, axis=0).astype(BF)
        mine = mine + sent(block, across_slides, by).astype(F32)
    return mine


def column_blocks(part):
    count = lax.axis_size("gx")
    index = lax.axis_index("gx")
    rows = part.shape[0] // count
    mine = lax.dynamic_slice_in_dim(part, index * rows, rows, axis=0)
    others = [
        lax.dynamic_slice_in_dim(part, (index ^ by) * rows, rows, axis=0).astype(BF)
        for by in range(count - 1, 0, -1)
    ]
    return mine, others


def reduce_columns(mine, others):
    count = lax.axis_size("gx")
    arrived = [
        swapped(block, "gx", by) for block, by in zip(others, range(count - 1, 0, -1))
    ]
    for block in arrived:
        mine = mine + block.astype(F32)
    return mine


def halve_columns(part):
    count, width = lax.axis_size("gx"), part.shape[1]
    index = lax.axis_index("gx")
    rows = part.shape[0] // count
    by = 1
    while by < count:
        bit = lax.rem(index // by, 2)
        blocks = part.reshape(-1, 2, rows, width)
        going = lax.dynamic_index_in_dim(blocks, 1 - bit, 1, keepdims=False).astype(BF)
        kept = lax.dynamic_index_in_dim(blocks, bit, 1, keepdims=False)
        part = (kept + swapped(going, "gx", by).astype(F32)).reshape(-1, width)
        by *= 2
    return part


def second_halvings(one, two):
    return jnp.concatenate([second_halving(one, False), second_halving(two, True)], axis=1)


def after(array, *earlier):
    return lax.optimization_barrier((array, *earlier))[0]


def local(tokens, weights, norm_gain, tissue, cotangent):
    tile_tokens = tokens[0]
    tile_rows, tile_cols, model_width = tile_tokens.shape
    tile = (tile_rows, tile_cols)
    head_dim = model_width // HEADS
    token_count = tile_rows * tile_cols
    slides = lax.axis_size("slide")
    rows_count = lax.axis_size("gy")
    cols_count = lax.axis_size("gx")
    weight_in = weights[:, : 3 * model_width]
    weight_out = weights[:, 3 * model_width :]
    face = RADIUS * tile_cols
    at_top = lax.axis_index("gy") == 0
    place = jnp.stack(
        [
            lax.axis_index("gy") * tile_rows,
            lax.axis_index("gx") * tile_cols,
            jnp.int32(tile_rows * rows_count),
            jnp.int32(tile_cols * cols_count),
            jnp.where(at_top, token_count - face, 0),
        ]
    ).astype(jnp.int32)

    flat = (token_count, model_width)
    grid = (tile_rows, tile_cols, model_width)
    tissue_mask = tissue[0].astype(F32).reshape(token_count, 1)
    tokens_flat = tile_tokens.reshape(flat)
    cot_flat = cotangent[0].reshape(flat)
    normed, branch_flat, facing, moments = run_prepare(
        place, tokens_flat, cot_flat, tissue_mask, norm_gain.reshape(1, model_width), face
    )
    normed_tile = normed.reshape(grid)
    rows = rows_around(normed_tile, facing.reshape(RADIUS, tile_cols, model_width))
    middle = column_halo(normed_tile)
    normed_ext = with_rows(middle, [column_halo(row) for row in rows])
    ext_rows, ext_cols = normed_ext.shape[:2]
    normed_ext = normed_ext.reshape(ext_rows * ext_cols, model_width)

    grad_attn = times_t(branch_flat, weight_out).astype(BF)
    queries = times(after(normed, *rows), weight_in[:, :model_width]).astype(BF)
    normed_late, branch_late, queries = lax.optimization_barrier((normed, branch_flat, queries))
    normed_pair = (normed, slide_swap(normed_late, False))
    branch_pair = (branch_flat, slide_swap(branch_late, False))

    found, owed = run_queries(place, queries, grad_attn, normed_ext, weights, head_dim, tile)
    attended, grad_queries = found[0], found[1]

    found_other = slide_swap(found, False)
    key_half = partner_half(normed_ext, owed[0])
    value_half = partner_half(normed_ext, owed[1])
    key_arrived, value_arrived = slide_swap(key_half, False), slide_swap(value_half, False)
    found_other = after(found_other, key_half, value_half)
    query_sent, query_kept = blocks_of(
        lambda index: pair_product(normed_pair, (grad_queries, found_other[1]), index, True), True
    )
    out_sent, out_kept = blocks_of(
        lambda index: pair_product((attended, found_other[0]), branch_pair, index, False), False
    )

    owed_grid = after(owed, *query_sent, *out_sent)
    owed_grid = owed_grid.reshape(2, ext_rows, ext_cols, model_width)
    outward = owed_columns(owed_grid)
    key_sent, key_kept = blocks_of(
        lambda index: halved_product(normed_ext, owed[0], key_arrived, index, True), True
    )
    value_sent, value_kept = blocks_of(
        lambda index: halved_product(normed_ext, owed[1], value_arrived, index, False), False
    )

    first_kept = lax.optimization_barrier((query_kept(), out_kept(), key_sent, value_sent))[:2]
    one = first_halving(query_sent, lambda: first_kept[0], True)
    two = first_halving(out_sent, lambda: first_kept[1], False)
    second_kept = lax.optimization_barrier((key_kept(), value_kept(), one, two))[:2]
    three = first_halving(key_sent, lambda: second_kept[0], True)
    four = first_halving(value_sent, lambda: second_kept[1], False)
    owed_cols = return_columns(owed_grid, *outward)
    owed_up = owed_rows(owed_cols)
    mine, others = column_blocks(after(second_halvings(three, four), *owed_up))
    first_sums = reduce_columns(*column_blocks(second_halvings(one, two)))
    owed_sum = return_rows(owed_cols, owed_up).astype(BF).reshape((2,) + flat)

    attended_late = after(attended, *key_sent, *value_sent)
    projection = times(attended_late, weight_out)
    block_output = (tokens_flat.astype(F32) + tissue_mask * projection).astype(BF)

    grad_projected = jnp.concatenate([grad_queries, owed_sum[0], owed_sum[1]], axis=-1)
    scaled = times_t(grad_projected, weight_in) * norm_gain
    inverse = moments[:, 1:2]
    normalized = (tokens_flat.astype(F32) - moments[:, :1]) * inverse
    first_mean = jnp.mean(scaled, axis=-1, keepdims=True)
    second_mean = jnp.mean(scaled * normalized, axis=-1, keepdims=True)
    input_grad = inverse * (scaled - first_mean - normalized * second_mean)
    input_grad = (cot_flat.astype(F32) + input_grad).astype(BF)

    second_sums = reduce_columns(after(mine, input_grad), others)
    inv_root = 1.0 / math.sqrt(slides * rows_count * cols_count * token_count)
    width = model_width
    weight_grads = jnp.concatenate(
        [first_sums[:, :width], second_sums, first_sums[:, width:]], axis=1
    )
    return (
        block_output.reshape((1,) + grid),
        input_grad.reshape((1,) + grid),
        weight_grads * inv_root,
    )


def solution(mesh):
    tile = P("slide", "gy", "gx", None)
    return jax.shard_map(
        local,
        mesh=mesh,
        in_specs=(tile, P(), P(), P("slide", "gy", "gx"), tile),
        out_specs=(tile, tile, P(("slide", "gy", "gx"), None)),
        check_vma=False,
    )
```

```python
import functools
import math

import jax
import jax.numpy as jnp
from jax import lax
from jax.experimental import pallas as pl
from jax.experimental.pallas import tpu as pltpu
from jax.sharding import PartitionSpec as P

HEADS = 16
RADIUS = 6
EPSILON = 1e-06
STRIP = 4
GROUP = 4
SIDE = 8
BF = jnp.bfloat16
F32 = jnp.float32


def swapped(array, axis, by):
    count = lax.axis_size(axis)
    return lax.ppermute(array, axis, [(i, i ^ by) for i in range(count)])


def moved(array, axis, by):
    count = lax.axis_size(axis)
    pairs = [(i, i + by) for i in range(count) if 0 <= i + by < count]
    return lax.ppermute(array, axis, pairs)


def rows_around(block, facing=None):
    rows_count = lax.axis_size("gy")
    if rows_count == 2:
        at_top = lax.axis_index("gy") == 0
        if facing is None:
            facing = jnp.where(at_top, block[-RADIUS:], block[:RADIUS])
        return (swapped(facing, "gy", 1),)
    return (moved(block[-RADIUS:], "gy", 1), moved(block[:RADIUS], "gy", -1))


def with_rows(block, rows):
    if len(rows) == 1:
        at_top = lax.axis_index("gy") == 0
        zero = jnp.zeros((), block.dtype)
        rows = (jnp.where(at_top, zero, rows[0]), jnp.where(at_top, rows[0], zero))
    return jnp.concatenate([rows[0], block, rows[1]], axis=0)


def facing_columns(to_right, to_left):
    even = lax.axis_index("gx") % 2 == 0
    return jnp.where(even, to_left, to_right), jnp.where(even, to_right, to_left)


def exchange_columns(out_one, out_two):
    count = lax.axis_size("gx")
    even = lax.axis_index("gx") % 2 == 0
    first, second = [], []
    for low in range(count - 1):
        pairs = first if low % 2 else second
        pairs += [(low, low + 1), (low + 1, low)]
    one = lax.ppermute(out_one, "gx", first)
    two = lax.ppermute(out_two, "gx", second)
    return jnp.where(even, one, two), jnp.where(even, two, one)


def column_halo(block):
    left, right = exchange_columns(*facing_columns(block[:, -SIDE:], block[:, :SIDE]))
    return jnp.concatenate([block, right, left], axis=1)


def owed_columns(grid):
    cols = grid.shape[2] - 2 * SIDE
    return facing_columns(grid[:, :, cols : cols + SIDE], grid[:, :, cols + SIDE :])


def return_columns(grid, out_one, out_two):
    cols = grid.shape[2] - 2 * SIDE
    from_left, from_right = exchange_columns(out_one, out_two)
    return grid[:, :, :cols].astype(F32) + jnp.concatenate([from_left, from_right], axis=2)


def owed_rows(grid):
    top, bottom = grid[:, :RADIUS].astype(BF), grid[:, -RADIUS:].astype(BF)
    if lax.axis_size("gy") == 2:
        return (jnp.where(lax.axis_index("gy") == 0, bottom, top),)
    return (top, bottom)


def return_rows(grid, outward):
    own = grid[:, RADIUS:-RADIUS]
    if len(outward) == 1:
        at_top = lax.axis_index("gy") == 0
        other = swapped(outward[0], "gy", 1)
        zero = jnp.zeros((), BF)
        above, below = jnp.where(at_top, zero, other), jnp.where(at_top, other, zero)
    else:
        above = moved(outward[1], "gy", 1)
        below = moved(outward[0], "gy", -1)
    rest = ((0, 0), (0, own.shape[1] - RADIUS), (0, 0), (0, 0))
    above = jnp.pad(above, rest)
    below = jnp.pad(below, (rest[0], rest[1][::-1], rest[2], rest[3]))
    return own + above.astype(F32) + below.astype(F32)


def in_hbm(array):
    return pltpu.with_memory_space_constraint(array, pltpu.HBM)


def prepare(
    place_ref, x_ref, gain_ref, normed_ref, face_ref, moment_ref
):
    block, width = x_ref.shape
    step = pl.program_id(0)
    rows = pl.ds(pl.multiple_of(step * block, block), block)
    x = x_ref[...].astype(F32)
    mean = jnp.sum(x, axis=1, keepdims=True) * (1.0 / width)
    centered = x - mean
    variance = jnp.sum(centered * centered, axis=1, keepdims=True) * (1.0 / width)
    inverse = lax.rsqrt(variance + EPSILON)
    normed_ref[rows, :] = (centered * inverse * gain_ref[...]).astype(BF)
    lane = lax.broadcasted_iota(jnp.int32, moment_ref.shape, 1)
    moment_ref[...] = jnp.where(lane == 0, mean, inverse)

    @pl.when(step == pl.num_programs(0) - 1)
    def _():
        first = pl.multiple_of(place_ref[4], 16)
        face_ref[...] = normed_ref[pl.ds(first, face_ref.shape[0]), :]


def run_prepare(place, tokens, gain, face):
    count, width = tokens.shape
    block = min(count, 128)
    part = lambda columns: pl.BlockSpec((block, columns), lambda step: (step, 0))
    return pl.pallas_call(
        prepare,
        grid=(count // block,),
        in_specs=[SCALARS, part(width), whole((1, width))],
        out_specs=[whole((count, width)), whole((face, width)), part(128)],
        out_shape=[
            jax.ShapeDtypeStruct((count, width), BF),
            jax.ShapeDtypeStruct((face, width), BF),
            jax.ShapeDtypeStruct((count, 128), F32),
        ],
        compiler_params=pltpu.CompilerParams(**PARAMS),
        cost_estimate=pl.CostEstimate(flops=0, bytes_accessed=3 * 1024 * 1024, transcendentals=0),
        name="prepare",
    )(place, in_hbm(tokens), in_hbm(gain))


def spread_heads(block, head_dim):
    lane_head = lax.broadcasted_iota(jnp.int32, block.shape, 1) // head_dim
    zero = jnp.zeros_like(block)
    return jnp.concatenate(
        [jnp.where(lane_head == head, block, zero) for head in range(GROUP)], axis=0
    )


def gather_heads(full, count, head_dim):
    lane_head = lax.broadcasted_iota(jnp.int32, (count, full.shape[1]), 1) // head_dim
    result = full[:count]
    for head in range(1, GROUP):
        result = jnp.where(lane_head == head, full[head * count : (head + 1) * count], result)
    return result


def times(left, right):
    return jnp.dot(left, right, preferred_element_type=F32)


def times_t(left, right):
    return lax.dot_general(left, right, (((1,), (1,)), ((), ())), preferred_element_type=F32)


def fill_bias(place_ref, bias_ref, tile_rows, tile_cols):
    strips, count, window = bias_ref.shape
    slots = tile_cols + 2 * SIDE
    own = lax.broadcasted_iota(jnp.int32, (count, window), 0)
    near = lax.broadcasted_iota(jnp.int32, (count, window), 1)
    own_row, own_col = own // tile_cols, own % tile_cols
    near_row, slot = near // slots, near % slots
    near_col = jnp.where(slot < tile_cols + SIDE, slot, slot - slots)
    row_gap = near_row - RADIUS - own_row
    col_gap = near_col - own_col
    col = place_ref[1] + near_col
    allowed = (jnp.abs(row_gap) <= RADIUS) & (jnp.abs(col_gap) <= RADIUS)
    allowed = allowed & (col >= 0) & (col < place_ref[3])
    for strip in range(strips):
        row = place_ref[0] + strip * STRIP + near_row - RADIUS
        kept = allowed & (row >= 0) & (row < place_ref[2])
        bias_ref[strip] = jnp.where(kept, 0.0, -1e30).astype(F32)


def query_pass(
    head_dim,
    tile,
    place_ref,
    q_ref,
    g_ref,
    normed_ref,
    key_w_ref,
    value_w_ref,
    out_ref,
    owed_ref,
    bias_ref,
    k_ref,
    v_ref,
    dk_ref,
    dv_ref,
):
    scaling = 1.0 / math.sqrt(head_dim)
    strips, count, window = bias_ref.shape
    step = (tile[1] + 2 * SIDE) * STRIP
    group = pl.program_id(0)

    @pl.when(group == 0)
    def _():
        fill_bias(place_ref, bias_ref, *tile)

    k_ref[...] = times(normed_ref[...], key_w_ref[...]).astype(BF)
    v_ref[...] = times(normed_ref[...], value_w_ref[...]).astype(BF)
    dk_ref[...] = jnp.zeros_like(dk_ref)
    dv_ref[...] = jnp.zeros_like(dv_ref)

    def dots(strip):
        own = pl.ds(strip * count, count)
        near = pl.ds(strip * step, window)
        queries = spread_heads(q_ref[own, :] * jnp.asarray(scaling, BF), head_dim)
        grads = spread_heads(g_ref[own, :], head_dim)
        scores = times_t(queries, k_ref[near, :])
        return queries, grads, scores, times_t(grads, v_ref[near, :])

    ahead = dots(0)
    for strip in range(strips):
        own = pl.ds(strip * count, count)
        near = pl.ds(strip * step, window)
        queries, grads, scores, grad_probs = ahead
        if strip + 1 < strips:
            ahead = dots(strip + 1)
        probs_parts, grad_parts = [], []
        for head in range(GROUP):
            part = slice(head * count, (head + 1) * count)
            masked = scores[part] + bias_ref[strip]
            row_max = jnp.max(masked, axis=1, keepdims=True)
            exponent = jnp.exp(masked - row_max)
            grad_part = grad_probs[part]
            total = jnp.sum(exponent, axis=1, keepdims=True)
            share = 1.0 / total
            delta = jnp.sum(exponent * grad_part, axis=1, keepdims=True) * share
            probs = exponent * share
            probs_parts.append(probs.astype(BF))
            grad_parts.append((probs * (grad_part - delta)).astype(BF))
        probs = jnp.concatenate(probs_parts, axis=0)
        grad_scores = jnp.concatenate(grad_parts, axis=0)
        attended = times(probs, v_ref[near, :])
        grad_queries = times(grad_scores, k_ref[near, :])
        out_ref[0, own, :] = gather_heads(attended, count, head_dim).astype(BF)
        out_ref[1, own, :] = (gather_heads(grad_queries, count, head_dim) * scaling).astype(BF)
        dk_ref[near, :] += product_t(grad_scores, queries)
        dv_ref[near, :] += product_t(probs, grads)
    owed_ref[0] = dk_ref[...].astype(BF)
    owed_ref[1] = dv_ref[...].astype(BF)


def whole(shape):
    return pl.BlockSpec(shape, lambda group: (0,) * len(shape))


def columns(rows, width, first=0):
    return pl.BlockSpec((rows, width), lambda group: (0, first + group))


def pair_columns(rows, width):
    return pl.BlockSpec((2, rows, width), lambda group: (0, 0, group))


SCALARS = pl.BlockSpec(memory_space=pltpu.SMEM)
PARAMS = dict(vmem_limit_bytes=24 * 1024 * 1024)


def window_shape(tile):
    return (tile[0] // STRIP, STRIP * tile[1], (STRIP + 2 * RADIUS) * (tile[1] + 2 * SIDE))


def attention_cost(tile, groups, part):
    strips, count, window = window_shape(tile)
    flops = 4 * 2 * groups * strips * GROUP * count * window * part
    return pl.CostEstimate(flops=flops, bytes_accessed=4 * 1024 * 1024, transcendentals=0)


def run_queries(place, queries, grads, normed_ext, weights, head_dim, tile):
    tokens, width = queries.shape
    ext = normed_ext.shape[0]
    part = GROUP * head_dim
    groups = width // part
    return pl.pallas_call(
        functools.partial(query_pass, head_dim, tile),
        grid=(groups,),
        in_specs=[
            SCALARS,
            columns(tokens, part),
            columns(tokens, part),
            pl.BlockSpec(normed_ext.shape, lambda group: (0, 0), pipeline_mode=pl.Buffered(1)),
            columns(width, part, groups),
            columns(width, part, 2 * groups),
        ],
        out_specs=[pair_columns(tokens, part), pair_columns(ext, part)],
        out_shape=[
            jax.ShapeDtypeStruct((2, tokens, width), BF),
            jax.ShapeDtypeStruct((2, ext, width), BF),
        ],
        scratch_shapes=[pltpu.VMEM(window_shape(tile), F32)]
        + [pltpu.VMEM((ext, part), BF)] * 2
        + [pltpu.VMEM((ext, part), F32)] * 2,
        compiler_params=pltpu.CompilerParams(**PARAMS),
        cost_estimate=attention_cost(tile, groups, part),
        name="query_pass",
    )(place, queries, grads, normed_ext, in_hbm(weights), in_hbm(weights))


def own_part(array, index, axis):
    return lax.dynamic_index_in_dim(array, index, axis, keepdims=False)


def product_t(left, right):
    return lax.dot_general(left, right, (((0,), (0,)), ((), ())), preferred_element_type=F32)


def slide_swap(array, high):
    return swapped(array, "slide", lax.axis_size("slide") // 2 if high else 1)


def partners(across_slides):
    if across_slides:
        index = lax.axis_index("slide") // 2
        return index, [(1, 1 - index)]
    index = lax.axis_index("gy")
    return index, [(by, index ^ by) for by in range(1, lax.axis_size("gy"))]


def sent(block, across_slides, by):
    return slide_swap(block, True) if across_slides else swapped(block, "gy", by)


def pick_rows(array, index, across_slides, width):
    rows = width // lax.axis_size("slide")
    core = lax.axis_index("slide") % 2
    if across_slides:
        return lax.dynamic_slice_in_dim(array, (2 * index + core) * rows, rows, axis=1)
    rest = rows // lax.axis_size("gy")
    parts = [
        lax.dynamic_slice_in_dim(array, (2 * high + core) * rows + index * rest, rest, axis=1)
        for high in range(lax.axis_size("slide") // 2)
    ]
    return jnp.concatenate(parts, axis=1)


def pair_product(lefts, rights, index, across_slides):
    total = None
    for left, right in zip(lefts, rights):
        term = product_t(pick_rows(left, index, across_slides, right.shape[1]), right)
        total = term if total is None else total + term
    return total


def partner_half(left, right):
    rows = left.shape[1] // lax.axis_size("slide")
    other = 1 - lax.axis_index("slide") % 2
    parts = [
        lax.dynamic_slice_in_dim(left, (2 * high + other) * rows, rows, axis=1)
        for high in range(lax.axis_size("slide") // 2)
    ]
    return product_t(jnp.concatenate(parts, axis=1), right).astype(BF)


def halved_product(left, right, arrived, index, across_slides):
    rows = arrived.shape[0] // 2
    if across_slides:
        match = lax.dynamic_slice_in_dim(arrived, index * rows, rows, axis=0)
    else:
        rest = rows // lax.axis_size("gy")
        match = jnp.concatenate(
            [
                lax.dynamic_slice_in_dim(arrived, high * rows + index * rest, rest, axis=0)
                for high in range(2)
            ],
            axis=0,
        )
    return product_t(pick_rows(left, index, across_slides, left.shape[1]), right) + match.astype(F32)


def blocks_of(product, across_slides):
    index, others = partners(across_slides)
    return [product(target).astype(BF) for _, target in others], lambda: product(index)


def first_halving(blocks, mine, across_slides):
    others = partners(across_slides)[1]
    arrived = [sent(block, across_slides, by) for block, (by, _) in zip(blocks, others)]
    total = mine()
    for block in arrived:
        total = total + block.astype(F32)
    return total


def second_halving(part, across_slides):
    index, others = partners(across_slides)
    rows = part.shape[0] // (len(others) + 1)
    mine = lax.dynamic_slice_in_dim(part, index * rows, rows, axis=0)
    for by, target in others:
        block = lax.dynamic_slice_in_dim(part, target * rows, rows, axis=0).astype(BF)
        mine = mine + sent(block, across_slides, by).astype(F32)
    return mine


def column_blocks(part):
    count = lax.axis_size("gx")
    index = lax.axis_index("gx")
    rows = part.shape[0] // count
    mine = lax.dynamic_slice_in_dim(part, index * rows, rows, axis=0)
    others = [
        lax.dynamic_slice_in_dim(part, (index ^ by) * rows, rows, axis=0).astype(BF)
        for by in range(count - 1, 0, -1)
    ]
    return mine, others


def reduce_columns(mine, others):
    count = lax.axis_size("gx")
    arrived = [
        swapped(block, "gx", by) for block, by in zip(others, range(count - 1, 0, -1))
    ]
    for block in arrived:
        mine = mine + block.astype(F32)
    return mine


def halve_columns(part):
    count, width = lax.axis_size("gx"), part.shape[1]
    index = lax.axis_index("gx")
    rows = part.shape[0] // count
    by = 1
    while by < count:
        bit = lax.rem(index // by, 2)
        blocks = part.reshape(-1, 2, rows, width)
        going = lax.dynamic_index_in_dim(blocks, 1 - bit, 1, keepdims=False).astype(BF)
        kept = lax.dynamic_index_in_dim(blocks, bit, 1, keepdims=False)
        part = (kept + swapped(going, "gx", by).astype(F32)).reshape(-1, width)
        by *= 2
    return part


def second_halvings(one, two):
    return jnp.concatenate([second_halving(one, False), second_halving(two, True)], axis=1)


def after(array, *earlier):
    return lax.optimization_barrier((array, *earlier))[0]


def local(tokens, weights, norm_gain, tissue, cotangent):
    tile_tokens = tokens[0]
    tile_rows, tile_cols, model_width = tile_tokens.shape
    tile = (tile_rows, tile_cols)
    head_dim = model_width // HEADS
    token_count = tile_rows * tile_cols
    slides = lax.axis_size("slide")
    rows_count = lax.axis_size("gy")
    cols_count = lax.axis_size("gx")
    weight_in = weights[:, : 3 * model_width]
    weight_out = weights[:, 3 * model_width :]
    face = RADIUS * tile_cols
    at_top = lax.axis_index("gy") == 0
    place = jnp.stack(
        [
            lax.axis_index("gy") * tile_rows,
            lax.axis_index("gx") * tile_cols,
            jnp.int32(tile_rows * rows_count),
            jnp.int32(tile_cols * cols_count),
            jnp.where(at_top, token_count - face, 0),
        ]
    ).astype(jnp.int32)

    flat = (token_count, model_width)
    grid = (tile_rows, tile_cols, model_width)
    tissue_mask = tissue[0].astype(F32).reshape(token_count, 1)
    tokens_flat = tile_tokens.reshape(flat)
    cot_flat = cotangent[0].reshape(flat)
    normed, facing, moments = run_prepare(
        place, tokens_flat, norm_gain.reshape(1, model_width), face
    )
    normed_tile = normed.reshape(grid)
    rows = rows_around(normed_tile, facing.reshape(RADIUS, tile_cols, model_width))
    middle = column_halo(normed_tile)
    normed_ext = with_rows(middle, [column_halo(row) for row in rows])
    ext_rows, ext_cols = normed_ext.shape[:2]
    normed_ext = normed_ext.reshape(ext_rows * ext_cols, model_width)

    queries = times(normed, weight_in[:, :model_width]).astype(BF)
    mask_late = after(tissue_mask, *rows)
    branch_flat = (mask_late * cot_flat.astype(F32)).astype(BF)
    grad_attn = times_t(branch_flat, weight_out).astype(BF)
    normed_late, branch_late, grad_attn = lax.optimization_barrier(
        (normed, branch_flat, grad_attn)
    )
    normed_pair = (normed, slide_swap(normed_late, False))
    branch_pair = (branch_flat, slide_swap(branch_late, False))

    found, owed = run_queries(place, queries, grad_attn, normed_ext, weights, head_dim, tile)
    attended, grad_queries = found[0], found[1]

    found_other = slide_swap(found, False)
    key_half = partner_half(normed_ext, owed[0])
    value_half = partner_half(normed_ext, owed[1])
    key_arrived, value_arrived = slide_swap(key_half, False), slide_swap(value_half, False)
    found_other = after(found_other, key_half, value_half)
    query_sent, query_kept = blocks_of(
        lambda index: pair_product(normed_pair, (grad_queries, found_other[1]), index, True), True
    )
    out_sent, out_kept = blocks_of(
        lambda index: pair_product((attended, found_other[0]), branch_pair, index, False), False
    )

    owed_grid = after(owed, *query_sent, *out_sent)
    owed_grid = owed_grid.reshape(2, ext_rows, ext_cols, model_width)
    outward = owed_columns(owed_grid)
    key_sent, key_kept = blocks_of(
        lambda index: halved_product(normed_ext, owed[0], key_arrived, index, True), True
    )
    value_sent, value_kept = blocks_of(
        lambda index: halved_product(normed_ext, owed[1], value_arrived, index, False), False
    )

    first_kept = lax.optimization_barrier((query_kept(), out_kept(), key_sent, value_sent))[:2]
    one = first_halving(query_sent, lambda: first_kept[0], True)
    two = first_halving(out_sent, lambda: first_kept[1], False)
    second_kept = lax.optimization_barrier((key_kept(), value_kept(), one, two))[:2]
    three = first_halving(key_sent, lambda: second_kept[0], True)
    four = first_halving(value_sent, lambda: second_kept[1], False)
    owed_cols = return_columns(owed_grid, *outward)
    owed_up = owed_rows(owed_cols)
    mine, others = column_blocks(after(second_halvings(three, four), *owed_up))
    first_sums = reduce_columns(*column_blocks(second_halvings(one, two)))
    owed_sum = return_rows(owed_cols, owed_up).astype(BF).reshape((2,) + flat)

    attended_late = after(attended, *key_sent, *value_sent)
    projection = times(attended_late, weight_out)
    block_output = (tokens_flat.astype(F32) + tissue_mask * projection).astype(BF)

    grad_projected = jnp.concatenate([grad_queries, owed_sum[0], owed_sum[1]], axis=-1)
    scaled = times_t(grad_projected, weight_in) * norm_gain
    inverse = moments[:, 1:2]
    normalized = (tokens_flat.astype(F32) - moments[:, :1]) * inverse
    first_mean = jnp.mean(scaled, axis=-1, keepdims=True)
    second_mean = jnp.mean(scaled * normalized, axis=-1, keepdims=True)
    input_grad = inverse * (scaled - first_mean - normalized * second_mean)
    input_grad = (cot_flat.astype(F32) + input_grad).astype(BF)

    second_sums = reduce_columns(after(mine, input_grad), others)
    inv_root = 1.0 / math.sqrt(slides * rows_count * cols_count * token_count)
    width = model_width
    weight_grads = jnp.concatenate(
        [first_sums[:, :width], second_sums, first_sums[:, width:]], axis=1
    )
    return (
        block_output.reshape((1,) + grid),
        input_grad.reshape((1,) + grid),
        weight_grads * inv_root,
    )


def solution(mesh):
    tile = P("slide", "gy", "gx", None)
    return jax.shard_map(
        local,
        mesh=mesh,
        in_specs=(tile, P(), P(), P("slide", "gy", "gx"), tile),
        out_specs=(tile, tile, P(("slide", "gy", "gx"), None)),
        check_vma=False,
    )
```
